512 devices in a mesh: mode: 8 (over z_hi, x), space: 64 (over y, z_lo, core).
Axes of the slice: x: 4, y: 4, z: 16 (z_hi: 2, z_lo: 8; z = z_hi * 8 + z_lo), core: 2. Of those that a mesh axis runs over, the one named last changes fastest.
Arguments:
- load_modes: float32 [96, 3, 64, 4, 128], P('mode', None, 'space'), may hold values from -8 to 8
- first_guess: float32 [96, 3, 64, 4, 128], P('mode', None, 'space'), may hold values from -4 to 4
- kl_fields: float32 [8, 64, 4, 128], P(None, 'space'), may hold values from -3 to 3
- region_labels: int32 [64, 4, 128], P('space'), may hold values from 0 to 2
- partner: int32 [96, 8], replicated, may hold values from 0 to 95, as said below
- variable: int32 [96, 8], replicated, may hold values from 0 to 7
- weight: float32 [96, 8], replicated, may hold values from 0.2 to 1
Outputs:
- solution_modes: float32 [96, 3, 64, 4, 128], P('mode', None, 'space')
The draws below stay inside these ranges and needn't reach their ends.
Inputs may be any that keep to these rules, and one draw needn't show every extreme that they name: partner[i, l] is never i.
All inputs are finite; a program needn't handle non-finite values.
Results may differ from the reference program's by a relative error of at most 0.00011.
Values sent between devices are 32-bit elements; how exact they have to be, the bound alone decides.
No kernel may reach another device: no remote copies, remote signals or barrier semaphores. Data moves between devices by JAX's collectives and lax.ppermute only.
A program may use at most 64 MiB of HBM per device.

```python
import math
import jax
import jax.numpy as jnp
from jax import lax

MODES = 96
KL = 8
LINKS = 8
CG_STEPS = 3
SWEEPS = 2
NY = 4
NZ = 128
NX = 64


def draw_partner(key, part):
    key = jax.random.fold_in(key, 1)
    shifts = jax.random.randint(key, (MODES, LINKS), 1, MODES)
    shifts = shifts.at[0, 0].set(MODES - 1)
    shifts = shifts.at[1, 0].set(MODES - 1)
    rows = jnp.arange(MODES, dtype=jnp.int32)[:, None]
    return ((rows + shifts) % MODES).astype(jnp.int32)


def place_ends(result, rng, smallest, top_value):
    extent = result.shape
    index_at = [jax.random.randint(jax.random.fold_in(rng, axis), (), 0, extent[axis]) for axis in range(len(extent))]
    result = result.at[tuple(index_at)].set(smallest)
    longest = extent.index(max(extent))
    index_at[longest] = (index_at[longest] + 1) % extent[longest]
    return result.at[tuple(index_at)].set(top_value)


def shard_levels(rng, dims, shards, low, high):
    level = 1.0
    for position, parts in shards:
        heights = jax.random.uniform(jax.random.fold_in(jax.random.fold_in(rng, 6), position), (parts,), jnp.float32, low / len(shards), high / len(shards))
        level = level * jnp.repeat(jnp.exp(heights), dims[position] // parts).reshape((-1,) + (1,) * (len(dims) - 1 - position))
    return level


def scatter_about(key, extent, deviation, limit, shards=(), held_as=jnp.bfloat16):
    result = deviation * jax.random.normal(key, extent, jnp.float32)
    if shards:
        result = result * shard_levels(key, extent, shards, -0.22, 0.18)
    return jnp.clip(result, -limit, limit).astype(held_as)


def setup_inputs(seed: int = 0) -> dict:
    key_of = jax.random.split(jax.random.key(seed), 8)
    return {
        "load_modes": scatter_about(key_of[0], (MODES, 3, NX, NY, NZ), 1.0, 8.0, ((0, 8), (2, 64)), jnp.float32),
        "first_guess": scatter_about(key_of[1], (MODES, 3, NX, NY, NZ), 0.5, 4.0, ((0, 8), (2, 64)), jnp.float32),
        "kl_fields": scatter_about(key_of[2], (KL, NX, NY, NZ), 0.3, 3.0, ((1, 64),), jnp.float32),
        "region_labels": place_ends(jax.random.randint(key_of[3], (NX, NY, NZ), 0, 3), jax.random.fold_in(key_of[3], 1), 0, 2).astype(jnp.int32),
        "partner": draw_partner(jax.random.fold_in(key_of[7], 71), 0),
        "variable": place_ends(jax.random.randint(key_of[5], (MODES, LINKS), 0, KL), jax.random.fold_in(key_of[5], 1), 0, KL - 1).astype(jnp.int32),
        "weight": jnp.clip(jnp.exp(jax.random.uniform(key_of[6], (MODES, LINKS), jnp.float32, math.log(0.2), math.log(1.0))), 0.2, 1.0),
    }


def trailing(array, index):
    return array[tuple([slice(None)] * (array.ndim - 3) + list(index))]


def neighbour(array, dimension, offset_side):
    index = [slice(1, -1), slice(1, -1), slice(1, -1)]
    length = array.shape[array.ndim - 3 + dimension]
    index[dimension] = slice(offset_side, length - 2 + offset_side)
    return trailing(array, index)


def stiffness(field, coefficient):
    lead_field = field.ndim - 3
    field = jnp.pad(field, [(0, 0)] * lead_field + [(0, 0), (1, 1), (1, 1)])
    lead_coef = coefficient.ndim - 3
    coefficient = jnp.pad(coefficient, [(0, 0)] * lead_coef + [(0, 0), (1, 1), (1, 1)])
    inner = [slice(1, -1), slice(1, -1), slice(1, -1)]
    centre_val = trailing(field, inner)
    centre_mod = trailing(coefficient, inner)
    running = None
    for dimension in range(3):
        weighting = jnp.where(jnp.arange(3) == dimension, 2.0, 1.0).astype(jnp.float32).reshape(3, 1, 1, 1)
        for offset_side in (0, 2):
            face_mod = 0.5 * (centre_mod + neighbour(coefficient, dimension, offset_side))
            change = centre_val - neighbour(field, dimension, offset_side)
            term = weighting * jnp.expand_dims(face_mod, -4) * change
            running = term if running is None else running + term
    return running


def coefficients(region_labels, kl_fields):
    mean_coef = jnp.where(region_labels == 0, 1.3, jnp.where(region_labels == 1, 1.0, 0.6)).astype(jnp.float32)
    copper = (region_labels == 1).astype(jnp.float32)
    return mean_coef, kl_fields * copper[None]


def pad_along(array, axis_number):
    widths = [(0, 0)] * array.ndim
    widths[axis_number] = (1, 1)
    return jnp.pad(array, widths)


def expand(values):
    return values[:, None, None, None, None]


def reference(load_modes, first_guess, kl_fields, region_labels, partner, variable, weight):
    mean_coef, varying = coefficients(region_labels, kl_fields)
    mean_padded = pad_along(mean_coef, 0)
    vary_padded = pad_along(varying, 1)
    iterate = first_guess
    for sweep_index in range(SWEEPS):
        padded = pad_along(iterate, 2)

        def link_term(running, link):
            rows = jnp.take(padded, partner[:, link], axis=0)
            moduli = jnp.take(vary_padded, variable[:, link], axis=0)
            return running + expand(weight[:, link]) * stiffness(rows, moduli), None

        coupling, _ = lax.scan(link_term, jnp.zeros_like(iterate), jnp.arange(LINKS, dtype=jnp.int32))
        right_side = load_modes - coupling
        estimate = iterate
        residual = right_side - stiffness(padded, mean_padded)
        direction = residual
        norm_now = jnp.sum(residual * residual, axis=(1, 2, 3, 4))
        for step_index in range(CG_STEPS):
            image = stiffness(pad_along(direction, 2), mean_padded)
            step_size = norm_now / jnp.sum(direction * image, axis=(1, 2, 3, 4))
            estimate = estimate + expand(step_size) * direction
            residual = residual - expand(step_size) * image
            norm_next = jnp.sum(residual * residual, axis=(1, 2, 3, 4))
            direction = residual + expand(norm_next / norm_now) * direction
            norm_now = norm_next
        iterate = estimate
    return iterate
```

```python
import functools

import jax
import jax.numpy as jnp
from jax import lax
from jax.experimental import pallas as pl
from jax.experimental.pallas import tpu as pltpu
from jax.sharding import Mesh
from jax.sharding import PartitionSpec as P

AXES = ("zh", "x", "y", "zl", "c")
GROUPS = ("c", "x")
DEPTH = ("zh", "zl")
NG, NM, NL, NK = 8, 12, 8, 8
NY, NZ, SHIFT = 4, 128, 4.0
QUAD = 4
TRI = NM // QUAD
ROWS = 3 * TRI
SLAB = NY * ROWS
F32 = jnp.float32


def flat(zh, x, y, zl, c):
    return (((zh * 4 + x) * 4 + y) * 8 + zl) * 2 + c


def moves():
    pairs = []
    for zh in range(2):
        for x in range(4):
            for y in range(4):
                for zl in range(8):
                    for c in range(2):
                        s = y * 16 + zl * 2 + c
                        z = s // 4
                        pairs.append((flat(zh, x, y, zl, c), flat(z // 8, x, s % 4, z % 8, zh)))
    return pairs


def slab_steps(step):
    def place(s):
        z = s // 4
        return ((z // 8) * 4 + s % 4) * 8 + z % 8

    return [(place(s), place(s + step)) for s in range(64) if 0 <= s + step < 64]


def depth_steps(step):
    return [(z, z + step) for z in range(16) if 0 <= z + step < 16]


def call(kernel, outs, scratch=()):
    return pl.pallas_call(
        kernel,
        out_shape=[jax.ShapeDtypeStruct(s, F32) for s in outs],
        scratch_shapes=[pltpu.VMEM(s, F32) for s in scratch],
    )


def faces(e, other):
    return 0.5 * (e + other)


def coupling_kernel(nk, *refs):
    first = nk > NK
    if first:
        (u, load, e0, em, ep, partner, variable, weight, out, us, mx, fx, fy, fz) = refs
    else:
        (u, e0, em, ep, partner, variable, weight, out, us, mx, fx, fy, fz) = refs
    for g in range(NG):
        for yc in range(NY * 3):
            us[yc, g * NM : (g + 1) * NM, :] = u[g, yc * NM : (yc + 1) * NM, :]
    lane = lax.broadcasted_iota(jnp.int32, (16, NG * NM), 1)
    pr, vr, wr = partner[...], variable[...], weight[...]
    links = NL + 1 if first else NL
    hit = [jnp.where(lane == pr[:, l : l + 1], wr[:, l : l + 1], 0.0) for l in range(links)]
    blocks = []
    for k in range(nk):
        acc = None
        for l in range(links):
            if (k == NK) != (l == NL):
                continue
            term = hit[l] if l == NL else jnp.where(vr[:, l : l + 1] == k, hit[l], 0.0)
            acc = term if acc is None else acc + term
        blocks.append(acc)
    mix = jnp.concatenate(blocks, axis=0)
    for yc in range(NY * 3):
        mx[yc] = lax.dot_general(
            mix,
            us[yc],
            (((1,), (0,)), ((), ())),
            precision=lax.Precision.HIGHEST,
            preferred_element_type=F32,
        )
    e = e0[...]
    zlane = lax.broadcasted_iota(jnp.int32, e.shape, 1)
    row = lax.broadcasted_iota(jnp.int32, e.shape, 0)
    zup = jnp.where(zlane == NZ - 1, 0.0, pltpu.roll(e, NZ - 1, 1))
    zdn = jnp.where(zlane == 0, 0.0, pltpu.roll(e, 1, 1))
    count = e.shape[0]
    yup = jnp.where(row % NY == NY - 1, 0.0, pltpu.roll(e, count - 1, 0))
    ydn = jnp.where(row % NY == 0, 0.0, pltpu.roll(e, 1, 0))
    fx[0] = faces(e, ep[...])
    fx[1] = faces(e, em[...])
    fy[0] = faces(e, yup)
    fy[1] = faces(e, ydn)
    fzu, fzd = faces(e, zup), faces(e, zdn)
    base = fx[0] + fx[1] + fy[0] + fy[1] + fzu + fzd
    fz[0] = jnp.where(zlane == NZ - 1, 0.0, fzu)
    fz[1] = jnp.where(zlane == 0, 0.0, fzd)
    fz[2] = base + fx[0] + fx[1]
    fz[3] = base + fy[0] + fy[1]
    fz[4] = base + fzu + fzd
    for y in range(NY):
        for c in range(3):
            own = up = down = None
            for k in range(nk):
                r = slice(k * NY + y, k * NY + y + 1)
                rows = slice(k * 16, k * 16 + 16)
                m = mx[y * 3 + c, rows, :]
                t = fz[2 + c, r, :] * m
                side = None
                if y + 1 < NY:
                    side = fy[0, r, :] * mx[(y + 1) * 3 + c, rows, :]
                if y > 0:
                    less = fy[1, r, :] * mx[(y - 1) * 3 + c, rows, :]
                    side = less if side is None else side + less
                t = t - (2.0 * side if c == 1 else side)
                side = fz[0, r, :] * pltpu.roll(m, NZ - 1, 1) + fz[1, r, :] * pltpu.roll(m, 1, 1)
                t = t - (2.0 * side if c == 2 else side)
                p, q = fx[0, r, :] * m, fx[1, r, :] * m
                own, up, down = (t, p, q) if own is None else (own + t, up + p, down + q)
            if c == 0:
                up, down = 2.0 * up, 2.0 * down
            yc = y * 3 + c
            own = load[yc * NM : (yc + 1) * NM, :] - own[:NM] if first else -own[:NM]
            for kind, val in enumerate((own, up, down)):
                at = (kind * NY + y) * ROWS + c * TRI
                for d in range(QUAD):
                    out[d, at : at + TRI, :] = val[d * TRI : (d + 1) * TRI]
    tail = e[NK * NY : NK * NY + NY] if first else jnp.zeros((NY, NZ), F32)
    for d in range(QUAD):
        out[d, 3 * SLAB : 3 * SLAB + NY, :] = tail


def edges_kernel(first, *refs):
    if first:
        q, own, up, down = refs
    else:
        q, rest, own, up, down = refs
    rs = []
    for s in range(QUAD):
        r = q[s, 0:SLAB, :]
        if not first:
            r = r + rest[s]
        if s > 0:
            r = r + q[s - 1, SLAB : 2 * SLAB, :]
        if s + 1 < QUAD:
            r = r + q[s + 1, 2 * SLAB : 3 * SLAB, :]
        own[s] = r
        rs.append(r)
    for j in range(3):
        up[j * SLAB : (j + 1) * SLAB, :] = rs[j + 1]
        down[j * SLAB : (j + 1) * SLAB, :] = rs[j]
    up[3 * SLAB : 4 * SLAB, :] = q[3, SLAB : 2 * SLAB, :]
    down[3 * SLAB : 4 * SLAB, :] = q[0, 2 * SLAB : 3 * SLAB, :]
    if first:
        for j in range(3):
            at = 4 * SLAB + j * NY
            up[at : at + NY, :] = q[j + 1, 3 * SLAB : 3 * SLAB + NY, :]
            down[at : at + NY, :] = q[j, 3 * SLAB : 3 * SLAB + NY, :]
        up[4 * SLAB + 12 :, :] = jnp.zeros((4, NZ), F32)
        down[4 * SLAB + 12 :, :] = jnp.zeros((4, NZ), F32)


def powers_kernel(first, *refs):
    if first:
        q, own, low, high, v0, v1, v2, v3, mom, ec, w0, w1, w2, dg = refs
        for j in range(3):
            at = 4 * SLAB + j * NY
            ec[j * NY : (j + 1) * NY, :] = low[at : at + NY, :]
            ec[(7 + j) * NY : (8 + j) * NY, :] = high[at : at + NY, :]
        for s in range(QUAD):
            ec[(3 + s) * NY : (4 + s) * NY, :] = q[s, 3 * SLAB : 3 * SLAB + NY, :]
    else:
        q, own, low, high, ec, v0, v1, v2, v3, mom, w0, w1, w2, dg = refs

    def rows(ref, at, y):
        return ref[at + y * ROWS : at + (y + 1) * ROWS, :]

    rid = lax.broadcasted_iota(jnp.int32, (ROWS, NZ), 0)
    wx = jnp.where(rid < TRI, 2.0, 1.0)
    wy = jnp.where((rid >= TRI) & (rid < 2 * TRI), 2.0, 1.0)
    wz = jnp.where(rid >= 2 * TRI, 2.0, 1.0)
    lane1 = lax.broadcasted_iota(jnp.int32, (1, NZ), 1)
    em = [[ec[p * NY + y : p * NY + y + 1, :] for y in range(NY)] for p in range(10)]
    zero = jnp.zeros((1, NZ), F32)

    def inside(p, y, val):
        return val if 3 <= p <= 6 else jnp.where(em[p][y] > 0.0, val, 0.0)

    for y in range(NY):
        for p in range(3):
            lo = rows(low, p * SLAB, y)
            hi = rows(high, p * SLAB, y)
            if p == 2:
                lo = lo + rows(q.at[0], 2 * SLAB, y)
            if p == 0:
                hi = hi + rows(q.at[QUAD - 1], SLAB, y)
            w0[p * NY + y] = inside(p, y, lo)
            w0[(7 + p) * NY + y] = inside(7 + p, y, hi)
        for s in range(QUAD):
            r = rows(own.at[s], 0, y)
            if s == 0:
                r = r + rows(low, 3 * SLAB, y)
            if s == QUAD - 1:
                r = r + rows(high, 3 * SLAB, y)
            w0[(3 + s) * NY + y] = r
            v0[s * NY + y] = r

    def face(p, y):
        e = em[p][y]
        xu, xd = faces(e, em[p + 1][y]), faces(e, em[p - 1][y])
        yu = faces(e, em[p][y + 1] if y + 1 < NY else zero)
        yd = faces(e, em[p][y - 1] if y > 0 else zero)
        zu = faces(e, jnp.where(lane1 == NZ - 1, 0.0, pltpu.roll(e, NZ - 1, 1)))
        zd = faces(e, jnp.where(lane1 == 0, 0.0, pltpu.roll(e, 1, 1)))
        return xu, xd, yu, yd, zu, zd

    coef = {}
    for p in range(1, 9):
        for y in range(NY):
            xu, xd, yu, yd, zu, zd = face(p, y)
            dg[p * NY + y] = wx * (xu + xd) + wy * (yu + yd) + wz * (zu + zd) - SHIFT
            coef[p, y] = (
                xu, xd, yu, yd,
                jnp.where(lane1 == NZ - 1, 0.0, zu),
                jnp.where(lane1 == 0, 0.0, zd),
            )

    def apply(src, p, y):
        xu, xd, yu, yd, zu, zd = coef[p, y]
        m = src[p * NY + y]
        t = dg[p * NY + y] * m
        t = t - wx * (xu * src[(p + 1) * NY + y] + xd * src[(p - 1) * NY + y])
        side = None
        if y + 1 < NY:
            side = yu * src[p * NY + y + 1]
        if y > 0:
            less = yd * src[p * NY + y - 1]
            side = less if side is None else side + less
        t = t - wy * side
        t = t - wz * (zu * pltpu.roll(m, NZ - 1, 1) + zd * pltpu.roll(m, 1, 1))
        return inside(p, y, t)

    for p in range(1, 9):
        for y in range(NY):
            t = apply(w0, p, y)
            w1[p * NY + y] = t
            if 3 <= p <= 6:
                v1[(p - 3) * NY + y] = t
    for p in range(2, 8):
        for y in range(NY):
            t = apply(w1, p, y)
            w2[p * NY + y] = t
            if 3 <= p <= 6:
                v2[(p - 3) * NY + y] = t
    sums = [None] * 6
    for p in range(3, 7):
        for y in range(NY):
            a, b, d = w0[p * NY + y], w1[p * NY + y], w2[p * NY + y]
            t = apply(w2, p, y)
            v3[(p - 3) * NY + y] = t
            for j, val in enumerate((a * a, a * b, b * b, b * d, d * d, d * t)):
                sums[j] = val if sums[j] is None else sums[j] + val
    lane = lax.broadcasted_iota(jnp.int32, (ROWS, NZ), 1)
    spot = lane - 8 * (rid % TRI)
    packed = jnp.zeros((ROWS, NZ), F32)
    for j in range(6):
        packed = jnp.where(spot == j, jnp.sum(sums[j], axis=1, keepdims=True), packed)
    mom[...] = jnp.broadcast_to(jnp.sum(packed, axis=0, keepdims=True), mom.shape)


def step_coefficients(mom):
    def inner(a, b):
        total = None
        for i, s in enumerate(a):
            for j, t in enumerate(b):
                term = s * t * mom[i + j]
                total = term if total is None else total + term
        return total

    def image(a):
        q = [SHIFT * s for s in a] + [None]
        for i, s in enumerate(a):
            q[i + 1] = s if q[i + 1] is None else q[i + 1] + s
        return q

    one = jnp.ones_like(mom[0])
    x, r, p = [], [one], [one]
    rr = mom[0]
    for step in range(3):
        q = image(p)
        alpha = rr / inner(p, q)
        x = [x[i] + alpha * s if i < len(x) else alpha * s for i, s in enumerate(p)]
        r = [r[i] - alpha * s if i < len(r) else -alpha * s for i, s in enumerate(q)]
        if step < 2:
            new = inner(r, r)
            beta = new / rr
            p = [s + beta * p[i] if i < len(p) else s for i, s in enumerate(r)]
            rr = new
    return x, r


def update_kernel(first, *refs):
    if first:
        mom, v0, v1, v2, v3, out, rest = refs
    else:
        mom, v0, v1, v2, before, out = refs
    total = jnp.sum(mom[...], axis=0, keepdims=True)
    rid = lax.broadcasted_iota(jnp.int32, (ROWS, NZ), 0)
    lane = lax.broadcasted_iota(jnp.int32, (ROWS, NZ), 1)
    spot = lane - 8 * (rid % TRI)
    picked = [jnp.sum(jnp.where(spot == j, total, 0.0), axis=1, keepdims=True) for j in range(6)]
    x, r = step_coefficients(picked)
    x = [jnp.broadcast_to(s, (ROWS, NZ)) for s in x]
    r = [jnp.broadcast_to(s, (ROWS, NZ)) for s in r]
    for s in range(QUAD):
        for y in range(NY):
            at = s * NY + y
            rows = slice(y * ROWS, (y + 1) * ROWS)
            a, b, d = v0[at], v1[at], v2[at]
            change = x[0] * a + x[1] * b + x[2] * d
            if first:
                rest[s, rows, :] = r[0] * a + r[1] * b + r[2] * d + r[3] * v3[at]
            else:
                change = change + before[s, rows, :]
            out[s, rows, :] = change


def spread_kernel(q, out):
    for y in range(NY):
        for c in range(3):
            for d in range(QUAD):
                at = y * ROWS + c * TRI
                piece = q[d, at : at + TRI, :]
                to = (y * 3 + c) * NM + d * TRI
                for g in range(NG):
                    out[g, to : to + TRI, :] = piece


def packed(field):
    return field[:, :, 0].transpose(2, 1, 0, 3).reshape(NY * 3 * NM, NZ)


def shards(load_modes, first_guess, kl_fields, region_labels, partner, variable, weight):
    mean = jnp.where(region_labels == 0, 1.3, jnp.where(region_labels == 1, 1.0, 0.6)).astype(F32)
    varying = jnp.where(region_labels[None] == 1, kl_fields, 0.0)
    moduli = jnp.concatenate([varying, mean[None]], 0).reshape((NK + 1) * NY, NZ)
    there = moves()
    back = [(b, a) for a, b in there]
    guess = lax.ppermute(jnp.concatenate([packed(first_guess), moduli], 0), AXES, there)
    load = lax.ppermute(packed(load_modes), AXES, there)
    e0 = guess[NY * 3 * NM :]
    guess = guess[: NY * 3 * NM]
    em = lax.ppermute(e0, ("zh", "y", "zl"), slab_steps(1))
    ep = lax.ppermute(e0, ("zh", "y", "zl"), slab_steps(-1))

    offset = (lax.axis_index("c") * 4 + lax.axis_index("x")) * NM
    own = offset + jnp.arange(NM, dtype=jnp.int32)[:, None]
    pad = ((0, 16 - NM), (0, 0))
    rows_partner = lax.dynamic_slice_in_dim(partner, offset, NM, 0)
    rows_partner = jnp.pad(jnp.concatenate([rows_partner, own], 1), pad, constant_values=-1)
    rows_variable = jnp.pad(lax.dynamic_slice_in_dim(variable, offset, NM, 0), pad)
    rows_weight = lax.dynamic_slice_in_dim(weight, offset, NM, 0)
    rows_weight = jnp.pad(jnp.concatenate([rows_weight, jnp.ones((NM, 1), F32)], 1), pad)
    links = (rows_partner, rows_variable, rows_weight)

    spread = jnp.broadcast_to(guess[None], (NG,) + guess.shape)
    chunk, cells = (QUAD, SLAB, NZ), (QUAD * NY, ROWS, NZ)
    for sweep in range(2):
        first = sweep == 0
        nk = NK + 1 if first else NK
        gathered = lax.all_to_all(spread, GROUPS, 0, 0, tiled=True)
        fields = (gathered, load, e0, em, ep) if first else (gathered, e0, em, ep)
        face_rows = ((NK + 1) * NY, NZ)
        (sent,) = call(
            functools.partial(coupling_kernel, nk),
            [(QUAD, 3 * SLAB + NY, NZ)],
            [
                (NY * 3, NG * NM, NZ),
                (NY * 3, nk * 16, NZ),
                (2,) + face_rows,
                (2,) + face_rows,
                (5,) + face_rows,
            ],
        )(*fields, *links)
        q = lax.all_to_all(sent, "y", 0, 0, tiled=True)
        edge = (4 * SLAB + 16 if first else 4 * SLAB, NZ)
        chunk_r, up, down = call(functools.partial(edges_kernel, first), [chunk, edge, edge])(
            *((q,) if first else (q, rest))
        )
        low = lax.ppermute(up, DEPTH, depth_steps(1))
        high = lax.ppermute(down, DEPTH, depth_steps(-1))
        scratch = [(10 * NY, ROWS, NZ)] * 4
        outs = [cells] * 4 + [(16, NZ)]
        if first:
            v0, v1, v2, v3, mom, ec = call(
                functools.partial(powers_kernel, True), outs + [(10 * NY, NZ)], scratch
            )(q, chunk_r, low, high)
        else:
            v0, v1, v2, v3, mom = call(functools.partial(powers_kernel, False), outs, scratch)(
                q, chunk_r, low, high, ec
            )
        mom = lax.all_to_all(mom, DEPTH, 0, 0, tiled=True)
        if first:
            change, rest = call(functools.partial(update_kernel, True), [chunk, chunk])(
                mom, v0, v1, v2, v3
            )
        else:
            (change,) = call(functools.partial(update_kernel, False), [chunk])(
                mom, v0, v1, v2, change
            )
        by_slab = lax.all_to_all(change, "y", 0, 0, tiled=True)
        if first:
            (spread,) = call(spread_kernel, [(NG, NY * 3 * NM, NZ)])(by_slab)
    total = lax.ppermute(by_slab, AXES, back)
    total = total.reshape(QUAD, NY, 3, TRI, NZ).transpose(0, 3, 2, 1, 4)
    return first_guess + total.reshape(NM, 3, 1, NY, NZ)


def solution(mesh):
    split = Mesh(mesh.devices.reshape(2, 4, 4, 8, 2), AXES)
    mode, space = ("zh", "x"), ("y", "zl", "c")
    return jax.shard_map(
        shards,
        mesh=split,
        in_specs=(
            P(mode, None, space, None, None),
            P(mode, None, space, None, None),
            P(None, space, None, None),
            P(space, None, None),
            P(),
            P(),
            P(),
        ),
        out_specs=P(mode, None, space, None, None),
        check_vma=False,
    )
```

```python
import functools

import jax
import jax.numpy as jnp
from jax import lax
from jax.experimental import pallas as pl
from jax.experimental.pallas import tpu as pltpu
from jax.sharding import Mesh
from jax.sharding import PartitionSpec as P

AXES = ("zh", "x", "y", "zp", "zq", "c")
SLABS = ("y", "zp", "zq", "c")
CHUNKS = ("y", "zp")
WITHIN = ("zq", "c")
NG, NM, NL, NK = 8, 12, 8, 8
NY, NZ, SHIFT = 4, 128, 4.0
QUAD = 4
TRI = NM // QUAD
ROWS = 3 * TRI
SLAB = NY * ROWS
F32 = jnp.float32


def line(count, step):
    return [(i, i + step) for i in range(count) if 0 <= i + step < count]


def call(kernel, outs, scratch=()):
    return pl.pallas_call(
        kernel,
        out_shape=[jax.ShapeDtypeStruct(s, F32) for s in outs],
        scratch_shapes=[pltpu.VMEM(s, F32) for s in scratch],
    )


def faces(e, other):
    return 0.5 * (e + other)


def coupling_kernel(nk, *refs):
    first = nk > NK
    if first:
        (near, far, load, e0, em, ep, partner, variable, weight, out, us, mx, fx, fy, fz) = refs
    else:
        (near, far, e0, em, ep, partner, variable, weight, out, us, mx, fx, fy, fz) = refs
    for g in range(NG):
        for yc in range(NY * 3):
            half = near if g < NG // 2 else far
            us[yc, g * NM : (g + 1) * NM, :] = half[g % (NG // 2), yc * NM : (yc + 1) * NM, :]
    lane = lax.broadcasted_iota(jnp.int32, (16, NG * NM), 1)
    pr, vr, wr = partner[...], variable[...], weight[...]
    links = NL + 1 if first else NL
    hit = [jnp.where(lane == pr[:, l : l + 1], wr[:, l : l + 1], 0.0) for l in range(links)]
    blocks = []
    for k in range(nk):
        acc = None
        for l in range(links):
            if (k == NK) != (l == NL):
                continue
            term = hit[l] if l == NL else jnp.where(vr[:, l : l + 1] == k, hit[l], 0.0)
            acc = term if acc is None else acc + term
        blocks.append(acc)
    mix = jnp.concatenate(blocks, axis=0)
    for yc in range(NY * 3):
        mx[yc] = lax.dot_general(
            mix,
            us[yc],
            (((1,), (0,)), ((), ())),
            precision=lax.Precision.HIGHEST,
            preferred_element_type=F32,
        )
    e = e0[...]
    zlane = lax.broadcasted_iota(jnp.int32, e.shape, 1)
    row = lax.broadcasted_iota(jnp.int32, e.shape, 0)
    zup = jnp.where(zlane == NZ - 1, 0.0, pltpu.roll(e, NZ - 1, 1))
    zdn = jnp.where(zlane == 0, 0.0, pltpu.roll(e, 1, 1))
    count = e.shape[0]
    yup = jnp.where(row % NY == NY - 1, 0.0, pltpu.roll(e, count - 1, 0))
    ydn = jnp.where(row % NY == 0, 0.0, pltpu.roll(e, 1, 0))
    fx[0] = faces(e, ep[...])
    fx[1] = faces(e, em[...])
    fy[0] = faces(e, yup)
    fy[1] = faces(e, ydn)
    fzu, fzd = faces(e, zup), faces(e, zdn)
    base = fx[0] + fx[1] + fy[0] + fy[1] + fzu + fzd
    fz[0] = jnp.where(zlane == NZ - 1, 0.0, fzu)
    fz[1] = jnp.where(zlane == 0, 0.0, fzd)
    fz[2] = base + fx[0] + fx[1]
    fz[3] = base + fy[0] + fy[1]
    fz[4] = base + fzu + fzd
    for y in range(NY):
        for c in range(3):
            own = up = down = None
            for k in range(nk):
                r = slice(k * NY + y, k * NY + y + 1)
                rows = slice(k * 16, k * 16 + 16)
                m = mx[y * 3 + c, rows, :]
                t = fz[2 + c, r, :] * m
                side = None
                if y + 1 < NY:
                    side = fy[0, r, :] * mx[(y + 1) * 3 + c, rows, :]
                if y > 0:
                    less = fy[1, r, :] * mx[(y - 1) * 3 + c, rows, :]
                    side = less if side is None else side + less
                t = t - (2.0 * side if c == 1 else side)
                side = fz[0, r, :] * pltpu.roll(m, NZ - 1, 1) + fz[1, r, :] * pltpu.roll(m, 1, 1)
                t = t - (2.0 * side if c == 2 else side)
                p, q = fx[0, r, :] * m, fx[1, r, :] * m
                own, up, down = (t, p, q) if own is None else (own + t, up + p, down + q)
            if c == 0:
                up, down = 2.0 * up, 2.0 * down
            yc = y * 3 + c
            own = load[yc * NM : (yc + 1) * NM, :] - own[:NM] if first else -own[:NM]
            for kind, val in enumerate((own, up, down)):
                at = (kind * NY + y) * ROWS + c * TRI
                for d in range(QUAD):
                    out[d, at : at + TRI, :] = val[d * TRI : (d + 1) * TRI]
    tail = e[NK * NY : NK * NY + NY] if first else jnp.zeros((NY, NZ), F32)
    for d in range(QUAD):
        out[d, 3 * SLAB : 3 * SLAB + NY, :] = tail


def edges_kernel(first, *refs):
    if first:
        q, own, up, down = refs
    else:
        q, rest, own, up, down = refs
    rs = []
    for s in range(QUAD):
        r = q[s, 0:SLAB, :]
        if not first:
            r = r + rest[s]
        if s > 0:
            r = r + q[s - 1, SLAB : 2 * SLAB, :]
        if s + 1 < QUAD:
            r = r + q[s + 1, 2 * SLAB : 3 * SLAB, :]
        own[s] = r
        rs.append(r)
    for j in range(3):
        up[j * SLAB : (j + 1) * SLAB, :] = rs[j + 1]
        down[j * SLAB : (j + 1) * SLAB, :] = rs[j]
    up[3 * SLAB : 4 * SLAB, :] = q[3, SLAB : 2 * SLAB, :]
    down[3 * SLAB : 4 * SLAB, :] = q[0, 2 * SLAB : 3 * SLAB, :]
    if first:
        for j in range(3):
            at = 4 * SLAB + j * NY
            up[at : at + NY, :] = q[j + 1, 3 * SLAB : 3 * SLAB + NY, :]
            down[at : at + NY, :] = q[j, 3 * SLAB : 3 * SLAB + NY, :]
        up[4 * SLAB + 12 :, :] = jnp.zeros((4, NZ), F32)
        down[4 * SLAB + 12 :, :] = jnp.zeros((4, NZ), F32)


def powers_kernel(first, *refs):
    if first:
        q, own, low, high, v0, v1, v2, v3, mom, ec, w0, w1, w2, dg = refs
        for j in range(3):
            at = 4 * SLAB + j * NY
            ec[j * NY : (j + 1) * NY, :] = low[at : at + NY, :]
            ec[(7 + j) * NY : (8 + j) * NY, :] = high[at : at + NY, :]
        for s in range(QUAD):
            ec[(3 + s) * NY : (4 + s) * NY, :] = q[s, 3 * SLAB : 3 * SLAB + NY, :]
    else:
        q, own, low, high, ec, v0, v1, v2, v3, mom, w0, w1, w2, dg = refs

    def rows(ref, at, y):
        return ref[at + y * ROWS : at + (y + 1) * ROWS, :]

    rid = lax.broadcasted_iota(jnp.int32, (ROWS, NZ), 0)
    wx = jnp.where(rid < TRI, 2.0, 1.0)
    wy = jnp.where((rid >= TRI) & (rid < 2 * TRI), 2.0, 1.0)
    wz = jnp.where(rid >= 2 * TRI, 2.0, 1.0)
    lane1 = lax.broadcasted_iota(jnp.int32, (1, NZ), 1)
    em = [[ec[p * NY + y : p * NY + y + 1, :] for y in range(NY)] for p in range(10)]
    zero = jnp.zeros((1, NZ), F32)

    def inside(p, y, val):
        return val if 3 <= p <= 6 else jnp.where(em[p][y] > 0.0, val, 0.0)

    for y in range(NY):
        for p in range(3):
            lo = rows(low, p * SLAB, y)
            hi = rows(high, p * SLAB, y)
            if p == 2:
                lo = lo + rows(q.at[0], 2 * SLAB, y)
            if p == 0:
                hi = hi + rows(q.at[QUAD - 1], SLAB, y)
            w0[p * NY + y] = inside(p, y, lo)
            w0[(7 + p) * NY + y] = inside(7 + p, y, hi)
        for s in range(QUAD):
            r = rows(own.at[s], 0, y)
            if s == 0:
                r = r + rows(low, 3 * SLAB, y)
            if s == QUAD - 1:
                r = r + rows(high, 3 * SLAB, y)
            w0[(3 + s) * NY + y] = r
            v0[s * NY + y] = r

    def face(p, y):
        e = em[p][y]
        xu, xd = faces(e, em[p + 1][y]), faces(e, em[p - 1][y])
        yu = faces(e, em[p][y + 1] if y + 1 < NY else zero)
        yd = faces(e, em[p][y - 1] if y > 0 else zero)
        zu = faces(e, jnp.where(lane1 == NZ - 1, 0.0, pltpu.roll(e, NZ - 1, 1)))
        zd = faces(e, jnp.where(lane1 == 0, 0.0, pltpu.roll(e, 1, 1)))
        return xu, xd, yu, yd, zu, zd

    coef = {}
    for p in range(1, 9):
        for y in range(NY):
            xu, xd, yu, yd, zu, zd = face(p, y)
            dg[p * NY + y] = wx * (xu + xd) + wy * (yu + yd) + wz * (zu + zd) - SHIFT
            coef[p, y] = (
                xu, xd, yu, yd,
                jnp.where(lane1 == NZ - 1, 0.0, zu),
                jnp.where(lane1 == 0, 0.0, zd),
            )

    def apply(src, p, y):
        xu, xd, yu, yd, zu, zd = coef[p, y]
        m = src[p * NY + y]
        t = dg[p * NY + y] * m
        t = t - wx * (xu * src[(p + 1) * NY + y] + xd * src[(p - 1) * NY + y])
        side = None
        if y + 1 < NY:
            side = yu * src[p * NY + y + 1]
        if y > 0:
            less = yd * src[p * NY + y - 1]
            side = less if side is None else side + less
        t = t - wy * side
        t = t - wz * (zu * pltpu.roll(m, NZ - 1, 1) + zd * pltpu.roll(m, 1, 1))
        return inside(p, y, t)

    for p in range(1, 9):
        for y in range(NY):
            t = apply(w0, p, y)
            w1[p * NY + y] = t
            if 3 <= p <= 6:
                v1[(p - 3) * NY + y] = t
    for p in range(2, 8):
        for y in range(NY):
            t = apply(w1, p, y)
            w2[p * NY + y] = t
            if 3 <= p <= 6:
                v2[(p - 3) * NY + y] = t
    sums = [None] * 6
    for p in range(3, 7):
        for y in range(NY):
            a, b, d = w0[p * NY + y], w1[p * NY + y], w2[p * NY + y]
            t = apply(w2, p, y)
            v3[(p - 3) * NY + y] = t
            for j, val in enumerate((a * a, a * b, b * b, b * d, d * d, d * t)):
                sums[j] = val if sums[j] is None else sums[j] + val
    lane = lax.broadcasted_iota(jnp.int32, (ROWS, NZ), 1)
    spot = lane - 8 * (rid % TRI)
    packed = jnp.zeros((ROWS, NZ), F32)
    for j in range(6):
        packed = jnp.where(spot == j, jnp.sum(sums[j], axis=1, keepdims=True), packed)
    mom[...] = jnp.broadcast_to(jnp.sum(packed, axis=0, keepdims=True), mom.shape)


def step_coefficients(mom):
    def inner(a, b):
        total = None
        for i, s in enumerate(a):
            for j, t in enumerate(b):
                term = s * t * mom[i + j]
                total = term if total is None else total + term
        return total

    def image(a):
        q = [SHIFT * s for s in a] + [None]
        for i, s in enumerate(a):
            q[i + 1] = s if q[i + 1] is None else q[i + 1] + s
        return q

    one = jnp.ones_like(mom[0])
    x, r, p = [], [one], [one]
    rr = mom[0]
    for step in range(3):
        q = image(p)
        alpha = rr / inner(p, q)
        x = [x[i] + alpha * s if i < len(x) else alpha * s for i, s in enumerate(p)]
        r = [r[i] - alpha * s if i < len(r) else -alpha * s for i, s in enumerate(q)]
        if step < 2:
            new = inner(r, r)
            beta = new / rr
            p = [s + beta * p[i] if i < len(p) else s for i, s in enumerate(r)]
            rr = new
    return x, r


def update_kernel(first, *refs):
    if first:
        mom, v0, v1, v2, v3, out, rest = refs
    else:
        mom, v0, v1, v2, before, out = refs
    total = jnp.sum(mom[...], axis=0, keepdims=True)
    rid = lax.broadcasted_iota(jnp.int32, (ROWS, NZ), 0)
    lane = lax.broadcasted_iota(jnp.int32, (ROWS, NZ), 1)
    spot = lane - 8 * (rid % TRI)
    picked = [jnp.sum(jnp.where(spot == j, total, 0.0), axis=1, keepdims=True) for j in range(6)]
    x, r = step_coefficients(picked)
    x = [jnp.broadcast_to(s, (ROWS, NZ)) for s in x]
    r = [jnp.broadcast_to(s, (ROWS, NZ)) for s in r]
    for s in range(QUAD):
        for y in range(NY):
            at = s * NY + y
            rows = slice(y * ROWS, (y + 1) * ROWS)
            a, b, d = v0[at], v1[at], v2[at]
            change = x[0] * a + x[1] * b + x[2] * d
            if first:
                rest[s, rows, :] = r[0] * a + r[1] * b + r[2] * d + r[3] * v3[at]
            else:
                change = change + before[s, rows, :]
            out[s, rows, :] = change


def merge_kernel(q, out, copies):
    for y in range(NY):
        for c in range(3):
            for d in range(QUAD):
                at = y * ROWS + c * TRI
                piece = q[d, at : at + TRI, :]
                to = (y * 3 + c) * NM + d * TRI
                out[to : to + TRI, :] = piece
                for g in range(NG // 2):
                    copies[g, to : to + TRI, :] = piece


def packed(field):
    return field[:, :, 0].transpose(2, 1, 0, 3).reshape(NY * 3 * NM, NZ)


def shards(load_modes, first_guess, kl_fields, region_labels, partner, variable, weight):
    mean = jnp.where(region_labels == 0, 1.3, jnp.where(region_labels == 1, 1.0, 0.6)).astype(F32)
    varying = jnp.where(region_labels[None] == 1, kl_fields, 0.0)
    moduli = jnp.concatenate([varying, mean[None]], 0).reshape((NK + 1) * NY, NZ)
    e0 = moduli
    em = lax.ppermute(e0, SLABS, line(64, 1))
    ep = lax.ppermute(e0, SLABS, line(64, -1))
    load = packed(load_modes)
    mine = packed(first_guess)
    copies = jnp.broadcast_to(mine[None], (NG // 2,) + mine.shape)

    half = lax.axis_index("zh") * (NG // 2 * NM)
    offset = half + lax.axis_index("x") * NM
    modes = NG * NM
    own = offset - half + jnp.arange(NM, dtype=jnp.int32)[:, None]
    pad = ((0, 16 - NM), (0, 0))
    rows_partner = (lax.dynamic_slice_in_dim(partner, offset, NM, 0) + modes - half) % modes
    rows_partner = jnp.pad(jnp.concatenate([rows_partner, own], 1), pad, constant_values=-1)
    rows_variable = jnp.pad(lax.dynamic_slice_in_dim(variable, offset, NM, 0), pad)
    rows_weight = lax.dynamic_slice_in_dim(weight, offset, NM, 0)
    rows_weight = jnp.pad(jnp.concatenate([rows_weight, jnp.ones((NM, 1), F32)], 1), pad)
    links = (rows_partner, rows_variable, rows_weight)

    chunk, cells = (QUAD, SLAB, NZ), (QUAD * NY, ROWS, NZ)
    for sweep in range(2):
        first = sweep == 0
        nk = NK + 1 if first else NK
        far = lax.ppermute(mine, "zh", [(0, 1), (1, 0)])
        near = lax.all_to_all(copies, "x", 0, 0, tiled=True)
        far = jnp.broadcast_to(far[None], (NG // 2,) + far.shape)
        far = lax.all_to_all(far, "x", 0, 0, tiled=True)
        fields = (near, far, load, e0, em, ep) if first else (near, far, e0, em, ep)
        face_rows = ((NK + 1) * NY, NZ)
        (sent,) = call(
            functools.partial(coupling_kernel, nk),
            [(QUAD, 3 * SLAB + NY, NZ)],
            [
                (NY * 3, NG * NM, NZ),
                (NY * 3, nk * 16, NZ),
                (2,) + face_rows,
                (2,) + face_rows,
                (5,) + face_rows,
            ],
        )(*fields, *links)
        q = lax.all_to_all(sent, WITHIN, 0, 0, tiled=True)
        edge = (4 * SLAB + 16 if first else 4 * SLAB, NZ)
        chunk_r, up, down = call(functools.partial(edges_kernel, first), [chunk, edge, edge])(
            *((q,) if first else (q, rest))
        )
        low = lax.ppermute(up, CHUNKS, line(16, 1))
        high = lax.ppermute(down, CHUNKS, line(16, -1))
        scratch = [(10 * NY, ROWS, NZ)] * 4
        outs = [cells] * 4 + [(16, NZ)]
        if first:
            v0, v1, v2, v3, mom, ec = call(
                functools.partial(powers_kernel, True), outs + [(10 * NY, NZ)], scratch
            )(q, chunk_r, low, high)
        else:
            v0, v1, v2, v3, mom = call(functools.partial(powers_kernel, False), outs, scratch)(
                q, chunk_r, low, high, ec
            )
        mom = lax.all_to_all(mom, CHUNKS, 0, 0, tiled=True)
        if first:
            change, rest = call(functools.partial(update_kernel, True), [chunk, chunk])(
                mom, v0, v1, v2, v3
            )
        else:
            (change,) = call(functools.partial(update_kernel, False), [chunk])(
                mom, v0, v1, v2, change
            )
        by_slab = lax.all_to_all(change, WITHIN, 0, 0, tiled=True)
        if first:
            rows = (NY * 3 * NM, NZ)
            mine, copies = call(merge_kernel, [rows, (NG // 2,) + rows])(by_slab)
    total = by_slab.reshape(QUAD, NY, 3, TRI, NZ).transpose(0, 3, 2, 1, 4)
    return first_guess + total.reshape(NM, 3, 1, NY, NZ)


def solution(mesh):
    split = Mesh(mesh.devices.reshape(2, 4, 4, 4, 2, 2), AXES)
    mode, space = ("zh", "x"), SLABS
    return jax.shard_map(
        shards,
        mesh=split,
        in_specs=(
            P(mode, None, space, None, None),
            P(mode, None, space, None, None),
            P(None, space, None, None),
            P(space, None, None),
            P(),
            P(),
            P(),
        ),
        out_specs=P(mode, None, space, None, None),
        check_vma=False,
    )
```

```python
import functools

import jax
import jax.numpy as jnp
from jax import lax
from jax.experimental import pallas as pl
from jax.experimental.pallas import tpu as pltpu
from jax.sharding import Mesh
from jax.sharding import PartitionSpec as P

AXES = ("zh", "x", "y", "zp", "zq", "c")
SLABS = ("y", "zp", "zq", "c")
CHUNKS = ("y", "zp")
WITHIN = ("zq", "c")
NG, NM, NL, NK = 8, 12, 8, 8
NY, NZ, SHIFT = 4, 128, 4.0
QUAD = 4
TRI = NM // QUAD
ROWS = 3 * TRI
SLAB = NY * ROWS
F32 = jnp.float32


def line(count, step):
    return [(i, i + step) for i in range(count) if 0 <= i + step < count]


def call(kernel, outs, scratch=()):
    vmem = pl.BlockSpec(memory_space=pltpu.VMEM)

    def run(*args):
        return pl.pallas_call(
            kernel,
            out_shape=[pltpu.VMEM(s, F32) for s in outs],
            in_specs=[vmem] * len(args),
            out_specs=[vmem] * len(outs),
            scratch_shapes=[pltpu.VMEM(s, F32) for s in scratch],
        )(*[pltpu.with_memory_space_constraint(a, pltpu.VMEM) for a in args])

    return run


def faces(e, other):
    return 0.5 * (e + other)


def coupling_kernel(nk, *refs):
    first = nk > NK
    if first:
        (u, load, e0, em, ep, partner, variable, weight, out, us, mx, fx, fy, fz) = refs
    else:
        (u, e0, em, ep, partner, variable, weight, out, us, mx, fx, fy, fz) = refs
    for g in range(NG):
        half, x = divmod(g, NG // 2)
        for y in range(NY):
            for c in range(3):
                yc = y * 3 + c
                if first:
                    at = (half * NY * 3 + yc) * NM
                    us[yc, g * NM : (g + 1) * NM, :] = u[x, at : at + NM, :]
                    continue
                for d in range(QUAD):
                    at, to = half * SLAB + y * ROWS + c * TRI, g * NM + d * TRI
                    us[yc, to : to + TRI, :] = u[x * QUAD + d, at : at + TRI, :]
    lane = lax.broadcasted_iota(jnp.int32, (16, NG * NM), 1)
    pr, vr, wr = partner[...], variable[...], weight[...]
    links = NL + 1 if first else NL
    hit = [jnp.where(lane == pr[:, l : l + 1], wr[:, l : l + 1], 0.0) for l in range(links)]
    blocks = []
    for k in range(nk):
        acc = None
        for l in range(links):
            if (k == NK) != (l == NL):
                continue
            term = hit[l] if l == NL else jnp.where(vr[:, l : l + 1] == k, hit[l], 0.0)
            acc = term if acc is None else acc + term
        blocks.append(acc)
    mix = jnp.concatenate(blocks, axis=0)
    for yc in range(NY * 3):
        mx[yc] = lax.dot_general(
            mix,
            us[yc],
            (((1,), (0,)), ((), ())),
            precision=lax.Precision.HIGHEST,
            preferred_element_type=F32,
        )
    e = e0[...]
    zlane = lax.broadcasted_iota(jnp.int32, e.shape, 1)
    row = lax.broadcasted_iota(jnp.int32, e.shape, 0)
    zup = jnp.where(zlane == NZ - 1, 0.0, pltpu.roll(e, NZ - 1, 1))
    zdn = jnp.where(zlane == 0, 0.0, pltpu.roll(e, 1, 1))
    count = e.shape[0]
    yup = jnp.where(row % NY == NY - 1, 0.0, pltpu.roll(e, count - 1, 0))
    ydn = jnp.where(row % NY == 0, 0.0, pltpu.roll(e, 1, 0))
    fx[0] = faces(e, ep[...])
    fx[1] = faces(e, em[...])
    fy[0] = faces(e, yup)
    fy[1] = faces(e, ydn)
    fzu, fzd = faces(e, zup), faces(e, zdn)
    base = fx[0] + fx[1] + fy[0] + fy[1] + fzu + fzd
    fz[0] = jnp.where(zlane == NZ - 1, 0.0, fzu)
    fz[1] = jnp.where(zlane == 0, 0.0, fzd)
    fz[2] = base + fx[0] + fx[1]
    fz[3] = base + fy[0] + fy[1]
    fz[4] = base + fzu + fzd
    for y in range(NY):
        for c in range(3):
            own = up = down = None
            for k in range(nk):
                r = slice(k * NY + y, k * NY + y + 1)
                rows = slice(k * 16, k * 16 + 16)
                m = mx[y * 3 + c, rows, :]
                t = fz[2 + c, r, :] * m
                side = None
                if y + 1 < NY:
                    side = fy[0, r, :] * mx[(y + 1) * 3 + c, rows, :]
                if y > 0:
                    less = fy[1, r, :] * mx[(y - 1) * 3 + c, rows, :]
                    side = less if side is None else side + less
                t = t - (2.0 * side if c == 1 else side)
                side = fz[0, r, :] * pltpu.roll(m, NZ - 1, 1) + fz[1, r, :] * pltpu.roll(m, 1, 1)
                t = t - (2.0 * side if c == 2 else side)
                p, q = fx[0, r, :] * m, fx[1, r, :] * m
                own, up, down = (t, p, q) if own is None else (own + t, up + p, down + q)
            if c == 0:
                up, down = 2.0 * up, 2.0 * down
            yc = y * 3 + c
            own = load[yc * NM : (yc + 1) * NM, :] - own[:NM] if first else -own[:NM]
            for kind, val in enumerate((own, up, down)):
                at = (kind * NY + y) * ROWS + c * TRI
                for d in range(QUAD):
                    out[d, at : at + TRI, :] = val[d * TRI : (d + 1) * TRI]
    tail = e[NK * NY : NK * NY + NY] if first else jnp.zeros((NY, NZ), F32)
    for d in range(QUAD):
        out[d, 3 * SLAB : 3 * SLAB + NY, :] = tail


def edges_kernel(first, *refs):
    if first:
        q, own, up, down = refs
    else:
        q, rest, own, up, down = refs
    rs = []
    for s in range(QUAD):
        r = q[s, 0:SLAB, :]
        if not first:
            r = r + rest[s]
        if s > 0:
            r = r + q[s - 1, SLAB : 2 * SLAB, :]
        if s + 1 < QUAD:
            r = r + q[s + 1, 2 * SLAB : 3 * SLAB, :]
        own[s] = r
        rs.append(r)
    for j in range(3):
        up[j * SLAB : (j + 1) * SLAB, :] = rs[j + 1]
        down[j * SLAB : (j + 1) * SLAB, :] = rs[j]
    up[3 * SLAB : 4 * SLAB, :] = q[3, SLAB : 2 * SLAB, :]
    down[3 * SLAB : 4 * SLAB, :] = q[0, 2 * SLAB : 3 * SLAB, :]
    if first:
        for j in range(3):
            at = 4 * SLAB + j * NY
            up[at : at + NY, :] = q[j + 1, 3 * SLAB : 3 * SLAB + NY, :]
            down[at : at + NY, :] = q[j, 3 * SLAB : 3 * SLAB + NY, :]
        up[4 * SLAB + 12 :, :] = jnp.zeros((4, NZ), F32)
        down[4 * SLAB + 12 :, :] = jnp.zeros((4, NZ), F32)


def powers_kernel(first, *refs):
    if first:
        q, own, low, high, v0, v1, v2, v3, mom, ec, w0, w1, w2, dg = refs
        for j in range(3):
            at = 4 * SLAB + j * NY
            ec[j * NY : (j + 1) * NY, :] = low[at : at + NY, :]
            ec[(7 + j) * NY : (8 + j) * NY, :] = high[at : at + NY, :]
        for s in range(QUAD):
            ec[(3 + s) * NY : (4 + s) * NY, :] = q[s, 3 * SLAB : 3 * SLAB + NY, :]
    else:
        q, own, low, high, ec, v0, v1, v2, v3, mom, w0, w1, w2, dg = refs

    def rows(ref, at, y):
        return ref[at + y * ROWS : at + (y + 1) * ROWS, :]

    rid = lax.broadcasted_iota(jnp.int32, (ROWS, NZ), 0)
    wx = jnp.where(rid < TRI, 2.0, 1.0)
    wy = jnp.where((rid >= TRI) & (rid < 2 * TRI), 2.0, 1.0)
    wz = jnp.where(rid >= 2 * TRI, 2.0, 1.0)
    lane1 = lax.broadcasted_iota(jnp.int32, (1, NZ), 1)
    em = [[ec[p * NY + y : p * NY + y + 1, :] for y in range(NY)] for p in range(10)]
    zero = jnp.zeros((1, NZ), F32)

    def inside(p, y, val):
        return val if 3 <= p <= 6 else jnp.where(em[p][y] > 0.0, val, 0.0)

    for y in range(NY):
        for p in range(3):
            lo = rows(low, p * SLAB, y)
            hi = rows(high, p * SLAB, y)
            if p == 2:
                lo = lo + rows(q.at[0], 2 * SLAB, y)
            if p == 0:
                hi = hi + rows(q.at[QUAD - 1], SLAB, y)
            w0[p * NY + y] = inside(p, y, lo)
            w0[(7 + p) * NY + y] = inside(7 + p, y, hi)
        for s in range(QUAD):
            r = rows(own.at[s], 0, y)
            if s == 0:
                r = r + rows(low, 3 * SLAB, y)
            if s == QUAD - 1:
                r = r + rows(high, 3 * SLAB, y)
            w0[(3 + s) * NY + y] = r
            v0[s * NY + y] = r

    def face(p, y):
        e = em[p][y]
        xu, xd = faces(e, em[p + 1][y]), faces(e, em[p - 1][y])
        yu = faces(e, em[p][y + 1] if y + 1 < NY else zero)
        yd = faces(e, em[p][y - 1] if y > 0 else zero)
        zu = faces(e, jnp.where(lane1 == NZ - 1, 0.0, pltpu.roll(e, NZ - 1, 1)))
        zd = faces(e, jnp.where(lane1 == 0, 0.0, pltpu.roll(e, 1, 1)))
        return xu, xd, yu, yd, zu, zd

    coef = {}
    for p in range(1, 9):
        for y in range(NY):
            xu, xd, yu, yd, zu, zd = face(p, y)
            dg[p * NY + y] = wx * (xu + xd) + wy * (yu + yd) + wz * (zu + zd) - SHIFT
            coef[p, y] = (
                xu, xd, yu, yd,
                jnp.where(lane1 == NZ - 1, 0.0, zu),
                jnp.where(lane1 == 0, 0.0, zd),
            )

    def apply(src, p, y):
        xu, xd, yu, yd, zu, zd = coef[p, y]
        m = src[p * NY + y]
        t = dg[p * NY + y] * m
        t = t - wx * (xu * src[(p + 1) * NY + y] + xd * src[(p - 1) * NY + y])
        side = None
        if y + 1 < NY:
            side = yu * src[p * NY + y + 1]
        if y > 0:
            less = yd * src[p * NY + y - 1]
            side = less if side is None else side + less
        t = t - wy * side
        t = t - wz * (zu * pltpu.roll(m, NZ - 1, 1) + zd * pltpu.roll(m, 1, 1))
        return inside(p, y, t)

    for p in range(1, 9):
        for y in range(NY):
            t = apply(w0, p, y)
            w1[p * NY + y] = t
            if 3 <= p <= 6:
                v1[(p - 3) * NY + y] = t
    for p in range(2, 8):
        for y in range(NY):
            t = apply(w1, p, y)
            w2[p * NY + y] = t
            if 3 <= p <= 6:
                v2[(p - 3) * NY + y] = t
    sums = [None] * 6
    for p in range(3, 7):
        for y in range(NY):
            a, b, d = w0[p * NY + y], w1[p * NY + y], w2[p * NY + y]
            t = apply(w2, p, y)
            v3[(p - 3) * NY + y] = t
            for j, val in enumerate((a * a, a * b, b * b, b * d, d * d, d * t)):
                sums[j] = val if sums[j] is None else sums[j] + val
    lane = lax.broadcasted_iota(jnp.int32, (ROWS, NZ), 1)
    spot = lane - 8 * (rid % TRI)
    packed = jnp.zeros((ROWS, NZ), F32)
    for j in range(6):
        packed = jnp.where(spot == j, jnp.sum(sums[j], axis=1, keepdims=True), packed)
    mom[...] = jnp.broadcast_to(jnp.sum(packed, axis=0, keepdims=True), mom.shape)


def step_coefficients(mom):
    def inner(a, b):
        total = None
        for i, s in enumerate(a):
            for j, t in enumerate(b):
                term = s * t * mom[i + j]
                total = term if total is None else total + term
        return total

    def image(a):
        q = [SHIFT * s for s in a] + [None]
        for i, s in enumerate(a):
            q[i + 1] = s if q[i + 1] is None else q[i + 1] + s
        return q

    one = jnp.ones_like(mom[0])
    x, r, p = [], [one], [one]
    rr = mom[0]
    for step in range(3):
        q = image(p)
        alpha = rr / inner(p, q)
        x = [x[i] + alpha * s if i < len(x) else alpha * s for i, s in enumerate(p)]
        r = [r[i] - alpha * s if i < len(r) else -alpha * s for i, s in enumerate(q)]
        if step < 2:
            new = inner(r, r)
            beta = new / rr
            p = [s + beta * p[i] if i < len(p) else s for i, s in enumerate(r)]
            rr = new
    return x, r


def update_kernel(first, *refs):
    if first:
        mom, v0, v1, v2, v3, out, rest = refs
    else:
        mom, v0, v1, v2, before, out = refs
    total = jnp.sum(mom[...], axis=0, keepdims=True)
    rid = lax.broadcasted_iota(jnp.int32, (ROWS, NZ), 0)
    lane = lax.broadcasted_iota(jnp.int32, (ROWS, NZ), 1)
    spot = lane - 8 * (rid % TRI)
    picked = [jnp.sum(jnp.where(spot == j, total, 0.0), axis=1, keepdims=True) for j in range(6)]
    x, r = step_coefficients(picked)
    x = [jnp.broadcast_to(s, (ROWS, NZ)) for s in x]
    r = [jnp.broadcast_to(s, (ROWS, NZ)) for s in r]
    for s in range(QUAD):
        for y in range(NY):
            at = s * NY + y
            rows = slice(y * ROWS, (y + 1) * ROWS)
            a, b, d = v0[at], v1[at], v2[at]
            change = x[0] * a + x[1] * b + x[2] * d
            if first:
                rest[s, rows, :] = r[0] * a + r[1] * b + r[2] * d + r[3] * v3[at]
            else:
                change = change + before[s, rows, :]
            out[s, rows, :] = change


def fan_kernel(blocks, near, far, out):
    for d in range(blocks):
        both = jnp.concatenate([near[d], far[d]], axis=0)
        for x in range(NG // 2):
            out[x * blocks + d] = both


def packed(field):
    return field[:, :, 0].transpose(2, 1, 0, 3).reshape(NY * 3 * NM, NZ)


def shards(load_modes, first_guess, kl_fields, region_labels, partner, variable, weight):
    mine = packed(first_guess)
    mine, kl_fields, region_labels = lax.optimization_barrier((mine, kl_fields, region_labels))
    mean = jnp.where(region_labels == 0, 1.3, jnp.where(region_labels == 1, 1.0, 0.6)).astype(F32)
    varying = jnp.where(region_labels[None] == 1, kl_fields, 0.0)
    e0 = jnp.concatenate([varying, mean[None]], 0).reshape((NK + 1) * NY, NZ)
    em = lax.ppermute(e0, SLABS, line(64, 1))
    ep = lax.ppermute(e0, SLABS, line(64, -1))
    load = packed(load_modes)
    swap = [(0, 1), (1, 0)]

    half = lax.axis_index("zh") * (NG // 2 * NM)
    offset = half + lax.axis_index("x") * NM
    modes = NG * NM
    own = offset - half + jnp.arange(NM, dtype=jnp.int32)[:, None]
    pad = ((0, 16 - NM), (0, 0))
    rows_partner = (lax.dynamic_slice_in_dim(partner, offset, NM, 0) + modes - half) % modes
    rows_partner = jnp.pad(jnp.concatenate([rows_partner, own], 1), pad, constant_values=-1)
    rows_variable = jnp.pad(lax.dynamic_slice_in_dim(variable, offset, NM, 0), pad)
    rows_weight = lax.dynamic_slice_in_dim(weight, offset, NM, 0)
    rows_weight = jnp.pad(jnp.concatenate([rows_weight, jnp.ones((NM, 1), F32)], 1), pad)
    links = (rows_partner, rows_variable, rows_weight)

    chunk, cells = (QUAD, SLAB, NZ), (QUAD * NY, ROWS, NZ)
    for sweep in range(2):
        first = sweep == 0
        nk = NK + 1 if first else NK
        blocks = 1 if first else QUAD
        mine = mine.reshape((blocks, -1, NZ))
        far = lax.ppermute(mine, "zh", swap)
        (copies,) = call(
            functools.partial(fan_kernel, blocks), [(NG // 2 * blocks, 2 * mine.shape[1], NZ)]
        )(mine, far)
        u = lax.all_to_all(copies, ("x",) if first else ("x",) + WITHIN, 0, 0, tiled=True)
        fields = (u, load, e0, em, ep) if first else (u, e0, em, ep)
        face_rows = ((NK + 1) * NY, NZ)
        (sent,) = call(
            functools.partial(coupling_kernel, nk),
            [(QUAD, 3 * SLAB + NY, NZ)],
            [
                (NY * 3, NG * NM, NZ),
                (NY * 3, nk * 16, NZ),
                (2,) + face_rows,
                (2,) + face_rows,
                (5,) + face_rows,
            ],
        )(*fields, *links)
        q = lax.all_to_all(sent, WITHIN, 0, 0, tiled=True)
        edge = (4 * SLAB + 16 if first else 4 * SLAB, NZ)
        chunk_r, up, down = call(functools.partial(edges_kernel, first), [chunk, edge, edge])(
            *((q,) if first else (q, rest))
        )
        low = lax.ppermute(up, CHUNKS, line(16, 1))
        high = lax.ppermute(down, CHUNKS, line(16, -1))
        scratch = [(10 * NY, ROWS, NZ)] * 4
        outs = [cells] * 4 + [(16, NZ)]
        if first:
            v0, v1, v2, v3, mom, ec = call(
                functools.partial(powers_kernel, True), outs + [(10 * NY, NZ)], scratch
            )(q, chunk_r, low, high)
        else:
            v0, v1, v2, v3, mom = call(functools.partial(powers_kernel, False), outs, scratch)(
                q, chunk_r, low, high, ec
            )
        mom = lax.all_to_all(mom, CHUNKS, 0, 0, tiled=True)
        if first:
            change, rest = call(functools.partial(update_kernel, True), [chunk, chunk])(
                mom, v0, v1, v2, v3
            )
        else:
            (change,) = call(functools.partial(update_kernel, False), [chunk])(
                mom, v0, v1, v2, change
            )
        mine = change
    by_slab = lax.all_to_all(change, WITHIN, 0, 0, tiled=True)
    total = by_slab.reshape(QUAD, NY, 3, TRI, NZ).transpose(0, 3, 2, 1, 4)
    return first_guess + total.reshape(NM, 3, 1, NY, NZ)


def solution(mesh):
    split = Mesh(mesh.devices.reshape(2, 4, 4, 4, 2, 2), AXES)
    mode, space = ("zh", "x"), SLABS
    return jax.shard_map(
        shards,
        mesh=split,
        in_specs=(
            P(mode, None, space, None, None),
            P(mode, None, space, None, None),
            P(None, space, None, None),
            P(space, None, None),
            P(),
            P(),
            P(),
        ),
        out_specs=P(mode, None, space, None, None),
        check_vma=False,
    )
```

```python
import functools

import jax
import jax.numpy as jnp
from jax import lax
from jax.experimental import pallas as pl
from jax.experimental.pallas import tpu as pltpu
from jax.sharding import Mesh
from jax.sharding import PartitionSpec as P

AXES = ("zh", "x", "y1", "y0", "zp", "zq", "c")
SWAP = [(0, 0), (1, 2), (2, 1), (3, 3)]
GROUPS = ("y0", "x")
SLABS = ("zh", "y1", "zp", "zq", "c")
CHUNKS = ("zh", "y1", "zp")
WITHIN = ("zq", "c")
NG, NM, NL, NK = 8, 12, 8, 8
NY, NZ, SHIFT = 4, 128, 4.0
QUAD = 4
TRI = NM // QUAD
ROWS = 3 * TRI
SLAB = NY * ROWS
F32 = jnp.float32


def line(inner, step):
    def place(i):
        y1, zh, low = i // (2 * inner), i // inner % 2, i % inner
        return (zh * 2 + y1) * inner + low

    count = 4 * inner
    return [(place(i), place(i + step)) for i in range(count) if 0 <= i + step < count]


def call(kernel, outs, scratch=()):
    vmem = pl.BlockSpec(memory_space=pltpu.VMEM)

    def run(*args):
        return pl.pallas_call(
            kernel,
            out_shape=[pltpu.VMEM(s, F32) for s in outs],
            in_specs=[vmem] * len(args),
            out_specs=[vmem] * len(outs),
            scratch_shapes=[pltpu.VMEM(s, F32) for s in scratch],
        )(*[pltpu.with_memory_space_constraint(a, pltpu.VMEM) for a in args])

    return run


def faces(e, other):
    return 0.5 * (e + other)


def coupling_kernel(nk, *refs):
    first = nk > NK
    if first:
        (u, load, e0, em, ep, partner, variable, weight, out, us, mx, fx, fy, fz) = refs
    else:
        (u, e0, em, ep, partner, variable, weight, out, us, mx, fx, fy, fz) = refs
    for g in range(NG):
        for yc in range(NY * 3):
            us[yc, g * NM : (g + 1) * NM, :] = u[g, yc * NM : (yc + 1) * NM, :]
    lane = lax.broadcasted_iota(jnp.int32, (16, NG * NM), 1)
    pr, vr, wr = partner[...], variable[...], weight[...]
    links = NL + 1 if first else NL
    hit = [jnp.where(lane == pr[:, l : l + 1], wr[:, l : l + 1], 0.0) for l in range(links)]
    blocks = []
    for k in range(nk):
        acc = None
        for l in range(links):
            if (k == NK) != (l == NL):
                continue
            term = hit[l] if l == NL else jnp.where(vr[:, l : l + 1] == k, hit[l], 0.0)
            acc = term if acc is None else acc + term
        blocks.append(acc)
    mix = jnp.concatenate(blocks, axis=0)
    for yc in range(NY * 3):
        mx[yc] = lax.dot_general(
            mix,
            us[yc],
            (((1,), (0,)), ((), ())),
            precision=lax.Precision.HIGHEST,
            preferred_element_type=F32,
        )
    e = e0[...]
    zlane = lax.broadcasted_iota(jnp.int32, e.shape, 1)
    row = lax.broadcasted_iota(jnp.int32, e.shape, 0)
    zup = jnp.where(zlane == NZ - 1, 0.0, pltpu.roll(e, NZ - 1, 1))
    zdn = jnp.where(zlane == 0, 0.0, pltpu.roll(e, 1, 1))
    count = e.shape[0]
    yup = jnp.where(row % NY == NY - 1, 0.0, pltpu.roll(e, count - 1, 0))
    ydn = jnp.where(row % NY == 0, 0.0, pltpu.roll(e, 1, 0))
    fx[0] = faces(e, ep[...])
    fx[1] = faces(e, em[...])
    fy[0] = faces(e, yup)
    fy[1] = faces(e, ydn)
    fzu, fzd = faces(e, zup), faces(e, zdn)
    base = fx[0] + fx[1] + fy[0] + fy[1] + fzu + fzd
    fz[0] = jnp.where(zlane == NZ - 1, 0.0, fzu)
    fz[1] = jnp.where(zlane == 0, 0.0, fzd)
    fz[2] = base + fx[0] + fx[1]
    fz[3] = base + fy[0] + fy[1]
    fz[4] = base + fzu + fzd
    for y in range(NY):
        for c in range(3):
            own = up = down = None
            for k in range(nk):
                r = slice(k * NY + y, k * NY + y + 1)
                rows = slice(k * 16, k * 16 + 16)
                m = mx[y * 3 + c, rows, :]
                t = fz[2 + c, r, :] * m
                side = None
                if y + 1 < NY:
                    side = fy[0, r, :] * mx[(y + 1) * 3 + c, rows, :]
                if y > 0:
                    less = fy[1, r, :] * mx[(y - 1) * 3 + c, rows, :]
                    side = less if side is None else side + less
                t = t - (2.0 * side if c == 1 else side)
                side = fz[0, r, :] * pltpu.roll(m, NZ - 1, 1) + fz[1, r, :] * pltpu.roll(m, 1, 1)
                t = t - (2.0 * side if c == 2 else side)
                p, q = fx[0, r, :] * m, fx[1, r, :] * m
                own, up, down = (t, p, q) if own is None else (own + t, up + p, down + q)
            if c == 0:
                up, down = 2.0 * up, 2.0 * down
            yc = y * 3 + c
            own = load[yc * NM : (yc + 1) * NM, :] - own[:NM] if first else -own[:NM]
            for kind, val in enumerate((own, up, down)):
                at = (kind * NY + y) * ROWS + c * TRI
                for d in range(QUAD):
                    out[d, at : at + TRI, :] = val[d * TRI : (d + 1) * TRI]
    tail = e[NK * NY : NK * NY + NY] if first else jnp.zeros((NY, NZ), F32)
    for d in range(QUAD):
        out[d, 3 * SLAB : 3 * SLAB + NY, :] = tail


def edges_kernel(first, *refs):
    if first:
        q, own, up, down = refs
    else:
        q, rest, own, up, down = refs
    rs = []
    for s in range(QUAD):
        r = q[s, 0:SLAB, :]
        if not first:
            r = r + rest[s]
        if s > 0:
            r = r + q[s - 1, SLAB : 2 * SLAB, :]
        if s + 1 < QUAD:
            r = r + q[s + 1, 2 * SLAB : 3 * SLAB, :]
        own[s] = r
        rs.append(r)
    for j in range(3):
        up[j * SLAB : (j + 1) * SLAB, :] = rs[j + 1]
        down[j * SLAB : (j + 1) * SLAB, :] = rs[j]
    up[3 * SLAB : 4 * SLAB, :] = q[3, SLAB : 2 * SLAB, :]
    down[3 * SLAB : 4 * SLAB, :] = q[0, 2 * SLAB : 3 * SLAB, :]
    if first:
        for j in range(3):
            at = 4 * SLAB + j * NY
            up[at : at + NY, :] = q[j + 1, 3 * SLAB : 3 * SLAB + NY, :]
            down[at : at + NY, :] = q[j, 3 * SLAB : 3 * SLAB + NY, :]
        up[4 * SLAB + 12 :, :] = jnp.zeros((4, NZ), F32)
        down[4 * SLAB + 12 :, :] = jnp.zeros((4, NZ), F32)


def powers_kernel(first, *refs):
    if first:
        q, own, low, high, v0, v1, v2, v3, mom, ec, w0, w1, w2, dg = refs
        for j in range(3):
            at = 4 * SLAB + j * NY
            ec[j * NY : (j + 1) * NY, :] = low[at : at + NY, :]
            ec[(7 + j) * NY : (8 + j) * NY, :] = high[at : at + NY, :]
        for s in range(QUAD):
            ec[(3 + s) * NY : (4 + s) * NY, :] = q[s, 3 * SLAB : 3 * SLAB + NY, :]
    else:
        q, own, low, high, ec, v0, v1, v2, v3, mom, w0, w1, w2, dg = refs

    def rows(ref, at, y):
        return ref[at + y * ROWS : at + (y + 1) * ROWS, :]

    rid = lax.broadcasted_iota(jnp.int32, (ROWS, NZ), 0)
    wx = jnp.where(rid < TRI, 2.0, 1.0)
    wy = jnp.where((rid >= TRI) & (rid < 2 * TRI), 2.0, 1.0)
    wz = jnp.where(rid >= 2 * TRI, 2.0, 1.0)
    lane1 = lax.broadcasted_iota(jnp.int32, (1, NZ), 1)
    em = [[ec[p * NY + y : p * NY + y + 1, :] for y in range(NY)] for p in range(10)]
    zero = jnp.zeros((1, NZ), F32)

    def inside(p, y, val):
        return val if 3 <= p <= 6 else jnp.where(em[p][y] > 0.0, val, 0.0)

    for y in range(NY):
        for p in range(3):
            lo = rows(low, p * SLAB, y)
            hi = rows(high, p * SLAB, y)
            if p == 2:
                lo = lo + rows(q.at[0], 2 * SLAB, y)
            if p == 0:
                hi = hi + rows(q.at[QUAD - 1], SLAB, y)
            w0[p * NY + y] = inside(p, y, lo)
            w0[(7 + p) * NY + y] = inside(7 + p, y, hi)
        for s in range(QUAD):
            r = rows(own.at[s], 0, y)
            if s == 0:
                r = r + rows(low, 3 * SLAB, y)
            if s == QUAD - 1:
                r = r + rows(high, 3 * SLAB, y)
            w0[(3 + s) * NY + y] = r
            v0[s * NY + y] = r

    def face(p, y):
        e = em[p][y]
        xu, xd = faces(e, em[p + 1][y]), faces(e, em[p - 1][y])
        yu = faces(e, em[p][y + 1] if y + 1 < NY else zero)
        yd = faces(e, em[p][y - 1] if y > 0 else zero)
        zu = faces(e, jnp.where(lane1 == NZ - 1, 0.0, pltpu.roll(e, NZ - 1, 1)))
        zd = faces(e, jnp.where(lane1 == 0, 0.0, pltpu.roll(e, 1, 1)))
        return xu, xd, yu, yd, zu, zd

    coef = {}
    for p in range(1, 9):
        for y in range(NY):
            xu, xd, yu, yd, zu, zd = face(p, y)
            dg[p * NY + y] = wx * (xu + xd) + wy * (yu + yd) + wz * (zu + zd) - SHIFT
            coef[p, y] = (
                xu, xd, yu, yd,
                jnp.where(lane1 == NZ - 1, 0.0, zu),
                jnp.where(lane1 == 0, 0.0, zd),
            )

    def apply(src, p, y):
        xu, xd, yu, yd, zu, zd = coef[p, y]
        m = src[p * NY + y]
        t = dg[p * NY + y] * m
        t = t - wx * (xu * src[(p + 1) * NY + y] + xd * src[(p - 1) * NY + y])
        side = None
        if y + 1 < NY:
            side = yu * src[p * NY + y + 1]
        if y > 0:
            less = yd * src[p * NY + y - 1]
            side = less if side is None else side + less
        t = t - wy * side
        t = t - wz * (zu * pltpu.roll(m, NZ - 1, 1) + zd * pltpu.roll(m, 1, 1))
        return inside(p, y, t)

    for p in range(1, 9):
        for y in range(NY):
            t = apply(w0, p, y)
            w1[p * NY + y] = t
            if 3 <= p <= 6:
                v1[(p - 3) * NY + y] = t
    for p in range(2, 8):
        for y in range(NY):
            t = apply(w1, p, y)
            w2[p * NY + y] = t
            if 3 <= p <= 6:
                v2[(p - 3) * NY + y] = t
    sums = [None] * 6
    for p in range(3, 7):
        for y in range(NY):
            a, b, d = w0[p * NY + y], w1[p * NY + y], w2[p * NY + y]
            t = apply(w2, p, y)
            v3[(p - 3) * NY + y] = t
            for j, val in enumerate((a * a, a * b, b * b, b * d, d * d, d * t)):
                sums[j] = val if sums[j] is None else sums[j] + val
    lane = lax.broadcasted_iota(jnp.int32, (ROWS, NZ), 1)
    spot = lane - 8 * (rid % TRI)
    packed = jnp.zeros((ROWS, NZ), F32)
    for j in range(6):
        packed = jnp.where(spot == j, jnp.sum(sums[j], axis=1, keepdims=True), packed)
    mom[...] = jnp.broadcast_to(jnp.sum(packed, axis=0, keepdims=True), mom.shape)


def step_coefficients(mom):
    def inner(a, b):
        total = None
        for i, s in enumerate(a):
            for j, t in enumerate(b):
                term = s * t * mom[i + j]
                total = term if total is None else total + term
        return total

    def image(a):
        q = [SHIFT * s for s in a] + [None]
        for i, s in enumerate(a):
            q[i + 1] = s if q[i + 1] is None else q[i + 1] + s
        return q

    one = jnp.ones_like(mom[0])
    x, r, p = [], [one], [one]
    rr = mom[0]
    for step in range(3):
        q = image(p)
        alpha = rr / inner(p, q)
        x = [x[i] + alpha * s if i < len(x) else alpha * s for i, s in enumerate(p)]
        r = [r[i] - alpha * s if i < len(r) else -alpha * s for i, s in enumerate(q)]
        if step < 2:
            new = inner(r, r)
            beta = new / rr
            p = [s + beta * p[i] if i < len(p) else s for i, s in enumerate(r)]
            rr = new
    return x, r


def update_kernel(first, *refs):
    if first:
        mom, v0, v1, v2, v3, out, rest = refs
    else:
        mom, v0, v1, v2, before, out = refs
    total = jnp.sum(mom[...], axis=0, keepdims=True)
    rid = lax.broadcasted_iota(jnp.int32, (ROWS, NZ), 0)
    lane = lax.broadcasted_iota(jnp.int32, (ROWS, NZ), 1)
    spot = lane - 8 * (rid % TRI)
    picked = [jnp.sum(jnp.where(spot == j, total, 0.0), axis=1, keepdims=True) for j in range(6)]
    x, r = step_coefficients(picked)
    x = [jnp.broadcast_to(s, (ROWS, NZ)) for s in x]
    r = [jnp.broadcast_to(s, (ROWS, NZ)) for s in r]
    for s in range(QUAD):
        for y in range(NY):
            at = s * NY + y
            rows = slice(y * ROWS, (y + 1) * ROWS)
            a, b, d = v0[at], v1[at], v2[at]
            change = x[0] * a + x[1] * b + x[2] * d
            if first:
                rest[s, rows, :] = r[0] * a + r[1] * b + r[2] * d + r[3] * v3[at]
            else:
                change = change + before[s, rows, :]
            out[s, rows, :] = change


def fan_kernel(field, out):
    own = field[: NY * 3 * NM, :]
    for g in range(NG):
        out[g] = own


def merge_kernel(q, out):
    for y in range(NY):
        for c in range(3):
            pieces = []
            for d in range(QUAD):
                at = y * ROWS + c * TRI
                pieces.append(q[d, at : at + TRI, :])
            own = jnp.concatenate(pieces, axis=0)
            to = (y * 3 + c) * NM
            for g in range(NG):
                out[g, to : to + NM, :] = own


def packed(field):
    return field[:, :, 0].transpose(2, 1, 0, 3).reshape(NY * 3 * NM, NZ)


def shards(load_modes, first_guess, kl_fields, region_labels, partner, variable, weight):
    mean = jnp.where(region_labels == 0, 1.3, jnp.where(region_labels == 1, 1.0, 0.6)).astype(F32)
    varying = jnp.where(region_labels[None] == 1, kl_fields, 0.0)
    moduli = jnp.concatenate([varying, mean[None]], 0).reshape((NK + 1) * NY, NZ)
    guess = jnp.concatenate([packed(first_guess), moduli], 0)
    guess = lax.ppermute(guess, ("zh", "y0"), SWAP)
    load = lax.ppermute(packed(load_modes), ("zh", "y0"), SWAP)
    e0 = guess[NY * 3 * NM :]
    em = lax.ppermute(e0, SLABS, line(16, 1))
    ep = lax.ppermute(e0, SLABS, line(16, -1))

    offset = (lax.axis_index("y0") * 4 + lax.axis_index("x")) * NM
    own = offset + jnp.arange(NM, dtype=jnp.int32)[:, None]
    pad = ((0, 16 - NM), (0, 0))
    rows_partner = lax.dynamic_slice_in_dim(partner, offset, NM, 0)
    rows_partner = jnp.pad(jnp.concatenate([rows_partner, own], 1), pad, constant_values=-1)
    rows_variable = jnp.pad(lax.dynamic_slice_in_dim(variable, offset, NM, 0), pad)
    rows_weight = lax.dynamic_slice_in_dim(weight, offset, NM, 0)
    rows_weight = jnp.pad(jnp.concatenate([rows_weight, jnp.ones((NM, 1), F32)], 1), pad)
    links = (rows_partner, rows_variable, rows_weight)

    chunk, cells = (QUAD, SLAB, NZ), (QUAD * NY, ROWS, NZ)
    for sweep in range(2):
        first = sweep == 0
        nk = NK + 1 if first else NK
        kernel = fan_kernel if first else merge_kernel
        (copies,) = call(kernel, [(NG, NY * 3 * NM, NZ)])(guess if first else by_slab)
        u = lax.all_to_all(copies, GROUPS, 0, 0, tiled=True)
        fields = (u, load, e0, em, ep) if first else (u, e0, em, ep)
        face_rows = ((NK + 1) * NY, NZ)
        (sent,) = call(
            functools.partial(coupling_kernel, nk),
            [(QUAD, 3 * SLAB + NY, NZ)],
            [
                (NY * 3, NG * NM, NZ),
                (NY * 3, nk * 16, NZ),
                (2,) + face_rows,
                (2,) + face_rows,
                (5,) + face_rows,
            ],
        )(*fields, *links)
        q = lax.all_to_all(sent, WITHIN, 0, 0, tiled=True)
        edge = (4 * SLAB + 16 if first else 4 * SLAB, NZ)
        chunk_r, up, down = call(functools.partial(edges_kernel, first), [chunk, edge, edge])(
            *((q,) if first else (q, rest))
        )
        low = lax.ppermute(up, CHUNKS, line(4, 1))
        high = lax.ppermute(down, CHUNKS, line(4, -1))
        scratch = [(10 * NY, ROWS, NZ)] * 4
        outs = [cells] * 4 + [(16, NZ)]
        if first:
            v0, v1, v2, v3, mom, ec = call(
                functools.partial(powers_kernel, True), outs + [(10 * NY, NZ)], scratch
            )(q, chunk_r, low, high)
        else:
            v0, v1, v2, v3, mom = call(functools.partial(powers_kernel, False), outs, scratch)(
                q, chunk_r, low, high, ec
            )
        mom = lax.all_to_all(mom, CHUNKS, 0, 0, tiled=True)
        if first:
            change, rest = call(functools.partial(update_kernel, True), [chunk, chunk])(
                mom, v0, v1, v2, v3
            )
        else:
            (change,) = call(functools.partial(update_kernel, False), [chunk])(
                mom, v0, v1, v2, change
            )
        by_slab = lax.all_to_all(change, WITHIN, 0, 0, tiled=True)
    total = lax.ppermute(by_slab, ("zh", "y0"), SWAP)
    total = total.reshape(QUAD, NY, 3, TRI, NZ).transpose(0, 3, 2, 1, 4)
    return first_guess + total.reshape(NM, 3, 1, NY, NZ)


def solution(mesh):
    split = Mesh(mesh.devices.reshape(2, 4, 2, 2, 4, 2, 2), AXES)
    mode, space = ("zh", "x"), ("y1", "y0", "zp", "zq", "c")
    return jax.shard_map(
        shards,
        mesh=split,
        in_specs=(
            P(mode, None, space, None, None),
            P(mode, None, space, None, None),
            P(None, space, None, None),
            P(space, None, None),
            P(),
            P(),
            P(),
        ),
        out_specs=P(mode, None, space, None, None),
        check_vma=False,
    )
```

```python
import functools

import jax
import jax.numpy as jnp
from jax import lax
from jax.experimental import pallas as pl
from jax.experimental.pallas import tpu as pltpu
from jax.sharding import Mesh
from jax.sharding import PartitionSpec as P

AXES = ("zh", "x", "y1", "y0", "zp", "zq", "c")
SWAP = [(0, 0), (1, 2), (2, 1), (3, 3)]
GROUPS = ("y0", "x")
SLABS = ("zh", "y1", "y0", "zp", "zq", "c")
LINES = ("zh", "y1", "y0", "zp")
CHUNKS = ("zh", "y1", "zp")
WITHIN = ("zq", "c")
NG, NM, NL, NK = 8, 12, 8, 8
NY, NZ, SHIFT = 4, 128, 4.0
QUAD = 4
TRI = NM // QUAD
ROWS = 3 * TRI
SLAB = NY * ROWS
F32 = jnp.float32


def line(inner, step, held=False):
    def place(i):
        y1, zh, low = i // (2 * inner), i // inner % 2, i % inner
        first = zh * 2 + y1
        return ((first * 2 + zh) if held else first) * inner + low

    count = 4 * inner
    return [(place(i), place(i + step)) for i in range(count) if 0 <= i + step < count]


def call(kernel, outs, scratch=()):
    vmem = pl.BlockSpec(memory_space=pltpu.VMEM)

    def run(*args):
        return pl.pallas_call(
            kernel,
            out_shape=[pltpu.VMEM(s, F32) for s in outs],
            in_specs=[vmem] * len(args),
            out_specs=[vmem] * len(outs),
            scratch_shapes=[pltpu.VMEM(s, F32) for s in scratch],
        )(*[pltpu.with_memory_space_constraint(a, pltpu.VMEM) for a in args])

    return run


def faces(e, other):
    return 0.5 * (e + other)


def coupling_kernel(nk, *refs):
    first = nk > NK
    if first:
        (u, load, e0, em, ep, partner, variable, weight, out, us, mx, fx, fy, fz) = refs
    else:
        (u, e0, em, ep, partner, variable, weight, out, us, mx, fx, fy, fz) = refs
    for g in range(NG):
        for yc in range(NY * 3):
            us[yc, g * NM : (g + 1) * NM, :] = u[g, yc * NM : (yc + 1) * NM, :]
    lane = lax.broadcasted_iota(jnp.int32, (16, NG * NM), 1)
    pr, vr, wr = partner[...], variable[...], weight[...]
    links = NL + 1 if first else NL
    hit = [jnp.where(lane == pr[:, l : l + 1], wr[:, l : l + 1], 0.0) for l in range(links)]
    blocks = []
    for k in range(nk):
        acc = None
        for l in range(links):
            if (k == NK) != (l == NL):
                continue
            term = hit[l] if l == NL else jnp.where(vr[:, l : l + 1] == k, hit[l], 0.0)
            acc = term if acc is None else acc + term
        blocks.append(acc)
    mix = jnp.concatenate(blocks, axis=0)
    for yc in range(NY * 3):
        mx[yc] = lax.dot_general(
            mix,
            us[yc],
            (((1,), (0,)), ((), ())),
            precision=lax.Precision.HIGHEST,
            preferred_element_type=F32,
        )
    e = e0[...]
    zlane = lax.broadcasted_iota(jnp.int32, e.shape, 1)
    row = lax.broadcasted_iota(jnp.int32, e.shape, 0)
    zup = jnp.where(zlane == NZ - 1, 0.0, pltpu.roll(e, NZ - 1, 1))
    zdn = jnp.where(zlane == 0, 0.0, pltpu.roll(e, 1, 1))
    count = e.shape[0]
    yup = jnp.where(row % NY == NY - 1, 0.0, pltpu.roll(e, count - 1, 0))
    ydn = jnp.where(row % NY == 0, 0.0, pltpu.roll(e, 1, 0))
    fx[0] = faces(e, ep[...])
    fx[1] = faces(e, em[...])
    fy[0] = faces(e, yup)
    fy[1] = faces(e, ydn)
    fzu, fzd = faces(e, zup), faces(e, zdn)
    base = fx[0] + fx[1] + fy[0] + fy[1] + fzu + fzd
    fz[0] = jnp.where(zlane == NZ - 1, 0.0, fzu)
    fz[1] = jnp.where(zlane == 0, 0.0, fzd)
    fz[2] = base + fx[0] + fx[1]
    fz[3] = base + fy[0] + fy[1]
    fz[4] = base + fzu + fzd
    for y in range(NY):
        for c in range(3):
            own = up = down = None
            for k in range(nk):
                r = slice(k * NY + y, k * NY + y + 1)
                rows = slice(k * 16, k * 16 + 16)
                m = mx[y * 3 + c, rows, :]
                t = fz[2 + c, r, :] * m
                side = None
                if y + 1 < NY:
                    side = fy[0, r, :] * mx[(y + 1) * 3 + c, rows, :]
                if y > 0:
                    less = fy[1, r, :] * mx[(y - 1) * 3 + c, rows, :]
                    side = less if side is None else side + less
                t = t - (2.0 * side if c == 1 else side)
                side = fz[0, r, :] * pltpu.roll(m, NZ - 1, 1) + fz[1, r, :] * pltpu.roll(m, 1, 1)
                t = t - (2.0 * side if c == 2 else side)
                p, q = fx[0, r, :] * m, fx[1, r, :] * m
                own, up, down = (t, p, q) if own is None else (own + t, up + p, down + q)
            if c == 0:
                up, down = 2.0 * up, 2.0 * down
            yc = y * 3 + c
            own = load[yc * NM : (yc + 1) * NM, :] - own[:NM] if first else -own[:NM]
            for kind, val in enumerate((own, up, down)):
                at = (kind * NY + y) * ROWS + c * TRI
                for d in range(QUAD):
                    out[d, at : at + TRI, :] = val[d * TRI : (d + 1) * TRI]
    tail = e[NK * NY : NK * NY + NY] if first else jnp.zeros((NY, NZ), F32)
    for d in range(QUAD):
        out[d, 3 * SLAB : 3 * SLAB + NY, :] = tail


def edges_kernel(first, *refs):
    if first:
        q, own, up, down = refs
    else:
        q, rest, own, up, down = refs
    rs = []
    for s in range(QUAD):
        r = q[s, 0:SLAB, :]
        if not first:
            r = r + rest[s]
        if s > 0:
            r = r + q[s - 1, SLAB : 2 * SLAB, :]
        if s + 1 < QUAD:
            r = r + q[s + 1, 2 * SLAB : 3 * SLAB, :]
        own[s] = r
        rs.append(r)
    for j in range(3):
        up[j * SLAB : (j + 1) * SLAB, :] = rs[j + 1]
        down[j * SLAB : (j + 1) * SLAB, :] = rs[j]
    up[3 * SLAB : 4 * SLAB, :] = q[3, SLAB : 2 * SLAB, :]
    down[3 * SLAB : 4 * SLAB, :] = q[0, 2 * SLAB : 3 * SLAB, :]
    if first:
        for j in range(3):
            at = 4 * SLAB + j * NY
            up[at : at + NY, :] = q[j + 1, 3 * SLAB : 3 * SLAB + NY, :]
            down[at : at + NY, :] = q[j, 3 * SLAB : 3 * SLAB + NY, :]
        up[4 * SLAB + 12 :, :] = jnp.zeros((4, NZ), F32)
        down[4 * SLAB + 12 :, :] = jnp.zeros((4, NZ), F32)


def powers_kernel(first, *refs):
    if first:
        q, own, low, high, v0, v1, v2, v3, mom, ec, w0, w1, w2, dg = refs
        for j in range(3):
            at = 4 * SLAB + j * NY
            ec[j * NY : (j + 1) * NY, :] = low[at : at + NY, :]
            ec[(7 + j) * NY : (8 + j) * NY, :] = high[at : at + NY, :]
        for s in range(QUAD):
            ec[(3 + s) * NY : (4 + s) * NY, :] = q[s, 3 * SLAB : 3 * SLAB + NY, :]
    else:
        q, own, low, high, ec, before, stack, mom, w0, w1, w2, dg = refs
        v0 = v1 = v2 = v3 = None
        stack[3] = before[...]

    def rows(ref, at, y):
        return ref[at + y * ROWS : at + (y + 1) * ROWS, :]

    def keep(k, s, y, val):
        if first:
            (v0, v1, v2, v3)[k][s * NY + y] = val
        elif k < 3:
            stack[k, s, y * ROWS : (y + 1) * ROWS, :] = val

    rid = lax.broadcasted_iota(jnp.int32, (ROWS, NZ), 0)
    wx = jnp.where(rid < TRI, 2.0, 1.0)
    wy = jnp.where((rid >= TRI) & (rid < 2 * TRI), 2.0, 1.0)
    wz = jnp.where(rid >= 2 * TRI, 2.0, 1.0)
    lane1 = lax.broadcasted_iota(jnp.int32, (1, NZ), 1)
    em = [[ec[p * NY + y : p * NY + y + 1, :] for y in range(NY)] for p in range(10)]
    zero = jnp.zeros((1, NZ), F32)

    def inside(p, y, val):
        return val if 3 <= p <= 6 else jnp.where(em[p][y] > 0.0, val, 0.0)

    for y in range(NY):
        for p in range(3):
            lo = rows(low, p * SLAB, y)
            hi = rows(high, p * SLAB, y)
            if p == 2:
                lo = lo + rows(q.at[0], 2 * SLAB, y)
            if p == 0:
                hi = hi + rows(q.at[QUAD - 1], SLAB, y)
            w0[p * NY + y] = inside(p, y, lo)
            w0[(7 + p) * NY + y] = inside(7 + p, y, hi)
        for s in range(QUAD):
            r = rows(own.at[s], 0, y)
            if s == 0:
                r = r + rows(low, 3 * SLAB, y)
            if s == QUAD - 1:
                r = r + rows(high, 3 * SLAB, y)
            w0[(3 + s) * NY + y] = r
            keep(0, s, y, r)

    def face(p, y):
        e = em[p][y]
        xu, xd = faces(e, em[p + 1][y]), faces(e, em[p - 1][y])
        yu = faces(e, em[p][y + 1] if y + 1 < NY else zero)
        yd = faces(e, em[p][y - 1] if y > 0 else zero)
        zu = faces(e, jnp.where(lane1 == NZ - 1, 0.0, pltpu.roll(e, NZ - 1, 1)))
        zd = faces(e, jnp.where(lane1 == 0, 0.0, pltpu.roll(e, 1, 1)))
        return xu, xd, yu, yd, zu, zd

    coef = {}
    for p in range(1, 9):
        for y in range(NY):
            xu, xd, yu, yd, zu, zd = face(p, y)
            dg[p * NY + y] = wx * (xu + xd) + wy * (yu + yd) + wz * (zu + zd) - SHIFT
            coef[p, y] = (
                xu, xd, yu, yd,
                jnp.where(lane1 == NZ - 1, 0.0, zu),
                jnp.where(lane1 == 0, 0.0, zd),
            )

    def apply(src, p, y):
        xu, xd, yu, yd, zu, zd = coef[p, y]
        m = src[p * NY + y]
        t = dg[p * NY + y] * m
        t = t - wx * (xu * src[(p + 1) * NY + y] + xd * src[(p - 1) * NY + y])
        side = None
        if y + 1 < NY:
            side = yu * src[p * NY + y + 1]
        if y > 0:
            less = yd * src[p * NY + y - 1]
            side = less if side is None else side + less
        t = t - wy * side
        t = t - wz * (zu * pltpu.roll(m, NZ - 1, 1) + zd * pltpu.roll(m, 1, 1))
        return inside(p, y, t)

    for p in range(1, 9):
        for y in range(NY):
            t = apply(w0, p, y)
            w1[p * NY + y] = t
            if 3 <= p <= 6:
                keep(1, p - 3, y, t)
    for p in range(2, 8):
        for y in range(NY):
            t = apply(w1, p, y)
            w2[p * NY + y] = t
            if 3 <= p <= 6:
                keep(2, p - 3, y, t)
    sums = [None] * 6
    for p in range(3, 7):
        for y in range(NY):
            a, b, d = w0[p * NY + y], w1[p * NY + y], w2[p * NY + y]
            t = apply(w2, p, y)
            keep(3, p - 3, y, t)
            for j, val in enumerate((a * a, a * b, b * b, b * d, d * d, d * t)):
                sums[j] = val if sums[j] is None else sums[j] + val
    lane = lax.broadcasted_iota(jnp.int32, (ROWS, NZ), 1)
    spot = lane - 8 * (rid % TRI)
    packed = jnp.zeros((ROWS, NZ), F32)
    for j in range(6):
        packed = jnp.where(spot == j, jnp.sum(sums[j], axis=1, keepdims=True), packed)
    mom[...] = jnp.broadcast_to(jnp.sum(packed, axis=0, keepdims=True), mom.shape)


def step_coefficients(mom):
    def inner(a, b):
        total = None
        for i, s in enumerate(a):
            for j, t in enumerate(b):
                term = s * t * mom[i + j]
                total = term if total is None else total + term
        return total

    def image(a):
        q = [SHIFT * s for s in a] + [None]
        for i, s in enumerate(a):
            q[i + 1] = s if q[i + 1] is None else q[i + 1] + s
        return q

    one = jnp.ones_like(mom[0])
    x, r, p = [], [one], [one]
    rr = mom[0]
    for step in range(3):
        q = image(p)
        alpha = rr / inner(p, q)
        x = [x[i] + alpha * s if i < len(x) else alpha * s for i, s in enumerate(p)]
        r = [r[i] - alpha * s if i < len(r) else -alpha * s for i, s in enumerate(q)]
        if step < 2:
            new = inner(r, r)
            beta = new / rr
            p = [s + beta * p[i] if i < len(p) else s for i, s in enumerate(r)]
            rr = new
    return x, r


def update_kernel(first, *refs):
    if first:
        mom, v0, v1, v2, v3, out, rest = refs
    else:
        mom, kept, stack, out = refs
    shares = mom[...] if first else jnp.where(kept[...] > 0.0, mom[...], 0.0)
    total = jnp.sum(shares, axis=0, keepdims=True)
    rid = lax.broadcasted_iota(jnp.int32, (ROWS, NZ), 0)
    lane = lax.broadcasted_iota(jnp.int32, (ROWS, NZ), 1)
    spot = lane - 8 * (rid % TRI)
    picked = [jnp.sum(jnp.where(spot == j, total, 0.0), axis=1, keepdims=True) for j in range(6)]
    x, r = step_coefficients(picked)
    x = [jnp.broadcast_to(s, (ROWS, NZ)) for s in x]
    r = [jnp.broadcast_to(s, (ROWS, NZ)) for s in r]
    for s in range(QUAD):
        for y in range(NY):
            at = s * NY + y
            rows = slice(y * ROWS, (y + 1) * ROWS)
            a, b, d = (v0[at], v1[at], v2[at]) if first else (stack[k, s, rows, :] for k in range(3))
            change = x[0] * a + x[1] * b + x[2] * d
            if first:
                rest[s, rows, :] = r[0] * a + r[1] * b + r[2] * d + r[3] * v3[at]
            else:
                change = change + stack[3, s, rows, :]
            out[s, rows, :] = change


def fan_kernel(field, out):
    own = field[: NY * 3 * NM, :]
    for g in range(NG):
        out[g] = own


def merge_kernel(q, out):
    for y in range(NY):
        for c in range(3):
            pieces = []
            for d in range(QUAD):
                at = y * ROWS + c * TRI
                pieces.append(q[d, at : at + TRI, :])
            own = jnp.concatenate(pieces, axis=0)
            to = (y * 3 + c) * NM
            for g in range(NG):
                out[g, to : to + NM, :] = own


def packed(field):
    return field[:, :, 0].transpose(2, 1, 0, 3).reshape(NY * 3 * NM, NZ)


def shards(load_modes, first_guess, kl_fields, region_labels, partner, variable, weight):
    mean = jnp.where(region_labels == 0, 1.3, jnp.where(region_labels == 1, 1.0, 0.6)).astype(F32)
    varying = jnp.where(region_labels[None] == 1, kl_fields, 0.0)
    moduli = jnp.concatenate([varying, mean[None]], 0).reshape((NK + 1) * NY, NZ)
    swapped = ("zh", "y0")
    guess = packed(lax.ppermute(first_guess, swapped, SWAP))
    load = packed(lax.ppermute(load_modes, swapped, SWAP))
    em = lax.ppermute(moduli, SLABS, line(16, 1, True))
    ep = lax.ppermute(moduli, SLABS, line(16, -1, True))
    held = lax.axis_index("zh") == lax.axis_index("y0")
    three = jnp.concatenate([moduli, em, ep], 0)
    three = jnp.where(held, three, lax.ppermute(three, swapped, [(0, 1), (3, 2)]))
    count = moduli.shape[0]
    e0, em, ep = three[:count], three[count : 2 * count], three[2 * count :]
    source = jnp.arange(32, dtype=jnp.int32)[:, None] // 4 % 2
    kept = jnp.broadcast_to((source == lax.axis_index("zh")).astype(F32), (32, NZ))

    offset = (lax.axis_index("y0") * 4 + lax.axis_index("x")) * NM
    own = offset + jnp.arange(NM, dtype=jnp.int32)[:, None]
    pad = ((0, 16 - NM), (0, 0))
    rows_partner = lax.dynamic_slice_in_dim(partner, offset, NM, 0)
    rows_partner = jnp.pad(jnp.concatenate([rows_partner, own], 1), pad, constant_values=-1)
    rows_variable = jnp.pad(lax.dynamic_slice_in_dim(variable, offset, NM, 0), pad)
    rows_weight = lax.dynamic_slice_in_dim(weight, offset, NM, 0)
    rows_weight = jnp.pad(jnp.concatenate([rows_weight, jnp.ones((NM, 1), F32)], 1), pad)
    links = (rows_partner, rows_variable, rows_weight)

    chunk, cells = (QUAD, SLAB, NZ), (QUAD * NY, ROWS, NZ)
    for sweep in range(2):
        first = sweep == 0
        nk = NK + 1 if first else NK
        kernel = fan_kernel if first else merge_kernel
        (copies,) = call(kernel, [(NG, NY * 3 * NM, NZ)])(guess if first else by_slab)
        u = lax.all_to_all(copies, GROUPS, 0, 0, tiled=True)
        fields = (u, load, e0, em, ep) if first else (u, e0, em, ep)
        face_rows = ((NK + 1) * NY, NZ)
        (sent,) = call(
            functools.partial(coupling_kernel, nk),
            [(QUAD, 3 * SLAB + NY, NZ)],
            [
                (NY * 3, NG * NM, NZ),
                (NY * 3, nk * 16, NZ),
                (2,) + face_rows,
                (2,) + face_rows,
                (5,) + face_rows,
            ],
        )(*fields, *links)
        q = lax.all_to_all(sent, WITHIN, 0, 0, tiled=True)
        edge = (4 * SLAB + 16 if first else 4 * SLAB, NZ)
        chunk_r, up, down = call(functools.partial(edges_kernel, first), [chunk, edge, edge])(
            *((q,) if first else (q, rest))
        )
        low = lax.ppermute(up, CHUNKS, line(4, 1))
        high = lax.ppermute(down, CHUNKS, line(4, -1))
        scratch = [(10 * NY, ROWS, NZ)] * 4
        if first:
            v0, v1, v2, v3, mom, ec = call(
                functools.partial(powers_kernel, True),
                [cells] * 4 + [(16, NZ), (10 * NY, NZ)],
                scratch,
            )(q, chunk_r, low, high)
            mom = lax.all_to_all(mom, CHUNKS, 0, 0, tiled=True)
            change, rest = call(functools.partial(update_kernel, True), [chunk, chunk])(
                mom, v0, v1, v2, v3
            )
        else:
            stack, mom = call(
                functools.partial(powers_kernel, False), [(4,) + chunk, (32, NZ)], scratch
            )(q, chunk_r, low, high, ec, change)
            stack = lax.ppermute(stack, swapped, SWAP)
            mom = lax.all_to_all(mom, LINES, 0, 0, tiled=True)
            (change,) = call(functools.partial(update_kernel, False), [chunk])(mom, kept, stack)
        by_slab = lax.all_to_all(change, WITHIN, 0, 0, tiled=True)
    total = by_slab.reshape(QUAD, NY, 3, TRI, NZ).transpose(0, 3, 2, 1, 4)
    return first_guess + total.reshape(NM, 3, 1, NY, NZ)


def solution(mesh):
    split = Mesh(mesh.devices.reshape(2, 4, 2, 2, 4, 2, 2), AXES)
    mode, space = ("zh", "x"), ("y1", "y0", "zp", "zq", "c")
    return jax.shard_map(
        shards,
        mesh=split,
        in_specs=(
            P(mode, None, space, None, None),
            P(mode, None, space, None, None),
            P(None, space, None, None),
            P(space, None, None),
            P(),
            P(),
            P(),
        ),
        out_specs=P(mode, None, space, None, None),
        check_vma=False,
    )
```

```python
import functools

import jax
import jax.numpy as jnp
from jax import lax
from jax.experimental import pallas as pl
from jax.experimental.pallas import tpu as pltpu
from jax.sharding import Mesh
from jax.sharding import PartitionSpec as P

AXES = ("zh", "x", "y1", "y0", "zp", "zq", "c")
SWAP = [(0, 0), (1, 2), (2, 1), (3, 3)]
GROUPS = ("y0", "x")
SLABS = ("zh", "y1", "y0", "zp", "zq", "c")
CHUNKS = ("zh", "y1", "zp")
WITHIN = ("zq", "c")
NG, NM, NL, NK = 8, 12, 8, 8
NY, NZ, SHIFT = 4, 128, 4.0
QUAD = 4
TRI = NM // QUAD
ROWS = 3 * TRI
SLAB = NY * ROWS
F32 = jnp.float32


def line(inner, step, held=False):
    def place(i):
        y1, zh, low = i // (2 * inner), i // inner % 2, i % inner
        first = zh * 2 + y1
        return ((first * 2 + zh) if held else first) * inner + low

    count = 4 * inner
    return [(place(i), place(i + step)) for i in range(count) if 0 <= i + step < count]


def call(kernel, outs, scratch=()):
    vmem = pl.BlockSpec(memory_space=pltpu.VMEM)

    def run(*args):
        return pl.pallas_call(
            kernel,
            out_shape=[pltpu.VMEM(s, F32) for s in outs],
            in_specs=[vmem] * len(args),
            out_specs=[vmem] * len(outs),
            scratch_shapes=[pltpu.VMEM(s, F32) for s in scratch],
        )(*[pltpu.with_memory_space_constraint(a, pltpu.VMEM) for a in args])

    return run


def faces(e, other):
    return 0.5 * (e + other)


def coupling_kernel(nk, *refs):
    first = nk > NK
    if first:
        (u, load, e0, em, ep, partner, variable, weight, out, us, mx, fx, fy, fz) = refs
    else:
        (u, e0, em, ep, partner, variable, weight, out, us, mx, fx, fy, fz) = refs
    for g in range(NG):
        for yc in range(NY * 3):
            us[yc, g * NM : (g + 1) * NM, :] = u[g, yc * NM : (yc + 1) * NM, :]
    lane = lax.broadcasted_iota(jnp.int32, (16, NG * NM), 1)
    pr, vr, wr = partner[...], variable[...], weight[...]
    links = NL + 1 if first else NL
    hit = [jnp.where(lane == pr[:, l : l + 1], wr[:, l : l + 1], 0.0) for l in range(links)]
    blocks = []
    for k in range(nk):
        acc = None
        for l in range(links):
            if (k == NK) != (l == NL):
                continue
            term = hit[l] if l == NL else jnp.where(vr[:, l : l + 1] == k, hit[l], 0.0)
            acc = term if acc is None else acc + term
        blocks.append(acc)
    mix = jnp.concatenate(blocks, axis=0)
    for yc in range(NY * 3):
        mx[yc] = lax.dot_general(
            mix,
            us[yc],
            (((1,), (0,)), ((), ())),
            precision=lax.Precision.HIGHEST,
            preferred_element_type=F32,
        )
    e = e0[...]
    zlane = lax.broadcasted_iota(jnp.int32, e.shape, 1)
    row = lax.broadcasted_iota(jnp.int32, e.shape, 0)
    zup = jnp.where(zlane == NZ - 1, 0.0, pltpu.roll(e, NZ - 1, 1))
    zdn = jnp.where(zlane == 0, 0.0, pltpu.roll(e, 1, 1))
    count = e.shape[0]
    yup = jnp.where(row % NY == NY - 1, 0.0, pltpu.roll(e, count - 1, 0))
    ydn = jnp.where(row % NY == 0, 0.0, pltpu.roll(e, 1, 0))
    fx[0] = faces(e, ep[...])
    fx[1] = faces(e, em[...])
    fy[0] = faces(e, yup)
    fy[1] = faces(e, ydn)
    fzu, fzd = faces(e, zup), faces(e, zdn)
    base = fx[0] + fx[1] + fy[0] + fy[1] + fzu + fzd
    fz[0] = jnp.where(zlane == NZ - 1, 0.0, fzu)
    fz[1] = jnp.where(zlane == 0, 0.0, fzd)
    fz[2] = base + fx[0] + fx[1]
    fz[3] = base + fy[0] + fy[1]
    fz[4] = base + fzu + fzd
    for y in range(NY):
        for c in range(3):
            own = up = down = None
            for k in range(nk):
                r = slice(k * NY + y, k * NY + y + 1)
                rows = slice(k * 16, k * 16 + 16)
                m = mx[y * 3 + c, rows, :]
                t = fz[2 + c, r, :] * m
                side = None
                if y + 1 < NY:
                    side = fy[0, r, :] * mx[(y + 1) * 3 + c, rows, :]
                if y > 0:
                    less = fy[1, r, :] * mx[(y - 1) * 3 + c, rows, :]
                    side = less if side is None else side + less
                t = t - (2.0 * side if c == 1 else side)
                side = fz[0, r, :] * pltpu.roll(m, NZ - 1, 1) + fz[1, r, :] * pltpu.roll(m, 1, 1)
                t = t - (2.0 * side if c == 2 else side)
                p, q = fx[0, r, :] * m, fx[1, r, :] * m
                own, up, down = (t, p, q) if own is None else (own + t, up + p, down + q)
            if c == 0:
                up, down = 2.0 * up, 2.0 * down
            yc = y * 3 + c
            own = load[yc * NM : (yc + 1) * NM, :] - own[:NM] if first else -own[:NM]
            for kind, val in enumerate((own, up, down)):
                at = (kind * NY + y) * ROWS + c * TRI
                for d in range(QUAD):
                    out[d, at : at + TRI, :] = val[d * TRI : (d + 1) * TRI]
    tail = e[NK * NY : NK * NY + NY] if first else jnp.zeros((NY, NZ), F32)
    for d in range(QUAD):
        out[d, 3 * SLAB : 3 * SLAB + NY, :] = tail


def edges_kernel(first, *refs):
    if first:
        q, own, up, down = refs
    else:
        q, rest, own, up, down = refs
    rs = []
    for s in range(QUAD):
        r = q[s, 0:SLAB, :]
        if not first:
            r = r + rest[s]
        if s > 0:
            r = r + q[s - 1, SLAB : 2 * SLAB, :]
        if s + 1 < QUAD:
            r = r + q[s + 1, 2 * SLAB : 3 * SLAB, :]
        own[s] = r
        rs.append(r)
    for j in range(3):
        up[j * SLAB : (j + 1) * SLAB, :] = rs[j + 1]
        down[j * SLAB : (j + 1) * SLAB, :] = rs[j]
    up[3 * SLAB : 4 * SLAB, :] = q[3, SLAB : 2 * SLAB, :]
    down[3 * SLAB : 4 * SLAB, :] = q[0, 2 * SLAB : 3 * SLAB, :]
    if first:
        for j in range(3):
            at = 4 * SLAB + j * NY
            up[at : at + NY, :] = q[j + 1, 3 * SLAB : 3 * SLAB + NY, :]
            down[at : at + NY, :] = q[j, 3 * SLAB : 3 * SLAB + NY, :]
        up[4 * SLAB + 12 :, :] = jnp.zeros((4, NZ), F32)
        down[4 * SLAB + 12 :, :] = jnp.zeros((4, NZ), F32)


def powers_kernel(first, *refs):
    if first:
        q, own, low, high, v0, v1, v2, v3, mom, ec, w0, w1, w2, dg = refs
        for j in range(3):
            at = 4 * SLAB + j * NY
            ec[j * NY : (j + 1) * NY, :] = low[at : at + NY, :]
            ec[(7 + j) * NY : (8 + j) * NY, :] = high[at : at + NY, :]
        for s in range(QUAD):
            ec[(3 + s) * NY : (4 + s) * NY, :] = q[s, 3 * SLAB : 3 * SLAB + NY, :]
    else:
        q, own, low, high, ec, v0, v1, v2, v3, mom, w0, w1, w2, dg = refs

    def rows(ref, at, y):
        return ref[at + y * ROWS : at + (y + 1) * ROWS, :]

    rid = lax.broadcasted_iota(jnp.int32, (ROWS, NZ), 0)
    wx = jnp.where(rid < TRI, 2.0, 1.0)
    wy = jnp.where((rid >= TRI) & (rid < 2 * TRI), 2.0, 1.0)
    wz = jnp.where(rid >= 2 * TRI, 2.0, 1.0)
    lane1 = lax.broadcasted_iota(jnp.int32, (1, NZ), 1)
    em = [[ec[p * NY + y : p * NY + y + 1, :] for y in range(NY)] for p in range(10)]
    zero = jnp.zeros((1, NZ), F32)

    def inside(p, y, val):
        return val if 3 <= p <= 6 else jnp.where(em[p][y] > 0.0, val, 0.0)

    for y in range(NY):
        for p in range(3):
            lo = rows(low, p * SLAB, y)
            hi = rows(high, p * SLAB, y)
            if p == 2:
                lo = lo + rows(q.at[0], 2 * SLAB, y)
            if p == 0:
                hi = hi + rows(q.at[QUAD - 1], SLAB, y)
            w0[p * NY + y] = inside(p, y, lo)
            w0[(7 + p) * NY + y] = inside(7 + p, y, hi)
        for s in range(QUAD):
            r = rows(own.at[s], 0, y)
            if s == 0:
                r = r + rows(low, 3 * SLAB, y)
            if s == QUAD - 1:
                r = r + rows(high, 3 * SLAB, y)
            w0[(3 + s) * NY + y] = r
            v0[s * NY + y] = r

    def face(p, y):
        e = em[p][y]
        xu, xd = faces(e, em[p + 1][y]), faces(e, em[p - 1][y])
        yu = faces(e, em[p][y + 1] if y + 1 < NY else zero)
        yd = faces(e, em[p][y - 1] if y > 0 else zero)
        zu = faces(e, jnp.where(lane1 == NZ - 1, 0.0, pltpu.roll(e, NZ - 1, 1)))
        zd = faces(e, jnp.where(lane1 == 0, 0.0, pltpu.roll(e, 1, 1)))
        return xu, xd, yu, yd, zu, zd

    coef = {}
    for p in range(1, 9):
        for y in range(NY):
            xu, xd, yu, yd, zu, zd = face(p, y)
            dg[p * NY + y] = wx * (xu + xd) + wy * (yu + yd) + wz * (zu + zd) - SHIFT
            coef[p, y] = (
                xu, xd, yu, yd,
                jnp.where(lane1 == NZ - 1, 0.0, zu),
                jnp.where(lane1 == 0, 0.0, zd),
            )

    def apply(src, p, y):
        xu, xd, yu, yd, zu, zd = coef[p, y]
        m = src[p * NY + y]
        t = dg[p * NY + y] * m
        t = t - wx * (xu * src[(p + 1) * NY + y] + xd * src[(p - 1) * NY + y])
        side = None
        if y + 1 < NY:
            side = yu * src[p * NY + y + 1]
        if y > 0:
            less = yd * src[p * NY + y - 1]
            side = less if side is None else side + less
        t = t - wy * side
        t = t - wz * (zu * pltpu.roll(m, NZ - 1, 1) + zd * pltpu.roll(m, 1, 1))
        return inside(p, y, t)

    for p in range(1, 9):
        for y in range(NY):
            t = apply(w0, p, y)
            w1[p * NY + y] = t
            if 3 <= p <= 6:
                v1[(p - 3) * NY + y] = t
    for p in range(2, 8):
        for y in range(NY):
            t = apply(w1, p, y)
            w2[p * NY + y] = t
            if 3 <= p <= 6:
                v2[(p - 3) * NY + y] = t
    sums = [None] * 6
    for p in range(3, 7):
        for y in range(NY):
            a, b, d = w0[p * NY + y], w1[p * NY + y], w2[p * NY + y]
            t = apply(w2, p, y)
            v3[(p - 3) * NY + y] = t
            for j, val in enumerate((a * a, a * b, b * b, b * d, d * d, d * t)):
                sums[j] = val if sums[j] is None else sums[j] + val
    lane = lax.broadcasted_iota(jnp.int32, (ROWS, NZ), 1)
    spot = lane - 8 * (rid % TRI)
    packed = jnp.zeros((ROWS, NZ), F32)
    for j in range(6):
        packed = jnp.where(spot == j, jnp.sum(sums[j], axis=1, keepdims=True), packed)
    mom[...] = jnp.broadcast_to(jnp.sum(packed, axis=0, keepdims=True), mom.shape)


def step_coefficients(mom):
    def inner(a, b):
        total = None
        for i, s in enumerate(a):
            for j, t in enumerate(b):
                term = s * t * mom[i + j]
                total = term if total is None else total + term
        return total

    def image(a):
        q = [SHIFT * s for s in a] + [None]
        for i, s in enumerate(a):
            q[i + 1] = s if q[i + 1] is None else q[i + 1] + s
        return q

    one = jnp.ones_like(mom[0])
    x, r, p = [], [one], [one]
    rr = mom[0]
    for step in range(3):
        q = image(p)
        alpha = rr / inner(p, q)
        x = [x[i] + alpha * s if i < len(x) else alpha * s for i, s in enumerate(p)]
        r = [r[i] - alpha * s if i < len(r) else -alpha * s for i, s in enumerate(q)]
        if step < 2:
            new = inner(r, r)
            beta = new / rr
            p = [s + beta * p[i] if i < len(p) else s for i, s in enumerate(r)]
            rr = new
    return x, r


def update_kernel(first, *refs):
    if first:
        mom, v0, v1, v2, v3, out, rest = refs
    else:
        mom, v0, v1, v2, before, out = refs
    total = jnp.sum(mom[...], axis=0, keepdims=True)
    rid = lax.broadcasted_iota(jnp.int32, (ROWS, NZ), 0)
    lane = lax.broadcasted_iota(jnp.int32, (ROWS, NZ), 1)
    spot = lane - 8 * (rid % TRI)
    picked = [jnp.sum(jnp.where(spot == j, total, 0.0), axis=1, keepdims=True) for j in range(6)]
    x, r = step_coefficients(picked)
    x = [jnp.broadcast_to(s, (ROWS, NZ)) for s in x]
    r = [jnp.broadcast_to(s, (ROWS, NZ)) for s in r]
    for s in range(QUAD):
        for y in range(NY):
            at = s * NY + y
            rows = slice(y * ROWS, (y + 1) * ROWS)
            a, b, d = v0[at], v1[at], v2[at]
            change = x[0] * a + x[1] * b + x[2] * d
            if first:
                rest[s, rows, :] = r[0] * a + r[1] * b + r[2] * d + r[3] * v3[at]
            else:
                change = change + before[s, rows, :]
            out[s, rows, :] = change


def fan_kernel(field, out):
    own = field[: NY * 3 * NM, :]
    for g in range(NG):
        out[g] = own


def merge_kernel(q, out):
    for y in range(NY):
        for c in range(3):
            pieces = []
            for d in range(QUAD):
                at = y * ROWS + c * TRI
                pieces.append(q[d, at : at + TRI, :])
            own = jnp.concatenate(pieces, axis=0)
            to = (y * 3 + c) * NM
            for g in range(NG):
                out[g, to : to + NM, :] = own


def packed(field):
    return field[:, :, 0].transpose(2, 1, 0, 3).reshape(NY * 3 * NM, NZ)


def shards(load_modes, first_guess, kl_fields, region_labels, partner, variable, weight):
    mean = jnp.where(region_labels == 0, 1.3, jnp.where(region_labels == 1, 1.0, 0.6)).astype(F32)
    varying = jnp.where(region_labels[None] == 1, kl_fields, 0.0)
    moduli = jnp.concatenate([varying, mean[None]], 0).reshape((NK + 1) * NY, NZ)
    swapped = ("zh", "y0")
    guess = packed(lax.ppermute(first_guess, swapped, SWAP))
    load = packed(lax.ppermute(load_modes, swapped, SWAP))
    em = lax.ppermute(moduli, SLABS, line(16, 1, True))
    ep = lax.ppermute(moduli, SLABS, line(16, -1, True))
    held = lax.axis_index("zh") == lax.axis_index("y0")
    three = jnp.concatenate([moduli, em, ep], 0)
    three = jnp.where(held, three, lax.ppermute(three, swapped, [(0, 1), (3, 2)]))
    count = moduli.shape[0]
    e0, em, ep = three[:count], three[count : 2 * count], three[2 * count :]

    offset = (lax.axis_index("y0") * 4 + lax.axis_index("x")) * NM
    own = offset + jnp.arange(NM, dtype=jnp.int32)[:, None]
    pad = ((0, 16 - NM), (0, 0))
    rows_partner = lax.dynamic_slice_in_dim(partner, offset, NM, 0)
    rows_partner = jnp.pad(jnp.concatenate([rows_partner, own], 1), pad, constant_values=-1)
    rows_variable = jnp.pad(lax.dynamic_slice_in_dim(variable, offset, NM, 0), pad)
    rows_weight = lax.dynamic_slice_in_dim(weight, offset, NM, 0)
    rows_weight = jnp.pad(jnp.concatenate([rows_weight, jnp.ones((NM, 1), F32)], 1), pad)
    links = (rows_partner, rows_variable, rows_weight)

    chunk, cells = (QUAD, SLAB, NZ), (QUAD * NY, ROWS, NZ)
    for sweep in range(2):
        first = sweep == 0
        nk = NK + 1 if first else NK
        kernel = fan_kernel if first else merge_kernel
        (copies,) = call(kernel, [(NG, NY * 3 * NM, NZ)])(guess if first else by_slab)
        u = lax.all_to_all(copies, GROUPS, 0, 0, tiled=True)
        fields = (u, load, e0, em, ep) if first else (u, e0, em, ep)
        face_rows = ((NK + 1) * NY, NZ)
        (sent,) = call(
            functools.partial(coupling_kernel, nk),
            [(QUAD, 3 * SLAB + NY, NZ)],
            [
                (NY * 3, NG * NM, NZ),
                (NY * 3, nk * 16, NZ),
                (2,) + face_rows,
                (2,) + face_rows,
                (5,) + face_rows,
            ],
        )(*fields, *links)
        q = lax.all_to_all(sent, WITHIN, 0, 0, tiled=True)
        edge = (4 * SLAB + 16 if first else 4 * SLAB, NZ)
        chunk_r, up, down = call(functools.partial(edges_kernel, first), [chunk, edge, edge])(
            *((q,) if first else (q, rest))
        )
        low = lax.ppermute(up, CHUNKS, line(4, 1))
        high = lax.ppermute(down, CHUNKS, line(4, -1))
        scratch = [(10 * NY, ROWS, NZ)] * 4
        outs = [cells] * 4 + [(16, NZ)]
        if first:
            v0, v1, v2, v3, mom, ec = call(
                functools.partial(powers_kernel, True), outs + [(10 * NY, NZ)], scratch
            )(q, chunk_r, low, high)
        else:
            v0, v1, v2, v3, mom = call(functools.partial(powers_kernel, False), outs, scratch)(
                q, chunk_r, low, high, ec
            )
        mom = lax.all_to_all(mom, CHUNKS, 0, 0, tiled=True)
        if first:
            change, rest = call(functools.partial(update_kernel, True), [chunk, chunk])(
                mom, v0, v1, v2, v3
            )
        else:
            (change,) = call(functools.partial(update_kernel, False), [chunk])(
                mom, v0, v1, v2, change
            )
        by_slab = lax.all_to_all(change, WITHIN, 0, 0, tiled=True)
    total = lax.ppermute(by_slab, swapped, SWAP)
    total = total.reshape(QUAD, NY, 3, TRI, NZ).transpose(0, 3, 2, 1, 4)
    return first_guess + total.reshape(NM, 3, 1, NY, NZ)


def solution(mesh):
    split = Mesh(mesh.devices.reshape(2, 4, 2, 2, 4, 2, 2), AXES)
    mode, space = ("zh", "x"), ("y1", "y0", "zp", "zq", "c")
    return jax.shard_map(
        shards,
        mesh=split,
        in_specs=(
            P(mode, None, space, None, None),
            P(mode, None, space, None, None),
            P(None, space, None, None),
            P(space, None, None),
            P(),
            P(),
            P(),
        ),
        out_specs=P(mode, None, space, None, None),
        check_vma=False,
    )
```

```python
import functools

import jax
import jax.numpy as jnp
from jax import lax
from jax.experimental import pallas as pl
from jax.experimental.pallas import tpu as pltpu
from jax.sharding import Mesh
from jax.sharding import PartitionSpec as P

AXES = ("zh", "x", "y1", "y0", "zp", "zq", "c")
SWAP = [(0, 0), (1, 2), (2, 1), (3, 3)]
GROUPS = ("y0", "x")
SLABS = ("zh", "y1", "y0", "zp", "zq", "c")
CHUNKS = ("zh", "y1", "zp")
WITHIN = ("zq", "c")
NG, NM, NL, NK = 8, 12, 8, 8
NY, NZ, SHIFT = 4, 128, 4.0
QUAD = 4
TRI = NM // QUAD
ROWS = 3 * TRI
SLAB = NY * ROWS
F32 = jnp.float32


def line(inner, step, held=False):
    def place(i):
        y1, zh, low = i // (2 * inner), i // inner % 2, i % inner
        first = zh * 2 + y1
        return ((first * 2 + zh) if held else first) * inner + low

    count = 4 * inner
    return [(place(i), place(i + step)) for i in range(count) if 0 <= i + step < count]


def call(kernel, outs, scratch=()):
    vmem = pl.BlockSpec(memory_space=pltpu.VMEM)

    def run(*args):
        return pl.pallas_call(
            kernel,
            out_shape=[pltpu.VMEM(s, F32) for s in outs],
            in_specs=[vmem] * len(args),
            out_specs=[vmem] * len(outs),
            scratch_shapes=[pltpu.VMEM(s, F32) for s in scratch],
        )(*[pltpu.with_memory_space_constraint(a, pltpu.VMEM) for a in args])

    return run


def faces(e, other):
    return 0.5 * (e + other)


def coupling_kernel(nk, *refs):
    first = nk > NK
    if first:
        (u, load, e0, em, ep, partner, variable, weight, out, us, mx, fx, fy, fz) = refs
    else:
        (u, e0, em, ep, partner, variable, weight, out, us, mx, fx, fy, fz) = refs
    for g in range(NG):
        for yc in range(NY * 3):
            us[yc, g * NM : (g + 1) * NM, :] = u[g, yc * NM : (yc + 1) * NM, :]
    lane = lax.broadcasted_iota(jnp.int32, (16, NG * NM), 1)
    pr, vr, wr = partner[...], variable[...], weight[...]
    links = NL + 1 if first else NL
    hit = [jnp.where(lane == pr[:, l : l + 1], wr[:, l : l + 1], 0.0) for l in range(links)]
    blocks = []
    for k in range(nk):
        acc = None
        for l in range(links):
            if (k == NK) != (l == NL):
                continue
            term = hit[l] if l == NL else jnp.where(vr[:, l : l + 1] == k, hit[l], 0.0)
            acc = term if acc is None else acc + term
        blocks.append(acc)
    mix = jnp.concatenate(blocks, axis=0)
    for yc in range(NY * 3):
        mx[yc] = lax.dot_general(
            mix,
            us[yc],
            (((1,), (0,)), ((), ())),
            precision=lax.Precision.HIGHEST,
            preferred_element_type=F32,
        )
    e = e0[...]
    zlane = lax.broadcasted_iota(jnp.int32, e.shape, 1)
    row = lax.broadcasted_iota(jnp.int32, e.shape, 0)
    zup = jnp.where(zlane == NZ - 1, 0.0, pltpu.roll(e, NZ - 1, 1))
    zdn = jnp.where(zlane == 0, 0.0, pltpu.roll(e, 1, 1))
    count = e.shape[0]
    yup = jnp.where(row % NY == NY - 1, 0.0, pltpu.roll(e, count - 1, 0))
    ydn = jnp.where(row % NY == 0, 0.0, pltpu.roll(e, 1, 0))
    fx[0] = faces(e, ep[...])
    fx[1] = faces(e, em[...])
    fy[0] = faces(e, yup)
    fy[1] = faces(e, ydn)
    fzu, fzd = faces(e, zup), faces(e, zdn)
    base = fx[0] + fx[1] + fy[0] + fy[1] + fzu + fzd
    fz[0] = jnp.where(zlane == NZ - 1, 0.0, fzu)
    fz[1] = jnp.where(zlane == 0, 0.0, fzd)
    fz[2] = base + fx[0] + fx[1]
    fz[3] = base + fy[0] + fy[1]
    fz[4] = base + fzu + fzd
    for y in range(NY):
        for c in range(3):
            own = up = down = None
            for k in range(nk):
                r = slice(k * NY + y, k * NY + y + 1)
                rows = slice(k * 16, k * 16 + 16)
                m = mx[y * 3 + c, rows, :]
                t = fz[2 + c, r, :] * m
                side = None
                if y + 1 < NY:
                    side = fy[0, r, :] * mx[(y + 1) * 3 + c, rows, :]
                if y > 0:
                    less = fy[1, r, :] * mx[(y - 1) * 3 + c, rows, :]
                    side = less if side is None else side + less
                t = t - (2.0 * side if c == 1 else side)
                side = fz[0, r, :] * pltpu.roll(m, NZ - 1, 1) + fz[1, r, :] * pltpu.roll(m, 1, 1)
                t = t - (2.0 * side if c == 2 else side)
                p, q = fx[0, r, :] * m, fx[1, r, :] * m
                own, up, down = (t, p, q) if own is None else (own + t, up + p, down + q)
            if c == 0:
                up, down = 2.0 * up, 2.0 * down
            yc = y * 3 + c
            own = load[yc * NM : (yc + 1) * NM, :] - own[:NM] if first else -own[:NM]
            for kind, val in enumerate((own, up, down)):
                at = (kind * NY + y) * ROWS + c * TRI
                for d in range(QUAD):
                    out[d, at : at + TRI, :] = val[d * TRI : (d + 1) * TRI]
    tail = e[NK * NY : NK * NY + NY] if first else jnp.zeros((NY, NZ), F32)
    for d in range(QUAD):
        out[d, 3 * SLAB : 3 * SLAB + NY, :] = tail


def edges_kernel(first, *refs):
    if first:
        q, own, up, down = refs
    else:
        q, rest, own, up, down = refs
    rs = []
    for s in range(QUAD):
        r = q[s, 0:SLAB, :]
        if not first:
            r = r + rest[s]
        if s > 0:
            r = r + q[s - 1, SLAB : 2 * SLAB, :]
        if s + 1 < QUAD:
            r = r + q[s + 1, 2 * SLAB : 3 * SLAB, :]
        own[s] = r
        rs.append(r)
    for j in range(3):
        up[j * SLAB : (j + 1) * SLAB, :] = rs[j + 1]
        down[j * SLAB : (j + 1) * SLAB, :] = rs[j]
    up[3 * SLAB : 4 * SLAB, :] = q[3, SLAB : 2 * SLAB, :]
    down[3 * SLAB : 4 * SLAB, :] = q[0, 2 * SLAB : 3 * SLAB, :]
    if first:
        for j in range(3):
            at = 4 * SLAB + j * NY
            up[at : at + NY, :] = q[j + 1, 3 * SLAB : 3 * SLAB + NY, :]
            down[at : at + NY, :] = q[j, 3 * SLAB : 3 * SLAB + NY, :]
        up[4 * SLAB + 12 :, :] = jnp.zeros((4, NZ), F32)
        down[4 * SLAB + 12 :, :] = jnp.zeros((4, NZ), F32)


def powers_kernel(first, *refs):
    if first:
        q, own, low, high, v0, v1, v2, v3, mom, ec, w0, w1, w2, dg = refs
        for j in range(3):
            at = 4 * SLAB + j * NY
            ec[j * NY : (j + 1) * NY, :] = low[at : at + NY, :]
            ec[(7 + j) * NY : (8 + j) * NY, :] = high[at : at + NY, :]
        for s in range(QUAD):
            ec[(3 + s) * NY : (4 + s) * NY, :] = q[s, 3 * SLAB : 3 * SLAB + NY, :]
    else:
        q, own, low, high, ec, v0, v1, v2, v3, mom, w0, w1, w2, dg = refs

    def rows(ref, at, y):
        return ref[at + y * ROWS : at + (y + 1) * ROWS, :]

    rid = lax.broadcasted_iota(jnp.int32, (ROWS, NZ), 0)
    wx = jnp.where(rid < TRI, 2.0, 1.0)
    wy = jnp.where((rid >= TRI) & (rid < 2 * TRI), 2.0, 1.0)
    wz = jnp.where(rid >= 2 * TRI, 2.0, 1.0)
    lane1 = lax.broadcasted_iota(jnp.int32, (1, NZ), 1)
    em = [[ec[p * NY + y : p * NY + y + 1, :] for y in range(NY)] for p in range(10)]
    zero = jnp.zeros((1, NZ), F32)

    def inside(p, y, val):
        return val if 3 <= p <= 6 else jnp.where(em[p][y] > 0.0, val, 0.0)

    for y in range(NY):
        for p in range(3):
            lo = rows(low, p * SLAB, y)
            hi = rows(high, p * SLAB, y)
            if p == 2:
                lo = lo + rows(q.at[0], 2 * SLAB, y)
            if p == 0:
                hi = hi + rows(q.at[QUAD - 1], SLAB, y)
            w0[p * NY + y] = inside(p, y, lo)
            w0[(7 + p) * NY + y] = inside(7 + p, y, hi)
        for s in range(QUAD):
            r = rows(own.at[s], 0, y)
            if s == 0:
                r = r + rows(low, 3 * SLAB, y)
            if s == QUAD - 1:
                r = r + rows(high, 3 * SLAB, y)
            w0[(3 + s) * NY + y] = r
            v0[s * NY + y] = r

    def face(p, y):
        e = em[p][y]
        xu, xd = faces(e, em[p + 1][y]), faces(e, em[p - 1][y])
        yu = faces(e, em[p][y + 1] if y + 1 < NY else zero)
        yd = faces(e, em[p][y - 1] if y > 0 else zero)
        zu = faces(e, jnp.where(lane1 == NZ - 1, 0.0, pltpu.roll(e, NZ - 1, 1)))
        zd = faces(e, jnp.where(lane1 == 0, 0.0, pltpu.roll(e, 1, 1)))
        return xu, xd, yu, yd, zu, zd

    coef = {}
    for p in range(1, 9):
        for y in range(NY):
            xu, xd, yu, yd, zu, zd = face(p, y)
            dg[p * NY + y] = wx * (xu + xd) + wy * (yu + yd) + wz * (zu + zd) - SHIFT
            coef[p, y] = (
                xu, xd, yu, yd,
                jnp.where(lane1 == NZ - 1, 0.0, zu),
                jnp.where(lane1 == 0, 0.0, zd),
            )

    def apply(src, p, y):
        xu, xd, yu, yd, zu, zd = coef[p, y]
        m = src[p * NY + y]
        t = dg[p * NY + y] * m
        t = t - wx * (xu * src[(p + 1) * NY + y] + xd * src[(p - 1) * NY + y])
        side = None
        if y + 1 < NY:
            side = yu * src[p * NY + y + 1]
        if y > 0:
            less = yd * src[p * NY + y - 1]
            side = less if side is None else side + less
        t = t - wy * side
        t = t - wz * (zu * pltpu.roll(m, NZ - 1, 1) + zd * pltpu.roll(m, 1, 1))
        return inside(p, y, t)

    for p in range(1, 9):
        for y in range(NY):
            t = apply(w0, p, y)
            w1[p * NY + y] = t
            if 3 <= p <= 6:
                v1[(p - 3) * NY + y] = t
    for p in range(2, 8):
        for y in range(NY):
            t = apply(w1, p, y)
            w2[p * NY + y] = t
            if 3 <= p <= 6:
                v2[(p - 3) * NY + y] = t
    sums = [None] * 6
    for p in range(3, 7):
        for y in range(NY):
            a, b, d = w0[p * NY + y], w1[p * NY + y], w2[p * NY + y]
            t = apply(w2, p, y)
            v3[(p - 3) * NY + y] = t
            for j, val in enumerate((a * a, a * b, b * b, b * d, d * d, d * t)):
                sums[j] = val if sums[j] is None else sums[j] + val
    lane = lax.broadcasted_iota(jnp.int32, (ROWS, NZ), 1)
    spot = lane - 8 * (rid % TRI)
    packed = jnp.zeros((ROWS, NZ), F32)
    for j in range(6):
        packed = jnp.where(spot == j, jnp.sum(sums[j], axis=1, keepdims=True), packed)
    mom[...] = jnp.broadcast_to(jnp.sum(packed, axis=0, keepdims=True), mom.shape)


def step_coefficients(mom):
    def inner(a, b):
        total = None
        for i, s in enumerate(a):
            for j, t in enumerate(b):
                term = s * t * mom[i + j]
                total = term if total is None else total + term
        return total

    def image(a):
        q = [SHIFT * s for s in a] + [None]
        for i, s in enumerate(a):
            q[i + 1] = s if q[i + 1] is None else q[i + 1] + s
        return q

    one = jnp.ones_like(mom[0])
    x, r, p = [], [one], [one]
    rr = mom[0]
    for step in range(3):
        q = image(p)
        alpha = rr / inner(p, q)
        x = [x[i] + alpha * s if i < len(x) else alpha * s for i, s in enumerate(p)]
        r = [r[i] - alpha * s if i < len(r) else -alpha * s for i, s in enumerate(q)]
        if step < 2:
            new = inner(r, r)
            beta = new / rr
            p = [s + beta * p[i] if i < len(p) else s for i, s in enumerate(r)]
            rr = new
    return x, r


def update_kernel(first, *refs):
    if first:
        mom, v0, v1, v2, v3, out, rest = refs
    else:
        mom, v0, v1, v2, before, out = refs
    total = jnp.sum(mom[...], axis=0, keepdims=True)
    rid = lax.broadcasted_iota(jnp.int32, (ROWS, NZ), 0)
    lane = lax.broadcasted_iota(jnp.int32, (ROWS, NZ), 1)
    spot = lane - 8 * (rid % TRI)
    picked = [jnp.sum(jnp.where(spot == j, total, 0.0), axis=1, keepdims=True) for j in range(6)]
    x, r = step_coefficients(picked)
    x = [jnp.broadcast_to(s, (ROWS, NZ)) for s in x]
    r = [jnp.broadcast_to(s, (ROWS, NZ)) for s in r]
    for s in range(QUAD):
        for y in range(NY):
            at = s * NY + y
            rows = slice(y * ROWS, (y + 1) * ROWS)
            a, b, d = v0[at], v1[at], v2[at]
            change = x[0] * a + x[1] * b + x[2] * d
            if first:
                rest[s, rows, :] = r[0] * a + r[1] * b + r[2] * d + r[3] * v3[at]
            else:
                change = change + before[s, rows, :]
            out[s, rows, :] = change


def fan_kernel(field, out):
    own = field[: NY * 3 * NM, :]
    for g in range(NG):
        out[g] = own


def merge_kernel(q, out):
    for y in range(NY):
        for c in range(3):
            pieces = []
            for d in range(QUAD):
                at = y * ROWS + c * TRI
                pieces.append(q[d, at : at + TRI, :])
            own = jnp.concatenate(pieces, axis=0)
            to = (y * 3 + c) * NM
            for g in range(NG):
                out[g, to : to + NM, :] = own


def packed(field):
    return field[:, :, 0].transpose(2, 1, 0, 3).reshape(NY * 3 * NM, NZ)


def shards(load_modes, first_guess, kl_fields, region_labels, partner, variable, weight):
    mean = jnp.where(region_labels == 0, 1.3, jnp.where(region_labels == 1, 1.0, 0.6)).astype(F32)
    varying = jnp.where(region_labels[None] == 1, kl_fields, 0.0)
    moduli = jnp.concatenate([varying, mean[None]], 0).reshape((NK + 1) * NY, NZ)
    swapped = ("zh", "y0")
    guess = packed(lax.ppermute(first_guess, swapped, SWAP))
    em = lax.ppermute(moduli, SLABS, line(16, 1, True))
    ep = lax.ppermute(moduli, SLABS, line(16, -1, True))
    em, ep, later = lax.optimization_barrier((em, ep, load_modes))
    load = packed(lax.ppermute(later, swapped, SWAP))
    held = lax.axis_index("zh") == lax.axis_index("y0")
    three = jnp.concatenate([moduli, em, ep], 0)
    three = jnp.where(held, three, lax.ppermute(three, swapped, [(0, 1), (3, 2)]))
    count = moduli.shape[0]
    e0, em, ep = three[:count], three[count : 2 * count], three[2 * count :]

    offset = (lax.axis_index("y0") * 4 + lax.axis_index("x")) * NM
    own = offset + jnp.arange(NM, dtype=jnp.int32)[:, None]
    pad = ((0, 16 - NM), (0, 0))
    rows_partner = lax.dynamic_slice_in_dim(partner, offset, NM, 0)
    rows_partner = jnp.pad(jnp.concatenate([rows_partner, own], 1), pad, constant_values=-1)
    rows_variable = jnp.pad(lax.dynamic_slice_in_dim(variable, offset, NM, 0), pad)
    rows_weight = lax.dynamic_slice_in_dim(weight, offset, NM, 0)
    rows_weight = jnp.pad(jnp.concatenate([rows_weight, jnp.ones((NM, 1), F32)], 1), pad)
    links = (rows_partner, rows_variable, rows_weight)

    chunk, cells = (QUAD, SLAB, NZ), (QUAD * NY, ROWS, NZ)
    for sweep in range(2):
        first = sweep == 0
        nk = NK + 1 if first else NK
        kernel = fan_kernel if first else merge_kernel
        (copies,) = call(kernel, [(NG, NY * 3 * NM, NZ)])(guess if first else by_slab)
        u = lax.all_to_all(copies, GROUPS, 0, 0, tiled=True)
        fields = (u, load, e0, em, ep) if first else (u, e0, em, ep)
        face_rows = ((NK + 1) * NY, NZ)
        (sent,) = call(
            functools.partial(coupling_kernel, nk),
            [(QUAD, 3 * SLAB + NY, NZ)],
            [
                (NY * 3, NG * NM, NZ),
                (NY * 3, nk * 16, NZ),
                (2,) + face_rows,
                (2,) + face_rows,
                (5,) + face_rows,
            ],
        )(*fields, *links)
        q = lax.all_to_all(sent, WITHIN, 0, 0, tiled=True)
        edge = (4 * SLAB + 16 if first else 4 * SLAB, NZ)
        chunk_r, up, down = call(functools.partial(edges_kernel, first), [chunk, edge, edge])(
            *((q,) if first else (q, rest))
        )
        low = lax.ppermute(up, CHUNKS, line(4, 1))
        high = lax.ppermute(down, CHUNKS, line(4, -1))
        scratch = [(10 * NY, ROWS, NZ)] * 4
        outs = [cells] * 4 + [(16, NZ)]
        if first:
            v0, v1, v2, v3, mom, ec = call(
                functools.partial(powers_kernel, True), outs + [(10 * NY, NZ)], scratch
            )(q, chunk_r, low, high)
        else:
            v0, v1, v2, v3, mom = call(functools.partial(powers_kernel, False), outs, scratch)(
                q, chunk_r, low, high, ec
            )
        mom = lax.all_to_all(mom, CHUNKS, 0, 0, tiled=True)
        if first:
            change, rest = call(functools.partial(update_kernel, True), [chunk, chunk])(
                mom, v0, v1, v2, v3
            )
        else:
            (change,) = call(functools.partial(update_kernel, False), [chunk])(
                mom, v0, v1, v2, change
            )
        by_slab = lax.all_to_all(change, WITHIN, 0, 0, tiled=True)
    total = lax.ppermute(by_slab, swapped, SWAP)
    total = total.reshape(QUAD, NY, 3, TRI, NZ).transpose(0, 3, 2, 1, 4)
    return first_guess + total.reshape(NM, 3, 1, NY, NZ)


def solution(mesh):
    split = Mesh(mesh.devices.reshape(2, 4, 2, 2, 4, 2, 2), AXES)
    mode, space = ("zh", "x"), ("y1", "y0", "zp", "zq", "c")
    return jax.shard_map(
        shards,
        mesh=split,
        in_specs=(
            P(mode, None, space, None, None),
            P(mode, None, space, None, None),
            P(None, space, None, None),
            P(space, None, None),
            P(),
            P(),
            P(),
        ),
        out_specs=P(mode, None, space, None, None),
        check_vma=False,
    )
```

```python
import functools

import jax
import jax.numpy as jnp
from jax import lax
from jax.experimental import pallas as pl
from jax.experimental.pallas import tpu as pltpu
from jax.sharding import Mesh
from jax.sharding import PartitionSpec as P

AXES = ("zh", "x", "y", "zp", "zq", "c")
SLABS = ("zh", "y", "zp", "zq", "c")
CHAIN = ("zh", "y", "zp")
CHUNKS = ("y", "zp")
WITHIN = ("zq", "c")
NX, NM, NT, NL, NK = 4, 12, 24, 8, 8
MODES = 2 * NX * NM
NY, NZ, SHIFT = 4, 128, 4.0
QUAD = 4
TRI = NM // QUAD
SIX = 2 * TRI
ROWS = 3 * SIX
SLAB = NY * ROWS
SENT = 3 * SLAB + 8
F32 = jnp.float32


def line(inner, step):
    count = 4 * inner
    pairs = []
    for zh in range(2):
        for i in range(count):
            j = i + step
            if 0 <= j < count:
                other = zh ^ (i // inner != j // inner)
                pairs.append((zh * count + i, other * count + j))
    return pairs


def call(kernel, outs, scratch=()):
    vmem = pl.BlockSpec(memory_space=pltpu.VMEM)

    def run(*args):
        return pl.pallas_call(
            kernel,
            out_shape=[pltpu.VMEM(s, F32) for s in outs],
            in_specs=[vmem] * len(args),
            out_specs=[vmem] * len(outs),
            scratch_shapes=[pltpu.VMEM(s, F32) for s in scratch],
        )(*[pltpu.with_memory_space_constraint(a, pltpu.VMEM) for a in args])

    return run


def faces(e, other):
    return 0.5 * (e + other)


def coupling_kernel(nk, *refs):
    first = nk > NK
    if first:
        (u, load, e0, em, ep, partner, variable, weight, out, us, mx, fx, fy, fz) = refs
    else:
        (u, e0, em, ep, partner, variable, weight, out, us, mx, fx, fy, fz) = refs
    for g in range(2 * NX):
        half, x = divmod(g, NX)
        for y in range(NY):
            for c in range(3):
                yc = y * 3 + c
                if first:
                    at = (half * NY * 3 + yc) * NM
                    us[yc, g * NM : (g + 1) * NM, :] = u[x, at : at + NM, :]
                    continue
                for d in range(QUAD):
                    at, to = y * ROWS + c * SIX + half * TRI, g * NM + d * TRI
                    us[yc, to : to + TRI, :] = u[x * QUAD + d, at : at + TRI, :]
    lane = lax.broadcasted_iota(jnp.int32, (NT, MODES), 1)
    pr, vr, wr = partner[...], variable[...], weight[...]
    links = NL + 1 if first else NL
    hit = [jnp.where(lane == pr[:, l : l + 1], wr[:, l : l + 1], 0.0) for l in range(links)]
    blocks = []
    for k in range(nk):
        acc = None
        for l in range(links):
            if (k == NK) != (l == NL):
                continue
            term = hit[l] if l == NL else jnp.where(vr[:, l : l + 1] == k, hit[l], 0.0)
            acc = term if acc is None else acc + term
        blocks.append(acc)
    mix = jnp.concatenate(blocks, axis=0)
    for yc in range(NY * 3):
        mx[yc] = lax.dot_general(
            mix,
            us[yc],
            (((1,), (0,)), ((), ())),
            precision=lax.Precision.HIGHEST,
            preferred_element_type=F32,
        )
    e = e0[...]
    zlane = lax.broadcasted_iota(jnp.int32, e.shape, 1)
    row = lax.broadcasted_iota(jnp.int32, e.shape, 0)
    zup = jnp.where(zlane == NZ - 1, 0.0, pltpu.roll(e, NZ - 1, 1))
    zdn = jnp.where(zlane == 0, 0.0, pltpu.roll(e, 1, 1))
    count = e.shape[0]
    yup = jnp.where(row % NY == NY - 1, 0.0, pltpu.roll(e, count - 1, 0))
    ydn = jnp.where(row % NY == 0, 0.0, pltpu.roll(e, 1, 0))
    fx[0] = faces(e, ep[...])
    fx[1] = faces(e, em[...])
    fy[0] = faces(e, yup)
    fy[1] = faces(e, ydn)
    fzu, fzd = faces(e, zup), faces(e, zdn)
    base = fx[0] + fx[1] + fy[0] + fy[1] + fzu + fzd
    fz[0] = jnp.where(zlane == NZ - 1, 0.0, fzu)
    fz[1] = jnp.where(zlane == 0, 0.0, fzd)
    fz[2] = base + fx[0] + fx[1]
    fz[3] = base + fy[0] + fy[1]
    fz[4] = base + fzu + fzd
    for y in range(NY):
        for c in range(3):
            own = up = down = None
            for k in range(nk):
                r = slice(k * NY + y, k * NY + y + 1)
                rows = slice(k * NT, (k + 1) * NT)
                m = mx[y * 3 + c, rows, :]
                t = fz[2 + c, r, :] * m
                side = None
                if y + 1 < NY:
                    side = fy[0, r, :] * mx[(y + 1) * 3 + c, rows, :]
                if y > 0:
                    less = fy[1, r, :] * mx[(y - 1) * 3 + c, rows, :]
                    side = less if side is None else side + less
                t = t - (2.0 * side if c == 1 else side)
                side = fz[0, r, :] * pltpu.roll(m, NZ - 1, 1) + fz[1, r, :] * pltpu.roll(m, 1, 1)
                t = t - (2.0 * side if c == 2 else side)
                p, q = fx[0, r, :] * m, fx[1, r, :] * m
                own, up, down = (t, p, q) if own is None else (own + t, up + p, down + q)
            if c == 0:
                up, down = 2.0 * up, 2.0 * down
            yc = y * 3 + c
            own = load[yc * NT : (yc + 1) * NT, :] - own if first else -own
            for kind, val in enumerate((own, up, down)):
                at = (kind * NY + y) * ROWS + c * SIX
                for d in range(QUAD):
                    out[d, at : at + SIX, :] = val[d * SIX : (d + 1) * SIX]
    zeros = jnp.zeros((NY, NZ), F32)
    tail = jnp.concatenate([e[NK * NY : NK * NY + NY] if first else zeros, zeros], axis=0)
    for d in range(QUAD):
        out[d, 3 * SLAB : SENT, :] = tail


def edges_kernel(first, *refs):
    if first:
        q, own, up, down = refs
    else:
        q, rest, own, up, down = refs
    rs = []
    for s in range(QUAD):
        r = q[s, 0:SLAB, :]
        if not first:
            r = r + rest[s]
        if s > 0:
            r = r + q[s - 1, SLAB : 2 * SLAB, :]
        if s + 1 < QUAD:
            r = r + q[s + 1, 2 * SLAB : 3 * SLAB, :]
        own[s] = r
        rs.append(r)
    for j in range(3):
        up[j * SLAB : (j + 1) * SLAB, :] = rs[j + 1]
        down[j * SLAB : (j + 1) * SLAB, :] = rs[j]
    up[3 * SLAB : 4 * SLAB, :] = q[3, SLAB : 2 * SLAB, :]
    down[3 * SLAB : 4 * SLAB, :] = q[0, 2 * SLAB : 3 * SLAB, :]
    if first:
        for j in range(3):
            at = 4 * SLAB + j * NY
            up[at : at + NY, :] = q[j + 1, 3 * SLAB : 3 * SLAB + NY, :]
            down[at : at + NY, :] = q[j, 3 * SLAB : 3 * SLAB + NY, :]
        up[4 * SLAB + 12 :, :] = jnp.zeros((4, NZ), F32)
        down[4 * SLAB + 12 :, :] = jnp.zeros((4, NZ), F32)


def powers_kernel(first, *refs):
    if first:
        q, own, low, high, v0, v1, v2, v3, mom, ec, w0, w1, w2, dg = refs
        for j in range(3):
            at = 4 * SLAB + j * NY
            ec[j * NY : (j + 1) * NY, :] = low[at : at + NY, :]
            ec[(7 + j) * NY : (8 + j) * NY, :] = high[at : at + NY, :]
        for s in range(QUAD):
            ec[(3 + s) * NY : (4 + s) * NY, :] = q[s, 3 * SLAB : 3 * SLAB + NY, :]
    else:
        q, own, low, high, ec, v0, v1, v2, v3, mom, w0, w1, w2, dg = refs

    def rows(ref, at, y):
        return ref[at + y * ROWS : at + (y + 1) * ROWS, :]

    rid = lax.broadcasted_iota(jnp.int32, (ROWS, NZ), 0)
    wx = jnp.where(rid < SIX, 2.0, 1.0)
    wy = jnp.where((rid >= SIX) & (rid < 2 * SIX), 2.0, 1.0)
    wz = jnp.where(rid >= 2 * SIX, 2.0, 1.0)
    lane1 = lax.broadcasted_iota(jnp.int32, (1, NZ), 1)
    em = [[ec[p * NY + y : p * NY + y + 1, :] for y in range(NY)] for p in range(10)]
    zero = jnp.zeros((1, NZ), F32)

    def inside(p, y, val):
        return val if 3 <= p <= 6 else jnp.where(em[p][y] > 0.0, val, 0.0)

    for y in range(NY):
        for p in range(3):
            lo = rows(low, p * SLAB, y)
            hi = rows(high, p * SLAB, y)
            if p == 2:
                lo = lo + rows(q.at[0], 2 * SLAB, y)
            if p == 0:
                hi = hi + rows(q.at[QUAD - 1], SLAB, y)
            w0[p * NY + y] = inside(p, y, lo)
            w0[(7 + p) * NY + y] = inside(7 + p, y, hi)
        for s in range(QUAD):
            r = rows(own.at[s], 0, y)
            if s == 0:
                r = r + rows(low, 3 * SLAB, y)
            if s == QUAD - 1:
                r = r + rows(high, 3 * SLAB, y)
            w0[(3 + s) * NY + y] = r
            v0[s * NY + y] = r

    def face(p, y):
        e = em[p][y]
        xu, xd = faces(e, em[p + 1][y]), faces(e, em[p - 1][y])
        yu = faces(e, em[p][y + 1] if y + 1 < NY else zero)
        yd = faces(e, em[p][y - 1] if y > 0 else zero)
        zu = faces(e, jnp.where(lane1 == NZ - 1, 0.0, pltpu.roll(e, NZ - 1, 1)))
        zd = faces(e, jnp.where(lane1 == 0, 0.0, pltpu.roll(e, 1, 1)))
        return xu, xd, yu, yd, zu, zd

    coef = {}
    for p in range(1, 9):
        for y in range(NY):
            xu, xd, yu, yd, zu, zd = face(p, y)
            dg[p * NY + y] = wx * (xu + xd) + wy * (yu + yd) + wz * (zu + zd) - SHIFT
            coef[p, y] = (
                xu, xd, yu, yd,
                jnp.where(lane1 == NZ - 1, 0.0, zu),
                jnp.where(lane1 == 0, 0.0, zd),
            )

    def apply(src, p, y):
        xu, xd, yu, yd, zu, zd = coef[p, y]
        m = src[p * NY + y]
        t = dg[p * NY + y] * m
        t = t - wx * (xu * src[(p + 1) * NY + y] + xd * src[(p - 1) * NY + y])
        side = None
        if y + 1 < NY:
            side = yu * src[p * NY + y + 1]
        if y > 0:
            less = yd * src[p * NY + y - 1]
            side = less if side is None else side + less
        t = t - wy * side
        t = t - wz * (zu * pltpu.roll(m, NZ - 1, 1) + zd * pltpu.roll(m, 1, 1))
        return inside(p, y, t)

    for p in range(1, 9):
        for y in range(NY):
            t = apply(w0, p, y)
            w1[p * NY + y] = t
            if 3 <= p <= 6:
                v1[(p - 3) * NY + y] = t
    for p in range(2, 8):
        for y in range(NY):
            t = apply(w1, p, y)
            w2[p * NY + y] = t
            if 3 <= p <= 6:
                v2[(p - 3) * NY + y] = t
    sums = [None] * 6
    for p in range(3, 7):
        for y in range(NY):
            a, b, d = w0[p * NY + y], w1[p * NY + y], w2[p * NY + y]
            t = apply(w2, p, y)
            v3[(p - 3) * NY + y] = t
            for j, val in enumerate((a * a, a * b, b * b, b * d, d * d, d * t)):
                sums[j] = val if sums[j] is None else sums[j] + val
    lane = lax.broadcasted_iota(jnp.int32, (ROWS, NZ), 1)
    spot = lane - 8 * (rid % SIX)
    packed = jnp.zeros((ROWS, NZ), F32)
    for j in range(6):
        packed = jnp.where(spot == j, jnp.sum(sums[j], axis=1, keepdims=True), packed)
    mom[...] = jnp.broadcast_to(jnp.sum(packed, axis=0, keepdims=True), mom.shape)


def step_coefficients(mom):
    def inner(a, b):
        total = None
        for i, s in enumerate(a):
            for j, t in enumerate(b):
                term = s * t * mom[i + j]
                total = term if total is None else total + term
        return total

    def image(a):
        q = [SHIFT * s for s in a] + [None]
        for i, s in enumerate(a):
            q[i + 1] = s if q[i + 1] is None else q[i + 1] + s
        return q

    one = jnp.ones_like(mom[0])
    x, r, p = [], [one], [one]
    rr = mom[0]
    for step in range(3):
        q = image(p)
        alpha = rr / inner(p, q)
        x = [x[i] + alpha * s if i < len(x) else alpha * s for i, s in enumerate(p)]
        r = [r[i] - alpha * s if i < len(r) else -alpha * s for i, s in enumerate(q)]
        if step < 2:
            new = inner(r, r)
            beta = new / rr
            p = [s + beta * p[i] if i < len(p) else s for i, s in enumerate(r)]
            rr = new
    return x, r


def update_kernel(first, *refs):
    if first:
        mom, v0, v1, v2, v3, out, rest = refs
    else:
        mom, half, v0, v1, v2, before, out = refs
        upper = half[...] > 0.0
    total = jnp.sum(mom[...], axis=0, keepdims=True)
    rid = lax.broadcasted_iota(jnp.int32, (ROWS, NZ), 0)
    lane = lax.broadcasted_iota(jnp.int32, (ROWS, NZ), 1)
    spot = lane - 8 * (rid % SIX)
    picked = [jnp.sum(jnp.where(spot == j, total, 0.0), axis=1, keepdims=True) for j in range(6)]
    x, r = step_coefficients(picked)
    x = [jnp.broadcast_to(s, (ROWS, NZ)) for s in x]
    r = [jnp.broadcast_to(s, (ROWS, NZ)) for s in r]
    for s in range(QUAD):
        for y in range(NY):
            at = s * NY + y
            rows = slice(y * ROWS, (y + 1) * ROWS)
            a, b, d = v0[at], v1[at], v2[at]
            change = x[0] * a + x[1] * b + x[2] * d
            if first:
                rest[s, rows, :] = r[0] * a + r[1] * b + r[2] * d + r[3] * v3[at]
            else:
                change = change + before[s, rows, :]
                for c in range(3):
                    at = c * SIX
                    pick = jnp.where(upper, change[at + TRI : at + SIX], change[at : at + TRI])
                    to = (y * 3 + c) * TRI
                    out[s, to : to + TRI, :] = pick
                continue
            out[s, rows, :] = change


def fan_kernel(blocks, field, out):
    for d in range(blocks):
        own = field[d]
        for x in range(NX):
            out[x * blocks + d] = own


def packed(field):
    return field.transpose(0, 3, 2, 1, 4).reshape(1, 2 * NY * 3 * NM, NZ)


def by_target(field):
    field = field.reshape(2, QUAD, TRI, 3, NY, NZ)
    return field.transpose(4, 3, 1, 0, 2, 5).reshape(NY * 3 * NT, NZ)


def rows_of(table, x):
    table = lax.dynamic_index_in_dim(table.reshape(2, NX, QUAD, TRI, -1), x, 1, keepdims=False)
    return table.transpose(1, 0, 2, 3).reshape(NT, -1)


def shards(load_modes, first_guess, kl_fields, region_labels, partner, variable, weight):
    mean = jnp.where(region_labels == 0, 1.3, jnp.where(region_labels == 1, 1.0, 0.6)).astype(F32)
    varying = jnp.where(region_labels[None] == 1, kl_fields, 0.0)
    moduli = jnp.concatenate([varying, mean[None]], 0).reshape((NK + 1) * NY, NZ)
    em = lax.ppermute(moduli, SLABS, line(16, 1))
    ep = lax.ppermute(moduli, SLABS, line(16, -1))
    e0 = moduli
    mine = jnp.concatenate([first_guess, load_modes], 0)
    far = lax.ppermute(mine, "zh", [(0, 1), (1, 0)])
    zh, x = lax.axis_index("zh"), lax.axis_index("x")
    lower = zh == 0
    both = jnp.stack([jnp.where(lower, mine, far), jnp.where(lower, far, mine)])
    both = both.reshape(2, 2, NM, 3, NY, NZ)
    guess, load = packed(both[:, 0]), by_target(both[:, 1])
    half = jnp.broadcast_to(zh.astype(F32), (TRI, NZ))

    own = rows_of(jnp.arange(MODES, dtype=jnp.int32), x)
    rows_partner = jnp.concatenate([rows_of(partner, x), own], 1)
    rows_variable = rows_of(variable, x)
    rows_weight = jnp.concatenate([rows_of(weight, x), jnp.ones((NT, 1), F32)], 1)
    links = (rows_partner, rows_variable, rows_weight)

    chunk, cells = (QUAD, SLAB, NZ), (QUAD * NY, ROWS, NZ)
    for sweep in range(2):
        first = sweep == 0
        nk = NK + 1 if first else NK
        blocks = 1 if first else QUAD
        field = guess if first else change
        (copies,) = call(
            functools.partial(fan_kernel, blocks), [(NX * blocks,) + field.shape[1:]]
        )(field)
        u = lax.all_to_all(copies, ("x",) if first else ("x",) + WITHIN, 0, 0, tiled=True)
        fields = (u, load, e0, em, ep) if first else (u, e0, em, ep)
        face_rows = ((NK + 1) * NY, NZ)
        (sent,) = call(
            functools.partial(coupling_kernel, nk),
            [(QUAD, SENT, NZ)],
            [
                (NY * 3, MODES, NZ),
                (NY * 3, nk * NT, NZ),
                (2,) + face_rows,
                (2,) + face_rows,
                (5,) + face_rows,
            ],
        )(*fields, *links)
        q = lax.all_to_all(sent, WITHIN, 0, 0, tiled=True)
        edge = (4 * SLAB + 16 if first else 4 * SLAB, NZ)
        chunk_r, up, down = call(functools.partial(edges_kernel, first), [chunk, edge, edge])(
            *((q,) if first else (q, rest))
        )
        low = lax.ppermute(up, CHAIN, line(4, 1))
        high = lax.ppermute(down, CHAIN, line(4, -1))
        scratch = [(10 * NY, ROWS, NZ)] * 4
        outs = [cells] * 4 + [(16, NZ)]
        if first:
            v0, v1, v2, v3, mom, ec = call(
                functools.partial(powers_kernel, True), outs + [(10 * NY, NZ)], scratch
            )(q, chunk_r, low, high)
        else:
            v0, v1, v2, v3, mom = call(functools.partial(powers_kernel, False), outs, scratch)(
                q, chunk_r, low, high, ec
            )
        mom = lax.all_to_all(mom, CHUNKS, 0, 0, tiled=True)
        if first:
            change, rest = call(functools.partial(update_kernel, True), [chunk, chunk])(
                mom, v0, v1, v2, v3
            )
        else:
            (total,) = call(
                functools.partial(update_kernel, False), [(QUAD, NY * 3 * TRI, NZ)]
            )(mom, half, v0, v1, v2, change)
    total = lax.all_to_all(total, WITHIN, 0, 0, tiled=True)
    total = total.reshape(QUAD, NY, 3, TRI, NZ).transpose(0, 3, 2, 1, 4)
    return first_guess + total.reshape(NM, 3, 1, NY, NZ)


def solution(mesh):
    split = Mesh(mesh.devices.reshape(2, 4, 4, 4, 2, 2), AXES)
    mode, space = ("zh", "x"), ("y", "zp", "zq", "c")
    return jax.shard_map(
        shards,
        mesh=split,
        in_specs=(
            P(mode, None, space, None, None),
            P(mode, None, space, None, None),
            P(None, space, None, None),
            P(space, None, None),
            P(),
            P(),
            P(),
        ),
        out_specs=P(mode, None, space, None, None),
        check_vma=False,
    )
```

```python
import functools

import jax
import jax.numpy as jnp
from jax import lax
from jax.experimental import pallas as pl
from jax.experimental.pallas import tpu as pltpu
from jax.sharding import Mesh
from jax.sharding import PartitionSpec as P

AXES = ("zh", "x", "y", "zp", "zq", "c")
SLABS = ("zh", "y", "zp", "zq", "c")
CHAIN = ("zh", "y", "zp")
CHUNKS = ("y", "zp")
WITHIN = ("zq", "c")
NX, NM, NT, NL, NK = 4, 12, 24, 8, 8
MODES = 2 * NX * NM
NY, NZ, SHIFT = 4, 128, 4.0
QUAD = 4
TRI = NM // QUAD
SIX = 2 * TRI
ROWS = 3 * SIX
SLAB = NY * ROWS
SENT = 3 * SLAB + 8
F32 = jnp.float32


def line(inner, step):
    count = 4 * inner
    pairs = []
    for zh in range(2):
        for i in range(count):
            j = i + step
            if 0 <= j < count:
                other = zh ^ (i // inner != j // inner)
                pairs.append((zh * count + i, other * count + j))
    return pairs


def call(kernel, outs, scratch=()):
    vmem = pl.BlockSpec(memory_space=pltpu.VMEM)

    def run(*args):
        return pl.pallas_call(
            kernel,
            out_shape=[pltpu.VMEM(s, F32) for s in outs],
            in_specs=[vmem] * len(args),
            out_specs=[vmem] * len(outs),
            scratch_shapes=[pltpu.VMEM(s, F32) for s in scratch],
        )(*[pltpu.with_memory_space_constraint(a, pltpu.VMEM) for a in args])

    return run


def faces(e, other):
    return 0.5 * (e + other)


def coupling_kernel(nk, *refs):
    first = nk > NK
    if first:
        (u, load, e0, em, ep, partner, variable, weight, out, us, mx, fx, fy, fz) = refs
    else:
        (u, e0, em, ep, partner, variable, weight, out, us, mx, fx, fy, fz) = refs
    for g in range(2 * NX):
        half, x = divmod(g, NX)
        for y in range(NY):
            for c in range(3):
                yc = y * 3 + c
                if first:
                    at = (half * NY * 3 + yc) * NM
                    us[yc, g * NM : (g + 1) * NM, :] = u[x, at : at + NM, :]
                    continue
                for d in range(QUAD):
                    at, to = y * ROWS + c * SIX + half * TRI, g * NM + d * TRI
                    us[yc, to : to + TRI, :] = u[x * QUAD + d, at : at + TRI, :]
    lane = lax.broadcasted_iota(jnp.int32, (NT, MODES), 1)
    pr, vr, wr = partner[...], variable[...], weight[...]
    links = NL + 1 if first else NL
    hit = [jnp.where(lane == pr[:, l : l + 1], wr[:, l : l + 1], 0.0) for l in range(links)]
    blocks = []
    for k in range(nk):
        acc = None
        for l in range(links):
            if (k == NK) != (l == NL):
                continue
            term = hit[l] if l == NL else jnp.where(vr[:, l : l + 1] == k, hit[l], 0.0)
            acc = term if acc is None else acc + term
        blocks.append(acc)
    mix = jnp.concatenate(blocks, axis=0)
    for yc in range(NY * 3):
        mx[yc] = lax.dot_general(
            mix,
            us[yc],
            (((1,), (0,)), ((), ())),
            precision=lax.Precision.HIGHEST,
            preferred_element_type=F32,
        )
    e = e0[...]
    zlane = lax.broadcasted_iota(jnp.int32, e.shape, 1)
    row = lax.broadcasted_iota(jnp.int32, e.shape, 0)
    zup = jnp.where(zlane == NZ - 1, 0.0, pltpu.roll(e, NZ - 1, 1))
    zdn = jnp.where(zlane == 0, 0.0, pltpu.roll(e, 1, 1))
    count = e.shape[0]
    yup = jnp.where(row % NY == NY - 1, 0.0, pltpu.roll(e, count - 1, 0))
    ydn = jnp.where(row % NY == 0, 0.0, pltpu.roll(e, 1, 0))
    fx[0] = faces(e, ep[...])
    fx[1] = faces(e, em[...])
    fy[0] = faces(e, yup)
    fy[1] = faces(e, ydn)
    fzu, fzd = faces(e, zup), faces(e, zdn)
    base = fx[0] + fx[1] + fy[0] + fy[1] + fzu + fzd
    fz[0] = jnp.where(zlane == NZ - 1, 0.0, fzu)
    fz[1] = jnp.where(zlane == 0, 0.0, fzd)
    fz[2] = base + fx[0] + fx[1]
    fz[3] = base + fy[0] + fy[1]
    fz[4] = base + fzu + fzd
    for y in range(NY):
        for c in range(3):
            own = up = down = None
            for k in range(nk):
                r = slice(k * NY + y, k * NY + y + 1)
                rows = slice(k * NT, (k + 1) * NT)
                m = mx[y * 3 + c, rows, :]
                t = fz[2 + c, r, :] * m
                side = None
                if y + 1 < NY:
                    side = fy[0, r, :] * mx[(y + 1) * 3 + c, rows, :]
                if y > 0:
                    less = fy[1, r, :] * mx[(y - 1) * 3 + c, rows, :]
                    side = less if side is None else side + less
                t = t - (2.0 * side if c == 1 else side)
                side = fz[0, r, :] * pltpu.roll(m, NZ - 1, 1) + fz[1, r, :] * pltpu.roll(m, 1, 1)
                t = t - (2.0 * side if c == 2 else side)
                p, q = fx[0, r, :] * m, fx[1, r, :] * m
                own, up, down = (t, p, q) if own is None else (own + t, up + p, down + q)
            if c == 0:
                up, down = 2.0 * up, 2.0 * down
            yc = y * 3 + c
            own = load[yc * NT : (yc + 1) * NT, :] - own if first else -own
            for kind, val in enumerate((own, up, down)):
                at = (kind * NY + y) * ROWS + c * SIX
                for d in range(QUAD):
                    out[d, at : at + SIX, :] = val[d * SIX : (d + 1) * SIX]
    zeros = jnp.zeros((NY, NZ), F32)
    tail = jnp.concatenate([e[NK * NY : NK * NY + NY] if first else zeros, zeros], axis=0)
    for d in range(QUAD):
        out[d, 3 * SLAB : SENT, :] = tail


def edges_kernel(first, *refs):
    if first:
        q, own, up, down = refs
    else:
        q, rest, own, up, down = refs
    rs = []
    for s in range(QUAD):
        r = q[s, 0:SLAB, :]
        if not first:
            r = r + rest[s]
        if s > 0:
            r = r + q[s - 1, SLAB : 2 * SLAB, :]
        if s + 1 < QUAD:
            r = r + q[s + 1, 2 * SLAB : 3 * SLAB, :]
        own[s] = r
        rs.append(r)
    for j in range(3):
        up[j * SLAB : (j + 1) * SLAB, :] = rs[j + 1]
        down[j * SLAB : (j + 1) * SLAB, :] = rs[j]
    up[3 * SLAB : 4 * SLAB, :] = q[3, SLAB : 2 * SLAB, :]
    down[3 * SLAB : 4 * SLAB, :] = q[0, 2 * SLAB : 3 * SLAB, :]
    if first:
        for j in range(3):
            at = 4 * SLAB + j * NY
            up[at : at + NY, :] = q[j + 1, 3 * SLAB : 3 * SLAB + NY, :]
            down[at : at + NY, :] = q[j, 3 * SLAB : 3 * SLAB + NY, :]
        up[4 * SLAB + 12 :, :] = jnp.zeros((4, NZ), F32)
        down[4 * SLAB + 12 :, :] = jnp.zeros((4, NZ), F32)


def powers_kernel(first, *refs):
    if first:
        q, own, low, high, v0, v1, v2, v3, mom, ec, w0, w1, w2, dg = refs
        for j in range(3):
            at = 4 * SLAB + j * NY
            ec[j * NY : (j + 1) * NY, :] = low[at : at + NY, :]
            ec[(7 + j) * NY : (8 + j) * NY, :] = high[at : at + NY, :]
        for s in range(QUAD):
            ec[(3 + s) * NY : (4 + s) * NY, :] = q[s, 3 * SLAB : 3 * SLAB + NY, :]
    else:
        q, own, low, high, ec, v0, v1, v2, v3, mom, w0, w1, w2, dg = refs

    def rows(ref, at, y):
        return ref[at + y * ROWS : at + (y + 1) * ROWS, :]

    rid = lax.broadcasted_iota(jnp.int32, (ROWS, NZ), 0)
    wx = jnp.where(rid < SIX, 2.0, 1.0)
    wy = jnp.where((rid >= SIX) & (rid < 2 * SIX), 2.0, 1.0)
    wz = jnp.where(rid >= 2 * SIX, 2.0, 1.0)
    lane1 = lax.broadcasted_iota(jnp.int32, (1, NZ), 1)
    em = [[ec[p * NY + y : p * NY + y + 1, :] for y in range(NY)] for p in range(10)]
    zero = jnp.zeros((1, NZ), F32)

    def inside(p, y, val):
        return val if 3 <= p <= 6 else jnp.where(em[p][y] > 0.0, val, 0.0)

    for y in range(NY):
        for p in range(3):
            lo = rows(low, p * SLAB, y)
            hi = rows(high, p * SLAB, y)
            if p == 2:
                lo = lo + rows(q.at[0], 2 * SLAB, y)
            if p == 0:
                hi = hi + rows(q.at[QUAD - 1], SLAB, y)
            w0[p * NY + y] = inside(p, y, lo)
            w0[(7 + p) * NY + y] = inside(7 + p, y, hi)
        for s in range(QUAD):
            r = rows(own.at[s], 0, y)
            if s == 0:
                r = r + rows(low, 3 * SLAB, y)
            if s == QUAD - 1:
                r = r + rows(high, 3 * SLAB, y)
            w0[(3 + s) * NY + y] = r
            v0[s * NY + y] = r

    def face(p, y):
        e = em[p][y]
        xu, xd = faces(e, em[p + 1][y]), faces(e, em[p - 1][y])
        yu = faces(e, em[p][y + 1] if y + 1 < NY else zero)
        yd = faces(e, em[p][y - 1] if y > 0 else zero)
        zu = faces(e, jnp.where(lane1 == NZ - 1, 0.0, pltpu.roll(e, NZ - 1, 1)))
        zd = faces(e, jnp.where(lane1 == 0, 0.0, pltpu.roll(e, 1, 1)))
        return xu, xd, yu, yd, zu, zd

    coef = {}
    for p in range(1, 9):
        for y in range(NY):
            xu, xd, yu, yd, zu, zd = face(p, y)
            dg[p * NY + y] = wx * (xu + xd) + wy * (yu + yd) + wz * (zu + zd) - SHIFT
            coef[p, y] = (
                xu, xd, yu, yd,
                jnp.where(lane1 == NZ - 1, 0.0, zu),
                jnp.where(lane1 == 0, 0.0, zd),
            )

    def apply(src, p, y):
        xu, xd, yu, yd, zu, zd = coef[p, y]
        m = src[p * NY + y]
        t = dg[p * NY + y] * m
        t = t - wx * (xu * src[(p + 1) * NY + y] + xd * src[(p - 1) * NY + y])
        side = None
        if y + 1 < NY:
            side = yu * src[p * NY + y + 1]
        if y > 0:
            less = yd * src[p * NY + y - 1]
            side = less if side is None else side + less
        t = t - wy * side
        t = t - wz * (zu * pltpu.roll(m, NZ - 1, 1) + zd * pltpu.roll(m, 1, 1))
        return inside(p, y, t)

    for p in range(1, 9):
        for y in range(NY):
            t = apply(w0, p, y)
            w1[p * NY + y] = t
            if 3 <= p <= 6:
                v1[(p - 3) * NY + y] = t
    for p in range(2, 8):
        for y in range(NY):
            t = apply(w1, p, y)
            w2[p * NY + y] = t
            if 3 <= p <= 6:
                v2[(p - 3) * NY + y] = t
    sums = [None] * 6
    for p in range(3, 7):
        for y in range(NY):
            a, b, d = w0[p * NY + y], w1[p * NY + y], w2[p * NY + y]
            t = apply(w2, p, y)
            v3[(p - 3) * NY + y] = t
            for j, val in enumerate((a * a, a * b, b * b, b * d, d * d, d * t)):
                sums[j] = val if sums[j] is None else sums[j] + val
    lane = lax.broadcasted_iota(jnp.int32, (ROWS, NZ), 1)
    spot = lane - 8 * (rid % SIX)
    packed = jnp.zeros((ROWS, NZ), F32)
    for j in range(6):
        packed = jnp.where(spot == j, jnp.sum(sums[j], axis=1, keepdims=True), packed)
    mom[...] = jnp.broadcast_to(jnp.sum(packed, axis=0, keepdims=True), mom.shape)


def step_coefficients(mom):
    def inner(a, b):
        total = None
        for i, s in enumerate(a):
            for j, t in enumerate(b):
                term = s * t * mom[i + j]
                total = term if total is None else total + term
        return total

    def image(a):
        q = [SHIFT * s for s in a] + [None]
        for i, s in enumerate(a):
            q[i + 1] = s if q[i + 1] is None else q[i + 1] + s
        return q

    one = jnp.ones_like(mom[0])
    x, r, p = [], [one], [one]
    rr = mom[0]
    for step in range(3):
        q = image(p)
        alpha = rr / inner(p, q)
        x = [x[i] + alpha * s if i < len(x) else alpha * s for i, s in enumerate(p)]
        r = [r[i] - alpha * s if i < len(r) else -alpha * s for i, s in enumerate(q)]
        if step < 2:
            new = inner(r, r)
            beta = new / rr
            p = [s + beta * p[i] if i < len(p) else s for i, s in enumerate(r)]
            rr = new
    return x, r


def update_kernel(first, *refs):
    if first:
        mom, v0, v1, v2, v3, out, rest = refs
    else:
        mom, half, v0, v1, v2, before, out = refs
        upper = half[...] > 0.0
    total = jnp.sum(mom[...], axis=0, keepdims=True)
    rid = lax.broadcasted_iota(jnp.int32, (ROWS, NZ), 0)
    lane = lax.broadcasted_iota(jnp.int32, (ROWS, NZ), 1)
    spot = lane - 8 * (rid % SIX)
    picked = [jnp.sum(jnp.where(spot == j, total, 0.0), axis=1, keepdims=True) for j in range(6)]
    x, r = step_coefficients(picked)
    x = [jnp.broadcast_to(s, (ROWS, NZ)) for s in x]
    r = [jnp.broadcast_to(s, (ROWS, NZ)) for s in r]
    for s in range(QUAD):
        for y in range(NY):
            at = s * NY + y
            rows = slice(y * ROWS, (y + 1) * ROWS)
            a, b, d = v0[at], v1[at], v2[at]
            change = x[0] * a + x[1] * b + x[2] * d
            if first:
                rest[s, rows, :] = r[0] * a + r[1] * b + r[2] * d + r[3] * v3[at]
            else:
                change = change + before[s, rows, :]
                for c in range(3):
                    at = c * SIX
                    pick = jnp.where(upper, change[at + TRI : at + SIX], change[at : at + TRI])
                    to = (y * 3 + c) * TRI
                    out[s, to : to + TRI, :] = pick
                continue
            out[s, rows, :] = change


def fan_kernel(blocks, field, out):
    for d in range(blocks):
        own = field[d]
        for x in range(NX):
            out[x * blocks + d] = own


def packed(field):
    return field.transpose(0, 3, 2, 1, 4).reshape(1, 2 * NY * 3 * NM, NZ)


def by_target(field):
    field = field.reshape(2, QUAD, TRI, 3, NY, NZ)
    return field.transpose(4, 3, 1, 0, 2, 5).reshape(NY * 3 * NT, NZ)


def rows_of(table, x):
    table = lax.dynamic_index_in_dim(table.reshape(2, NX, QUAD, TRI, -1), x, 1, keepdims=False)
    return table.transpose(1, 0, 2, 3).reshape(NT, -1)


def shards(load_modes, first_guess, kl_fields, region_labels, partner, variable, weight):
    mean = jnp.where(region_labels == 0, 1.3, jnp.where(region_labels == 1, 1.0, 0.6)).astype(F32)
    varying = jnp.where(region_labels[None] == 1, kl_fields, 0.0)
    moduli = jnp.concatenate([varying, mean[None]], 0).reshape((NK + 1) * NY, NZ)
    em = lax.ppermute(moduli, SLABS, line(16, 1))
    ep = lax.ppermute(moduli, SLABS, line(16, -1))
    e0 = moduli
    swap = [(0, 1), (1, 0)]
    zh, x = lax.axis_index("zh"), lax.axis_index("x")
    lower = zh == 0

    def halves(mine):
        far = lax.ppermute(mine, "zh", swap)
        both = jnp.stack([jnp.where(lower, mine, far), jnp.where(lower, far, mine)])
        return both.reshape(2, NM, 3, NY, NZ)

    guess, load = packed(halves(first_guess)), by_target(halves(load_modes))
    half = jnp.broadcast_to(zh.astype(F32), (TRI, NZ))

    own = rows_of(jnp.arange(MODES, dtype=jnp.int32), x)
    rows_partner = jnp.concatenate([rows_of(partner, x), own], 1)
    rows_variable = rows_of(variable, x)
    rows_weight = jnp.concatenate([rows_of(weight, x), jnp.ones((NT, 1), F32)], 1)
    links = (rows_partner, rows_variable, rows_weight)

    chunk, cells = (QUAD, SLAB, NZ), (QUAD * NY, ROWS, NZ)
    for sweep in range(2):
        first = sweep == 0
        nk = NK + 1 if first else NK
        blocks = 1 if first else QUAD
        field = guess if first else change
        (copies,) = call(
            functools.partial(fan_kernel, blocks), [(NX * blocks,) + field.shape[1:]]
        )(field)
        u = lax.all_to_all(copies, ("x",) if first else ("x",) + WITHIN, 0, 0, tiled=True)
        fields = (u, load, e0, em, ep) if first else (u, e0, em, ep)
        face_rows = ((NK + 1) * NY, NZ)
        (sent,) = call(
            functools.partial(coupling_kernel, nk),
            [(QUAD, SENT, NZ)],
            [
                (NY * 3, MODES, NZ),
                (NY * 3, nk * NT, NZ),
                (2,) + face_rows,
                (2,) + face_rows,
                (5,) + face_rows,
            ],
        )(*fields, *links)
        q = lax.all_to_all(sent, WITHIN, 0, 0, tiled=True)
        edge = (4 * SLAB + 16 if first else 4 * SLAB, NZ)
        chunk_r, up, down = call(functools.partial(edges_kernel, first), [chunk, edge, edge])(
            *((q,) if first else (q, rest))
        )
        low = lax.ppermute(up, CHAIN, line(4, 1))
        high = lax.ppermute(down, CHAIN, line(4, -1))
        scratch = [(10 * NY, ROWS, NZ)] * 4
        outs = [cells] * 4 + [(16, NZ)]
        if first:
            v0, v1, v2, v3, mom, ec = call(
                functools.partial(powers_kernel, True), outs + [(10 * NY, NZ)], scratch
            )(q, chunk_r, low, high)
        else:
            v0, v1, v2, v3, mom = call(functools.partial(powers_kernel, False), outs, scratch)(
                q, chunk_r, low, high, ec
            )
        mom = lax.all_to_all(mom, CHUNKS, 0, 0, tiled=True)
        if first:
            change, rest = call(functools.partial(update_kernel, True), [chunk, chunk])(
                mom, v0, v1, v2, v3
            )
        else:
            (total,) = call(
                functools.partial(update_kernel, False), [(QUAD, NY * 3 * TRI, NZ)]
            )(mom, half, v0, v1, v2, change)
    total = lax.all_to_all(total, WITHIN, 0, 0, tiled=True)
    total = total.reshape(QUAD, NY, 3, TRI, NZ).transpose(0, 3, 2, 1, 4)
    return first_guess + total.reshape(NM, 3, 1, NY, NZ)


def solution(mesh):
    split = Mesh(mesh.devices.reshape(2, 4, 4, 4, 2, 2), AXES)
    mode, space = ("zh", "x"), ("y", "zp", "zq", "c")
    return jax.shard_map(
        shards,
        mesh=split,
        in_specs=(
            P(mode, None, space, None, None),
            P(mode, None, space, None, None),
            P(None, space, None, None),
            P(space, None, None),
            P(),
            P(),
            P(),
        ),
        out_specs=P(mode, None, space, None, None),
        check_vma=False,
    )
```

```python
import functools

import jax
import jax.numpy as jnp
from jax import lax
from jax.experimental import pallas as pl
from jax.experimental.pallas import tpu as pltpu
from jax.sharding import Mesh
from jax.sharding import PartitionSpec as P

AXES = ("zh", "x", "y", "zp", "zq", "c")
SLABS = ("zh", "y", "zp", "zq", "c")
CHAIN = ("zh", "y", "zp")
CHUNKS = ("y", "zp")
WITHIN = ("zq", "c")
NX, NM, NT, NL, NK = 4, 12, 24, 8, 8
MODES = 2 * NX * NM
NY, NZ, SHIFT = 4, 128, 4.0
QUAD = 4
TRI = NM // QUAD
SIX = 2 * TRI
ROWS = 3 * SIX
SLAB = NY * ROWS
SENT = 3 * SLAB + 8
F32 = jnp.float32


def line(inner, step):
    count = 4 * inner
    pairs = []
    for zh in range(2):
        for i in range(count):
            j = i + step
            if 0 <= j < count:
                other = zh ^ (i // inner != j // inner)
                pairs.append((zh * count + i, other * count + j))
    return pairs


def call(kernel, outs, scratch=()):
    vmem = pl.BlockSpec(memory_space=pltpu.VMEM)

    def run(*args):
        return pl.pallas_call(
            kernel,
            out_shape=[pltpu.VMEM(s, F32) for s in outs],
            in_specs=[vmem] * len(args),
            out_specs=[vmem] * len(outs),
            scratch_shapes=[pltpu.VMEM(s, F32) for s in scratch],
        )(*[pltpu.with_memory_space_constraint(a, pltpu.VMEM) for a in args])

    return run


def faces(e, other):
    return 0.5 * (e + other)


def coupling_kernel(nk, *refs):
    first = nk > NK
    if first:
        (u, load, e0, em, ep, partner, variable, weight, out, us, mx, fx, fy, fz) = refs
    else:
        (u, e0, em, ep, partner, variable, weight, out, us, mx, fx, fy, fz) = refs
    for g in range(2 * NX):
        half, x = divmod(g, NX)
        for y in range(NY):
            for c in range(3):
                yc = y * 3 + c
                if first:
                    at = (half * NY * 3 + yc) * NM
                    us[yc, g * NM : (g + 1) * NM, :] = u[x, at : at + NM, :]
                    continue
                for d in range(QUAD):
                    at, to = y * ROWS + c * SIX + half * TRI, g * NM + d * TRI
                    us[yc, to : to + TRI, :] = u[x * QUAD + d, at : at + TRI, :]
    lane = lax.broadcasted_iota(jnp.int32, (NT, MODES), 1)
    pr, vr, wr = partner[...], variable[...], weight[...]
    links = NL + 1 if first else NL
    hit = [jnp.where(lane == pr[:, l : l + 1], wr[:, l : l + 1], 0.0) for l in range(links)]
    blocks = []
    for k in range(nk):
        acc = None
        for l in range(links):
            if (k == NK) != (l == NL):
                continue
            term = hit[l] if l == NL else jnp.where(vr[:, l : l + 1] == k, hit[l], 0.0)
            acc = term if acc is None else acc + term
        blocks.append(acc)
    mix = jnp.concatenate(blocks, axis=0)
    for yc in range(NY * 3):
        mx[yc] = lax.dot_general(
            mix,
            us[yc],
            (((1,), (0,)), ((), ())),
            precision=lax.Precision.HIGHEST,
            preferred_element_type=F32,
        )
    e = e0[...]
    zlane = lax.broadcasted_iota(jnp.int32, e.shape, 1)
    row = lax.broadcasted_iota(jnp.int32, e.shape, 0)
    zup = jnp.where(zlane == NZ - 1, 0.0, pltpu.roll(e, NZ - 1, 1))
    zdn = jnp.where(zlane == 0, 0.0, pltpu.roll(e, 1, 1))
    count = e.shape[0]
    yup = jnp.where(row % NY == NY - 1, 0.0, pltpu.roll(e, count - 1, 0))
    ydn = jnp.where(row % NY == 0, 0.0, pltpu.roll(e, 1, 0))
    fx[0] = faces(e, ep[...])
    fx[1] = faces(e, em[...])
    fy[0] = faces(e, yup)
    fy[1] = faces(e, ydn)
    fzu, fzd = faces(e, zup), faces(e, zdn)
    base = fx[0] + fx[1] + fy[0] + fy[1] + fzu + fzd
    fz[0] = jnp.where(zlane == NZ - 1, 0.0, fzu)
    fz[1] = jnp.where(zlane == 0, 0.0, fzd)
    fz[2] = base + fx[0] + fx[1]
    fz[3] = base + fy[0] + fy[1]
    fz[4] = base + fzu + fzd
    for y in range(NY):
        for c in range(3):
            own = up = down = None
            for k in range(nk):
                r = slice(k * NY + y, k * NY + y + 1)
                rows = slice(k * NT, (k + 1) * NT)
                m = mx[y * 3 + c, rows, :]
                t = fz[2 + c, r, :] * m
                side = None
                if y + 1 < NY:
                    side = fy[0, r, :] * mx[(y + 1) * 3 + c, rows, :]
                if y > 0:
                    less = fy[1, r, :] * mx[(y - 1) * 3 + c, rows, :]
                    side = less if side is None else side + less
                t = t - (2.0 * side if c == 1 else side)
                side = fz[0, r, :] * pltpu.roll(m, NZ - 1, 1) + fz[1, r, :] * pltpu.roll(m, 1, 1)
                t = t - (2.0 * side if c == 2 else side)
                p, q = fx[0, r, :] * m, fx[1, r, :] * m
                own, up, down = (t, p, q) if own is None else (own + t, up + p, down + q)
            if c == 0:
                up, down = 2.0 * up, 2.0 * down
            yc = y * 3 + c
            own = load[yc * NT : (yc + 1) * NT, :] - own if first else -own
            for kind, val in enumerate((own, up, down)):
                at = (kind * NY + y) * ROWS + c * SIX
                for d in range(QUAD):
                    out[d, at : at + SIX, :] = val[d * SIX : (d + 1) * SIX]
    zeros = jnp.zeros((NY, NZ), F32)
    tail = jnp.concatenate([e[NK * NY : NK * NY + NY] if first else zeros, zeros], axis=0)
    for d in range(QUAD):
        out[d, 3 * SLAB : SENT, :] = tail


def edges_kernel(first, *refs):
    if first:
        q, own, up, down = refs
    else:
        q, rest, own, up, down = refs
    rs = []
    for s in range(QUAD):
        r = q[s, 0:SLAB, :]
        if not first:
            r = r + rest[s]
        if s > 0:
            r = r + q[s - 1, SLAB : 2 * SLAB, :]
        if s + 1 < QUAD:
            r = r + q[s + 1, 2 * SLAB : 3 * SLAB, :]
        own[s] = r
        rs.append(r)
    for j in range(3):
        up[j * SLAB : (j + 1) * SLAB, :] = rs[j + 1]
        down[j * SLAB : (j + 1) * SLAB, :] = rs[j]
    up[3 * SLAB : 4 * SLAB, :] = q[3, SLAB : 2 * SLAB, :]
    down[3 * SLAB : 4 * SLAB, :] = q[0, 2 * SLAB : 3 * SLAB, :]
    if first:
        for j in range(3):
            at = 4 * SLAB + j * NY
            up[at : at + NY, :] = q[j + 1, 3 * SLAB : 3 * SLAB + NY, :]
            down[at : at + NY, :] = q[j, 3 * SLAB : 3 * SLAB + NY, :]
        up[4 * SLAB + 12 :, :] = jnp.zeros((4, NZ), F32)
        down[4 * SLAB + 12 :, :] = jnp.zeros((4, NZ), F32)


def powers_kernel(first, *refs):
    if first:
        q, own, low, high, v0, v1, v2, v3, mom, ec, w0, w1, w2, dg = refs
        for j in range(3):
            at = 4 * SLAB + j * NY
            ec[j * NY : (j + 1) * NY, :] = low[at : at + NY, :]
            ec[(7 + j) * NY : (8 + j) * NY, :] = high[at : at + NY, :]
        for s in range(QUAD):
            ec[(3 + s) * NY : (4 + s) * NY, :] = q[s, 3 * SLAB : 3 * SLAB + NY, :]
    else:
        q, own, low, high, ec, v0, v1, v2, v3, mom, w0, w1, w2, dg = refs

    def rows(ref, at, y):
        return ref[at + y * ROWS : at + (y + 1) * ROWS, :]

    rid = lax.broadcasted_iota(jnp.int32, (ROWS, NZ), 0)
    wx = jnp.where(rid < SIX, 2.0, 1.0)
    wy = jnp.where((rid >= SIX) & (rid < 2 * SIX), 2.0, 1.0)
    wz = jnp.where(rid >= 2 * SIX, 2.0, 1.0)
    lane1 = lax.broadcasted_iota(jnp.int32, (1, NZ), 1)
    em = [[ec[p * NY + y : p * NY + y + 1, :] for y in range(NY)] for p in range(10)]
    zero = jnp.zeros((1, NZ), F32)

    def inside(p, y, val):
        return val if 3 <= p <= 6 else jnp.where(em[p][y] > 0.0, val, 0.0)

    for y in range(NY):
        for p in range(3):
            lo = rows(low, p * SLAB, y)
            hi = rows(high, p * SLAB, y)
            if p == 2:
                lo = lo + rows(q.at[0], 2 * SLAB, y)
            if p == 0:
                hi = hi + rows(q.at[QUAD - 1], SLAB, y)
            w0[p * NY + y] = inside(p, y, lo)
            w0[(7 + p) * NY + y] = inside(7 + p, y, hi)
        for s in range(QUAD):
            r = rows(own.at[s], 0, y)
            if s == 0:
                r = r + rows(low, 3 * SLAB, y)
            if s == QUAD - 1:
                r = r + rows(high, 3 * SLAB, y)
            w0[(3 + s) * NY + y] = r
            v0[s * NY + y] = r

    def face(p, y):
        e = em[p][y]
        xu, xd = faces(e, em[p + 1][y]), faces(e, em[p - 1][y])
        yu = faces(e, em[p][y + 1] if y + 1 < NY else zero)
        yd = faces(e, em[p][y - 1] if y > 0 else zero)
        zu = faces(e, jnp.where(lane1 == NZ - 1, 0.0, pltpu.roll(e, NZ - 1, 1)))
        zd = faces(e, jnp.where(lane1 == 0, 0.0, pltpu.roll(e, 1, 1)))
        return xu, xd, yu, yd, zu, zd

    coef = {}
    for p in range(1, 9):
        for y in range(NY):
            xu, xd, yu, yd, zu, zd = face(p, y)
            dg[p * NY + y] = wx * (xu + xd) + wy * (yu + yd) + wz * (zu + zd) - SHIFT
            coef[p, y] = (
                xu, xd, yu, yd,
                jnp.where(lane1 == NZ - 1, 0.0, zu),
                jnp.where(lane1 == 0, 0.0, zd),
            )

    def apply(src, p, y):
        xu, xd, yu, yd, zu, zd = coef[p, y]
        m = src[p * NY + y]
        t = dg[p * NY + y] * m
        t = t - wx * (xu * src[(p + 1) * NY + y] + xd * src[(p - 1) * NY + y])
        side = None
        if y + 1 < NY:
            side = yu * src[p * NY + y + 1]
        if y > 0:
            less = yd * src[p * NY + y - 1]
            side = less if side is None else side + less
        t = t - wy * side
        t = t - wz * (zu * pltpu.roll(m, NZ - 1, 1) + zd * pltpu.roll(m, 1, 1))
        return inside(p, y, t)

    for p in range(1, 9):
        for y in range(NY):
            t = apply(w0, p, y)
            w1[p * NY + y] = t
            if 3 <= p <= 6:
                v1[(p - 3) * NY + y] = t
    for p in range(2, 8):
        for y in range(NY):
            t = apply(w1, p, y)
            w2[p * NY + y] = t
            if 3 <= p <= 6:
                v2[(p - 3) * NY + y] = t
    sums = [None] * 6
    for p in range(3, 7):
        for y in range(NY):
            a, b, d = w0[p * NY + y], w1[p * NY + y], w2[p * NY + y]
            t = apply(w2, p, y)
            v3[(p - 3) * NY + y] = t
            for j, val in enumerate((a * a, a * b, b * b, b * d, d * d, d * t)):
                sums[j] = val if sums[j] is None else sums[j] + val
    lane = lax.broadcasted_iota(jnp.int32, (ROWS, NZ), 1)
    spot = lane - 8 * (rid % SIX)
    packed = jnp.zeros((ROWS, NZ), F32)
    for j in range(6):
        packed = jnp.where(spot == j, jnp.sum(sums[j], axis=1, keepdims=True), packed)
    mom[...] = jnp.broadcast_to(jnp.sum(packed, axis=0, keepdims=True), mom.shape)


def step_coefficients(mom):
    def inner(a, b):
        total = None
        for i, s in enumerate(a):
            for j, t in enumerate(b):
                term = s * t * mom[i + j]
                total = term if total is None else total + term
        return total

    def image(a):
        q = [SHIFT * s for s in a] + [None]
        for i, s in enumerate(a):
            q[i + 1] = s if q[i + 1] is None else q[i + 1] + s
        return q

    one = jnp.ones_like(mom[0])
    x, r, p = [], [one], [one]
    rr = mom[0]
    for step in range(3):
        q = image(p)
        alpha = rr / inner(p, q)
        x = [x[i] + alpha * s if i < len(x) else alpha * s for i, s in enumerate(p)]
        r = [r[i] - alpha * s if i < len(r) else -alpha * s for i, s in enumerate(q)]
        if step < 2:
            new = inner(r, r)
            beta = new / rr
            p = [s + beta * p[i] if i < len(p) else s for i, s in enumerate(r)]
            rr = new
    return x, r


def update_kernel(first, *refs):
    if first:
        mom, v0, v1, v2, v3, out, rest = refs
    else:
        mom, half, v0, v1, v2, before, out = refs
        upper = half[...] > 0.0
    total = jnp.sum(mom[...], axis=0, keepdims=True)
    rid = lax.broadcasted_iota(jnp.int32, (ROWS, NZ), 0)
    lane = lax.broadcasted_iota(jnp.int32, (ROWS, NZ), 1)
    spot = lane - 8 * (rid % SIX)
    picked = [jnp.sum(jnp.where(spot == j, total, 0.0), axis=1, keepdims=True) for j in range(6)]
    x, r = step_coefficients(picked)
    x = [jnp.broadcast_to(s, (ROWS, NZ)) for s in x]
    r = [jnp.broadcast_to(s, (ROWS, NZ)) for s in r]
    for s in range(QUAD):
        for y in range(NY):
            at = s * NY + y
            rows = slice(y * ROWS, (y + 1) * ROWS)
            a, b, d = v0[at], v1[at], v2[at]
            change = x[0] * a + x[1] * b + x[2] * d
            if first:
                rest[s, rows, :] = r[0] * a + r[1] * b + r[2] * d + r[3] * v3[at]
            else:
                change = change + before[s, rows, :]
                for c in range(3):
                    at = c * SIX
                    pick = jnp.where(upper, change[at + TRI : at + SIX], change[at : at + TRI])
                    to = (y * 3 + c) * TRI
                    out[s, to : to + TRI, :] = pick
                continue
            out[s, rows, :] = change


def fan_kernel(blocks, field, out):
    for d in range(blocks):
        own = field[d]
        for x in range(NX):
            out[x * blocks + d] = own


def packed(field):
    return field.transpose(0, 3, 2, 1, 4).reshape(1, 2 * NY * 3 * NM, NZ)


def by_target(field):
    field = field.reshape(2, QUAD, TRI, 3, NY, NZ)
    return field.transpose(4, 3, 1, 0, 2, 5).reshape(NY * 3 * NT, NZ)


def rows_of(table, x):
    table = lax.dynamic_index_in_dim(table.reshape(2, NX, QUAD, TRI, -1), x, 1, keepdims=False)
    return table.transpose(1, 0, 2, 3).reshape(NT, -1)


def shards(load_modes, first_guess, kl_fields, region_labels, partner, variable, weight):
    swap = [(0, 1), (1, 0)]
    zh, x = lax.axis_index("zh"), lax.axis_index("x")
    lower = zh == 0

    def halves(mine, far):
        both = jnp.stack([jnp.where(lower, mine, far), jnp.where(lower, far, mine)])
        return both.reshape(2, NM, 3, NY, NZ)

    far = lax.ppermute(first_guess, "zh", swap)
    load = by_target(halves(load_modes, lax.ppermute(load_modes, "zh", swap)))
    far, kl_fields, region_labels, partner, variable, weight = lax.optimization_barrier(
        (far, kl_fields, region_labels, partner, variable, weight)
    )
    guess = packed(halves(first_guess, far))
    mean = jnp.where(region_labels == 0, 1.3, jnp.where(region_labels == 1, 1.0, 0.6)).astype(F32)
    varying = jnp.where(region_labels[None] == 1, kl_fields, 0.0)
    e0 = jnp.concatenate([varying, mean[None]], 0).reshape((NK + 1) * NY, NZ)
    em = lax.ppermute(e0, SLABS, line(16, 1))
    ep = lax.ppermute(e0, SLABS, line(16, -1))
    half = jnp.broadcast_to(zh.astype(F32), (TRI, NZ))

    own = rows_of(jnp.arange(MODES, dtype=jnp.int32), x)
    rows_partner = jnp.concatenate([rows_of(partner, x), own], 1)
    rows_variable = rows_of(variable, x)
    rows_weight = jnp.concatenate([rows_of(weight, x), jnp.ones((NT, 1), F32)], 1)
    links = (rows_partner, rows_variable, rows_weight)

    chunk, cells = (QUAD, SLAB, NZ), (QUAD * NY, ROWS, NZ)
    for sweep in range(2):
        first = sweep == 0
        nk = NK + 1 if first else NK
        blocks = 1 if first else QUAD
        field = guess if first else change
        (copies,) = call(
            functools.partial(fan_kernel, blocks), [(NX * blocks,) + field.shape[1:]]
        )(field)
        u = lax.all_to_all(copies, ("x",) if first else ("x",) + WITHIN, 0, 0, tiled=True)
        fields = (u, load, e0, em, ep) if first else (u, e0, em, ep)
        face_rows = ((NK + 1) * NY, NZ)
        (sent,) = call(
            functools.partial(coupling_kernel, nk),
            [(QUAD, SENT, NZ)],
            [
                (NY * 3, MODES, NZ),
                (NY * 3, nk * NT, NZ),
                (2,) + face_rows,
                (2,) + face_rows,
                (5,) + face_rows,
            ],
        )(*fields, *links)
        q = lax.all_to_all(sent, WITHIN, 0, 0, tiled=True)
        edge = (4 * SLAB + 16 if first else 4 * SLAB, NZ)
        chunk_r, up, down = call(functools.partial(edges_kernel, first), [chunk, edge, edge])(
            *((q,) if first else (q, rest))
        )
        low = lax.ppermute(up, CHAIN, line(4, 1))
        high = lax.ppermute(down, CHAIN, line(4, -1))
        scratch = [(10 * NY, ROWS, NZ)] * 4
        outs = [cells] * 4 + [(16, NZ)]
        if first:
            v0, v1, v2, v3, mom, ec = call(
                functools.partial(powers_kernel, True), outs + [(10 * NY, NZ)], scratch
            )(q, chunk_r, low, high)
        else:
            v0, v1, v2, v3, mom = call(functools.partial(powers_kernel, False), outs, scratch)(
                q, chunk_r, low, high, ec
            )
        mom = lax.all_to_all(mom, CHUNKS, 0, 0, tiled=True)
        if first:
            change, rest = call(functools.partial(update_kernel, True), [chunk, chunk])(
                mom, v0, v1, v2, v3
            )
        else:
            (total,) = call(
                functools.partial(update_kernel, False), [(QUAD, NY * 3 * TRI, NZ)]
            )(mom, half, v0, v1, v2, change)
    total = lax.all_to_all(total, WITHIN, 0, 0, tiled=True)
    total = total.reshape(QUAD, NY, 3, TRI, NZ).transpose(0, 3, 2, 1, 4)
    return first_guess + total.reshape(NM, 3, 1, NY, NZ)


def solution(mesh):
    split = Mesh(mesh.devices.reshape(2, 4, 4, 4, 2, 2), AXES)
    mode, space = ("zh", "x"), ("y", "zp", "zq", "c")
    return jax.shard_map(
        shards,
        mesh=split,
        in_specs=(
            P(mode, None, space, None, None),
            P(mode, None, space, None, None),
            P(None, space, None, None),
            P(space, None, None),
            P(),
            P(),
            P(),
        ),
        out_specs=P(mode, None, space, None, None),
        check_vma=False,
    )
```

```python
import functools

import jax
import jax.numpy as jnp
from jax import lax
from jax.experimental import pallas as pl
from jax.experimental.pallas import tpu as pltpu
from jax.sharding import Mesh
from jax.sharding import PartitionSpec as P

AXES = ("zh", "x", "y", "zp", "zq", "c")
SLABS = ("zh", "y", "zp", "zq", "c")
CHAIN = ("zh", "y", "zp")
CHUNKS = ("y", "zp")
WITHIN = ("zq", "c")
NX, NM, NT, NL, NK = 4, 12, 24, 8, 8
MODES = 2 * NX * NM
NY, NZ, SHIFT = 4, 128, 4.0
QUAD = 4
TRI = NM // QUAD
SIX = 2 * TRI
ROWS = 3 * SIX
SLAB = NY * ROWS
SENT = 3 * SLAB + 8
F32 = jnp.float32


def line(inner, step):
    count = 4 * inner
    pairs = []
    for zh in range(2):
        for i in range(count):
            j = i + step
            if 0 <= j < count:
                other = zh ^ (i // inner != j // inner)
                pairs.append((zh * count + i, other * count + j))
    return pairs


def call(kernel, outs, scratch=()):
    vmem = pl.BlockSpec(memory_space=pltpu.VMEM)

    def run(*args):
        return pl.pallas_call(
            kernel,
            out_shape=[pltpu.VMEM(s, F32) for s in outs],
            in_specs=[vmem] * len(args),
            out_specs=[vmem] * len(outs),
            scratch_shapes=[pltpu.VMEM(s, F32) for s in scratch],
        )(*[pltpu.with_memory_space_constraint(a, pltpu.VMEM) for a in args])

    return run


def faces(e, other):
    return 0.5 * (e + other)


def coupling_kernel(nk, *refs):
    first = nk > NK
    if first:
        (u, load, e0, em, ep, partner, variable, weight, out, us, mx, fx, fy, fz) = refs
    else:
        (u, e0, em, ep, partner, variable, weight, out, us, mx, fx, fy, fz) = refs
    for g in range(2 * NX):
        half, x = divmod(g, NX)
        for y in range(NY):
            for c in range(3):
                yc = y * 3 + c
                if first:
                    at = (half * NY * 3 + yc) * NM
                    us[yc, g * NM : (g + 1) * NM, :] = u[x, at : at + NM, :]
                    continue
                for d in range(QUAD):
                    at, to = y * ROWS + c * SIX + half * TRI, g * NM + d * TRI
                    us[yc, to : to + TRI, :] = u[x * QUAD + d, at : at + TRI, :]
    lane = lax.broadcasted_iota(jnp.int32, (NT, MODES), 1)
    pr, vr, wr = partner[...], variable[...], weight[...]
    links = NL + 1 if first else NL
    hit = [jnp.where(lane == pr[:, l : l + 1], wr[:, l : l + 1], 0.0) for l in range(links)]
    blocks = []
    for k in range(nk):
        acc = None
        for l in range(links):
            if (k == NK) != (l == NL):
                continue
            term = hit[l] if l == NL else jnp.where(vr[:, l : l + 1] == k, hit[l], 0.0)
            acc = term if acc is None else acc + term
        blocks.append(acc)
    mix = jnp.concatenate(blocks, axis=0)
    for yc in range(NY * 3):
        mx[yc] = lax.dot_general(
            mix,
            us[yc],
            (((1,), (0,)), ((), ())),
            precision=lax.Precision.HIGHEST,
            preferred_element_type=F32,
        )
    e = e0[...]
    zlane = lax.broadcasted_iota(jnp.int32, e.shape, 1)
    row = lax.broadcasted_iota(jnp.int32, e.shape, 0)
    zup = jnp.where(zlane == NZ - 1, 0.0, pltpu.roll(e, NZ - 1, 1))
    zdn = jnp.where(zlane == 0, 0.0, pltpu.roll(e, 1, 1))
    count = e.shape[0]
    yup = jnp.where(row % NY == NY - 1, 0.0, pltpu.roll(e, count - 1, 0))
    ydn = jnp.where(row % NY == 0, 0.0, pltpu.roll(e, 1, 0))
    fx[0] = faces(e, ep[...])
    fx[1] = faces(e, em[...])
    fy[0] = faces(e, yup)
    fy[1] = faces(e, ydn)
    fzu, fzd = faces(e, zup), faces(e, zdn)
    base = fx[0] + fx[1] + fy[0] + fy[1] + fzu + fzd
    fz[0] = jnp.where(zlane == NZ - 1, 0.0, fzu)
    fz[1] = jnp.where(zlane == 0, 0.0, fzd)
    fz[2] = base + fx[0] + fx[1]
    fz[3] = base + fy[0] + fy[1]
    fz[4] = base + fzu + fzd
    for y in range(NY):
        for c in range(3):
            own = up = down = None
            for k in range(nk):
                r = slice(k * NY + y, k * NY + y + 1)
                rows = slice(k * NT, (k + 1) * NT)
                m = mx[y * 3 + c, rows, :]
                t = fz[2 + c, r, :] * m
                side = None
                if y + 1 < NY:
                    side = fy[0, r, :] * mx[(y + 1) * 3 + c, rows, :]
                if y > 0:
                    less = fy[1, r, :] * mx[(y - 1) * 3 + c, rows, :]
                    side = less if side is None else side + less
                t = t - (2.0 * side if c == 1 else side)
                side = fz[0, r, :] * pltpu.roll(m, NZ - 1, 1) + fz[1, r, :] * pltpu.roll(m, 1, 1)
                t = t - (2.0 * side if c == 2 else side)
                p, q = fx[0, r, :] * m, fx[1, r, :] * m
                own, up, down = (t, p, q) if own is None else (own + t, up + p, down + q)
            if c == 0:
                up, down = 2.0 * up, 2.0 * down
            yc = y * 3 + c
            own = load[yc * NT : (yc + 1) * NT, :] - own if first else -own
            for kind, val in enumerate((own, up, down)):
                at = (kind * NY + y) * ROWS + c * SIX
                for d in range(QUAD):
                    out[d, at : at + SIX, :] = val[d * SIX : (d + 1) * SIX]
    zeros = jnp.zeros((NY, NZ), F32)
    tail = jnp.concatenate([e[NK * NY : NK * NY + NY] if first else zeros, zeros], axis=0)
    for d in range(QUAD):
        out[d, 3 * SLAB : SENT, :] = tail


def edges_kernel(first, *refs):
    if first:
        q, own, up, down = refs
    else:
        q, rest, own, up, down = refs
    rs = []
    for s in range(QUAD):
        r = q[s, 0:SLAB, :]
        if not first:
            r = r + rest[s]
        if s > 0:
            r = r + q[s - 1, SLAB : 2 * SLAB, :]
        if s + 1 < QUAD:
            r = r + q[s + 1, 2 * SLAB : 3 * SLAB, :]
        own[s] = r
        rs.append(r)
    for j in range(3):
        up[j * SLAB : (j + 1) * SLAB, :] = rs[j + 1]
        down[j * SLAB : (j + 1) * SLAB, :] = rs[j]
    up[3 * SLAB : 4 * SLAB, :] = q[3, SLAB : 2 * SLAB, :]
    down[3 * SLAB : 4 * SLAB, :] = q[0, 2 * SLAB : 3 * SLAB, :]
    if first:
        for j in range(3):
            at = 4 * SLAB + j * NY
            up[at : at + NY, :] = q[j + 1, 3 * SLAB : 3 * SLAB + NY, :]
            down[at : at + NY, :] = q[j, 3 * SLAB : 3 * SLAB + NY, :]
        up[4 * SLAB + 12 :, :] = jnp.zeros((4, NZ), F32)
        down[4 * SLAB + 12 :, :] = jnp.zeros((4, NZ), F32)


def powers_kernel(first, *refs):
    if first:
        q, own, low, high, v0, v1, v2, v3, mom, ec, w0, w1, w2, dg = refs
        for j in range(3):
            at = 4 * SLAB + j * NY
            ec[j * NY : (j + 1) * NY, :] = low[at : at + NY, :]
            ec[(7 + j) * NY : (8 + j) * NY, :] = high[at : at + NY, :]
        for s in range(QUAD):
            ec[(3 + s) * NY : (4 + s) * NY, :] = q[s, 3 * SLAB : 3 * SLAB + NY, :]
    else:
        q, own, low, high, ec, v0, v1, v2, v3, mom, w0, w1, w2, dg = refs

    def rows(ref, at, y):
        return ref[at + y * ROWS : at + (y + 1) * ROWS, :]

    rid = lax.broadcasted_iota(jnp.int32, (ROWS, NZ), 0)
    wx = jnp.where(rid < SIX, 2.0, 1.0)
    wy = jnp.where((rid >= SIX) & (rid < 2 * SIX), 2.0, 1.0)
    wz = jnp.where(rid >= 2 * SIX, 2.0, 1.0)
    lane1 = lax.broadcasted_iota(jnp.int32, (1, NZ), 1)
    em = [[ec[p * NY + y : p * NY + y + 1, :] for y in range(NY)] for p in range(10)]
    zero = jnp.zeros((1, NZ), F32)

    def inside(p, y, val):
        return val if 3 <= p <= 6 else jnp.where(em[p][y] > 0.0, val, 0.0)

    for y in range(NY):
        for p in range(3):
            lo = rows(low, p * SLAB, y)
            hi = rows(high, p * SLAB, y)
            if p == 2:
                lo = lo + rows(q.at[0], 2 * SLAB, y)
            if p == 0:
                hi = hi + rows(q.at[QUAD - 1], SLAB, y)
            w0[p * NY + y] = inside(p, y, lo)
            w0[(7 + p) * NY + y] = inside(7 + p, y, hi)
        for s in range(QUAD):
            r = rows(own.at[s], 0, y)
            if s == 0:
                r = r + rows(low, 3 * SLAB, y)
            if s == QUAD - 1:
                r = r + rows(high, 3 * SLAB, y)
            w0[(3 + s) * NY + y] = r
            v0[s * NY + y] = r

    def face(p, y):
        e = em[p][y]
        xu, xd = faces(e, em[p + 1][y]), faces(e, em[p - 1][y])
        yu = faces(e, em[p][y + 1] if y + 1 < NY else zero)
        yd = faces(e, em[p][y - 1] if y > 0 else zero)
        zu = faces(e, jnp.where(lane1 == NZ - 1, 0.0, pltpu.roll(e, NZ - 1, 1)))
        zd = faces(e, jnp.where(lane1 == 0, 0.0, pltpu.roll(e, 1, 1)))
        return xu, xd, yu, yd, zu, zd

    coef = {}
    for p in range(1, 9):
        for y in range(NY):
            xu, xd, yu, yd, zu, zd = face(p, y)
            dg[p * NY + y] = wx * (xu + xd) + wy * (yu + yd) + wz * (zu + zd) - SHIFT
            coef[p, y] = (
                xu, xd, yu, yd,
                jnp.where(lane1 == NZ - 1, 0.0, zu),
                jnp.where(lane1 == 0, 0.0, zd),
            )

    def apply(src, p, y):
        xu, xd, yu, yd, zu, zd = coef[p, y]
        m = src[p * NY + y]
        t = dg[p * NY + y] * m
        t = t - wx * (xu * src[(p + 1) * NY + y] + xd * src[(p - 1) * NY + y])
        side = None
        if y + 1 < NY:
            side = yu * src[p * NY + y + 1]
        if y > 0:
            less = yd * src[p * NY + y - 1]
            side = less if side is None else side + less
        t = t - wy * side
        t = t - wz * (zu * pltpu.roll(m, NZ - 1, 1) + zd * pltpu.roll(m, 1, 1))
        return inside(p, y, t)

    for p in range(1, 9):
        for y in range(NY):
            t = apply(w0, p, y)
            w1[p * NY + y] = t
            if 3 <= p <= 6:
                v1[(p - 3) * NY + y] = t
    for p in range(2, 8):
        for y in range(NY):
            t = apply(w1, p, y)
            w2[p * NY + y] = t
            if 3 <= p <= 6:
                v2[(p - 3) * NY + y] = t
    sums = [None] * 6
    for p in range(3, 7):
        for y in range(NY):
            a, b, d = w0[p * NY + y], w1[p * NY + y], w2[p * NY + y]
            t = apply(w2, p, y)
            v3[(p - 3) * NY + y] = t
            for j, val in enumerate((a * a, a * b, b * b, b * d, d * d, d * t)):
                sums[j] = val if sums[j] is None else sums[j] + val
    lane = lax.broadcasted_iota(jnp.int32, (ROWS, NZ), 1)
    spot = lane - 8 * (rid % SIX)
    packed = jnp.zeros((ROWS, NZ), F32)
    for j in range(6):
        packed = jnp.where(spot == j, jnp.sum(sums[j], axis=1, keepdims=True), packed)
    mom[...] = jnp.broadcast_to(jnp.sum(packed, axis=0, keepdims=True), mom.shape)


def step_coefficients(mom):
    def inner(a, b):
        total = None
        for i, s in enumerate(a):
            for j, t in enumerate(b):
                term = s * t * mom[i + j]
                total = term if total is None else total + term
        return total

    def image(a):
        q = [SHIFT * s for s in a] + [None]
        for i, s in enumerate(a):
            q[i + 1] = s if q[i + 1] is None else q[i + 1] + s
        return q

    one = jnp.ones_like(mom[0])
    x, r, p = [], [one], [one]
    rr = mom[0]
    for step in range(3):
        q = image(p)
        alpha = rr / inner(p, q)
        x = [x[i] + alpha * s if i < len(x) else alpha * s for i, s in enumerate(p)]
        r = [r[i] - alpha * s if i < len(r) else -alpha * s for i, s in enumerate(q)]
        if step < 2:
            new = inner(r, r)
            beta = new / rr
            p = [s + beta * p[i] if i < len(p) else s for i, s in enumerate(r)]
            rr = new
    return x, r


def update_kernel(first, *refs):
    if first:
        mom, v0, v1, v2, v3, out, rest = refs
    else:
        mom, half, v0, v1, v2, before, out = refs
        upper = half[...] > 0.0
    total = jnp.sum(mom[...], axis=0, keepdims=True)
    rid = lax.broadcasted_iota(jnp.int32, (ROWS, NZ), 0)
    lane = lax.broadcasted_iota(jnp.int32, (ROWS, NZ), 1)
    spot = lane - 8 * (rid % SIX)
    picked = [jnp.sum(jnp.where(spot == j, total, 0.0), axis=1, keepdims=True) for j in range(6)]
    x, r = step_coefficients(picked)
    x = [jnp.broadcast_to(s, (ROWS, NZ)) for s in x]
    r = [jnp.broadcast_to(s, (ROWS, NZ)) for s in r]
    for s in range(QUAD):
        for y in range(NY):
            at = s * NY + y
            rows = slice(y * ROWS, (y + 1) * ROWS)
            a, b, d = v0[at], v1[at], v2[at]
            change = x[0] * a + x[1] * b + x[2] * d
            if first:
                rest[s, rows, :] = r[0] * a + r[1] * b + r[2] * d + r[3] * v3[at]
            else:
                change = change + before[s, rows, :]
                for c in range(3):
                    at = c * SIX
                    pick = jnp.where(upper, change[at + TRI : at + SIX], change[at : at + TRI])
                    to = (y * 3 + c) * TRI
                    out[s, to : to + TRI, :] = pick
                continue
            out[s, rows, :] = change


def fan_kernel(blocks, field, out):
    for d in range(blocks):
        own = field[d]
        for x in range(NX):
            out[x * blocks + d] = own


def packed(field):
    return field.transpose(0, 3, 2, 1, 4).reshape(1, 2 * NY * 3 * NM, NZ)


def by_target(field):
    field = field.reshape(2, QUAD, TRI, 3, NY, NZ)
    return field.transpose(4, 3, 1, 0, 2, 5).reshape(NY * 3 * NT, NZ)


def rows_of(table, x):
    table = lax.dynamic_index_in_dim(table.reshape(2, NX, QUAD, TRI, -1), x, 1, keepdims=False)
    return table.transpose(1, 0, 2, 3).reshape(NT, -1)


def shards(load_modes, first_guess, kl_fields, region_labels, partner, variable, weight):
    swap = [(0, 1), (1, 0)]
    zh, x = lax.axis_index("zh"), lax.axis_index("x")
    lower = zh == 0

    def halves(mine, far):
        both = jnp.stack([jnp.where(lower, mine, far), jnp.where(lower, far, mine)])
        return both.reshape(2, NM, 3, NY, NZ)

    far = lax.ppermute(first_guess, "zh", swap)
    load = by_target(halves(load_modes, lax.ppermute(load_modes, "zh", swap)))
    guess = packed(halves(first_guess, far))
    fan = functools.partial(fan_kernel, 1)
    (copies,) = call(fan, [(NX,) + guess.shape[1:]])(guess)
    copies, kl_fields, region_labels, partner, variable, weight = lax.optimization_barrier(
        (copies, kl_fields, region_labels, partner, variable, weight)
    )
    mean = jnp.where(region_labels == 0, 1.3, jnp.where(region_labels == 1, 1.0, 0.6)).astype(F32)
    varying = jnp.where(region_labels[None] == 1, kl_fields, 0.0)
    e0 = jnp.concatenate([varying, mean[None]], 0).reshape((NK + 1) * NY, NZ)
    em = lax.ppermute(e0, SLABS, line(16, 1))
    ep = lax.ppermute(e0, SLABS, line(16, -1))
    half = jnp.broadcast_to(zh.astype(F32), (TRI, NZ))

    own = rows_of(jnp.arange(MODES, dtype=jnp.int32), x)
    rows_partner = jnp.concatenate([rows_of(partner, x), own], 1)
    rows_variable = rows_of(variable, x)
    rows_weight = jnp.concatenate([rows_of(weight, x), jnp.ones((NT, 1), F32)], 1)
    links = (rows_partner, rows_variable, rows_weight)

    chunk, cells = (QUAD, SLAB, NZ), (QUAD * NY, ROWS, NZ)
    for sweep in range(2):
        first = sweep == 0
        nk = NK + 1 if first else NK
        if not first:
            fan = functools.partial(fan_kernel, QUAD)
            (copies,) = call(fan, [(NX * QUAD,) + change.shape[1:]])(change)
        u = lax.all_to_all(copies, ("x",) if first else ("x",) + WITHIN, 0, 0, tiled=True)
        fields = (u, load, e0, em, ep) if first else (u, e0, em, ep)
        face_rows = ((NK + 1) * NY, NZ)
        (sent,) = call(
            functools.partial(coupling_kernel, nk),
            [(QUAD, SENT, NZ)],
            [
                (NY * 3, MODES, NZ),
                (NY * 3, nk * NT, NZ),
                (2,) + face_rows,
                (2,) + face_rows,
                (5,) + face_rows,
            ],
        )(*fields, *links)
        q = lax.all_to_all(sent, WITHIN, 0, 0, tiled=True)
        edge = (4 * SLAB + 16 if first else 4 * SLAB, NZ)
        chunk_r, up, down = call(functools.partial(edges_kernel, first), [chunk, edge, edge])(
            *((q,) if first else (q, rest))
        )
        low = lax.ppermute(up, CHAIN, line(4, 1))
        high = lax.ppermute(down, CHAIN, line(4, -1))
        scratch = [(10 * NY, ROWS, NZ)] * 4
        outs = [cells] * 4 + [(16, NZ)]
        if first:
            v0, v1, v2, v3, mom, ec = call(
                functools.partial(powers_kernel, True), outs + [(10 * NY, NZ)], scratch
            )(q, chunk_r, low, high)
        else:
            v0, v1, v2, v3, mom = call(functools.partial(powers_kernel, False), outs, scratch)(
                q, chunk_r, low, high, ec
            )
        mom = lax.all_to_all(mom, CHUNKS, 0, 0, tiled=True)
        if first:
            change, rest = call(functools.partial(update_kernel, True), [chunk, chunk])(
                mom, v0, v1, v2, v3
            )
        else:
            (total,) = call(
                functools.partial(update_kernel, False), [(QUAD, NY * 3 * TRI, NZ)]
            )(mom, half, v0, v1, v2, change)
    total = lax.all_to_all(total, WITHIN, 0, 0, tiled=True)
    total = total.reshape(QUAD, NY, 3, TRI, NZ).transpose(0, 3, 2, 1, 4)
    return first_guess + total.reshape(NM, 3, 1, NY, NZ)


def solution(mesh):
    split = Mesh(mesh.devices.reshape(2, 4, 4, 4, 2, 2), AXES)
    mode, space = ("zh", "x"), ("y", "zp", "zq", "c")
    return jax.shard_map(
        shards,
        mesh=split,
        in_specs=(
            P(mode, None, space, None, None),
            P(mode, None, space, None, None),
            P(None, space, None, None),
            P(space, None, None),
            P(),
            P(),
            P(),
        ),
        out_specs=P(mode, None, space, None, None),
        check_vma=False,
    )
```

```python
import functools

import jax
import jax.numpy as jnp
from jax import lax
from jax.experimental import pallas as pl
from jax.experimental.pallas import tpu as pltpu
from jax.sharding import Mesh
from jax.sharding import PartitionSpec as P

AXES = ("zh", "x", "y", "zp", "zq", "c")
SLABS = ("zh", "y", "zp", "zq", "c")
CHAIN = ("zh", "y", "zp")
CHUNKS = ("y", "zp")
WITHIN = ("zq", "c")
NX, NM, NT, NL, NK = 4, 12, 24, 8, 8
MODES = 2 * NX * NM
NY, NZ, SHIFT = 4, 128, 4.0
QUAD = 4
TRI = NM // QUAD
SIX = 2 * TRI
ROWS = 3 * SIX
SLAB = NY * ROWS
SENT = 3 * SLAB + 8
F32 = jnp.float32


def line(inner, step):
    count = 4 * inner
    pairs = []
    for zh in range(2):
        for i in range(count):
            j = i + step
            if 0 <= j < count:
                other = zh ^ (i // inner != j // inner)
                pairs.append((zh * count + i, other * count + j))
    return pairs


def call(kernel, outs, scratch=()):
    vmem = pl.BlockSpec(memory_space=pltpu.VMEM)

    def run(*args):
        return pl.pallas_call(
            kernel,
            out_shape=[pltpu.VMEM(s, F32) for s in outs],
            in_specs=[vmem] * len(args),
            out_specs=[vmem] * len(outs),
            scratch_shapes=[pltpu.VMEM(s, F32) for s in scratch],
        )(*[pltpu.with_memory_space_constraint(a, pltpu.VMEM) for a in args])

    return run


def faces(e, other):
    return 0.5 * (e + other)


def coupling_kernel(nk, *refs):
    first = nk > NK
    if first:
        (u, load, e0, em, ep, partner, variable, weight, out, us, mx, fx, fy, fz) = refs
    else:
        (u, e0, em, ep, partner, variable, weight, out, us, mx, fx, fy, fz) = refs

    def lanes(yc):
        return slice(yc % 2 * NZ, (yc % 2 + 1) * NZ)

    def mixed(y, c, rows):
        yc = y * 3 + c
        return mx[yc // 2, rows, lanes(yc)]

    for g in range(2 * NX):
        half, x = divmod(g, NX)
        for y in range(NY):
            for c in range(3):
                yc = y * 3 + c
                if first:
                    at = (half * NY * 3 + yc) * NM
                    us[yc // 2, g * NM : (g + 1) * NM, lanes(yc)] = u[x, at : at + NM, :]
                    continue
                for d in range(QUAD):
                    at, to = y * ROWS + c * SIX + half * TRI, g * NM + d * TRI
                    us[yc // 2, to : to + TRI, lanes(yc)] = u[x * QUAD + d, at : at + TRI, :]
    lane = lax.broadcasted_iota(jnp.int32, (NT, MODES), 1)
    pr, vr, wr = partner[...], variable[...], weight[...]
    links = NL + 1 if first else NL
    hit = [jnp.where(lane == pr[:, l : l + 1], wr[:, l : l + 1], 0.0) for l in range(links)]
    blocks = []
    for k in range(nk):
        acc = None
        for l in range(links):
            if (k == NK) != (l == NL):
                continue
            term = hit[l] if l == NL else jnp.where(vr[:, l : l + 1] == k, hit[l], 0.0)
            acc = term if acc is None else acc + term
        blocks.append(acc)
    mix = jnp.concatenate(blocks, axis=0)
    for pair in range(NY * 3 // 2):
        mx[pair] = lax.dot_general(
            mix,
            us[pair],
            (((1,), (0,)), ((), ())),
            precision=lax.Precision.HIGHEST,
            preferred_element_type=F32,
        )
    e = e0[...]
    zlane = lax.broadcasted_iota(jnp.int32, e.shape, 1)
    row = lax.broadcasted_iota(jnp.int32, e.shape, 0)
    zup = jnp.where(zlane == NZ - 1, 0.0, pltpu.roll(e, NZ - 1, 1))
    zdn = jnp.where(zlane == 0, 0.0, pltpu.roll(e, 1, 1))
    count = e.shape[0]
    yup = jnp.where(row % NY == NY - 1, 0.0, pltpu.roll(e, count - 1, 0))
    ydn = jnp.where(row % NY == 0, 0.0, pltpu.roll(e, 1, 0))
    fx[0] = faces(e, ep[...])
    fx[1] = faces(e, em[...])
    fy[0] = faces(e, yup)
    fy[1] = faces(e, ydn)
    fzu, fzd = faces(e, zup), faces(e, zdn)
    base = fx[0] + fx[1] + fy[0] + fy[1] + fzu + fzd
    fz[0] = jnp.where(zlane == NZ - 1, 0.0, fzu)
    fz[1] = jnp.where(zlane == 0, 0.0, fzd)
    fz[2] = base + fx[0] + fx[1]
    fz[3] = base + fy[0] + fy[1]
    fz[4] = base + fzu + fzd
    for y in range(NY):
        for c in range(3):
            own = up = down = None
            for k in range(nk):
                r = slice(k * NY + y, k * NY + y + 1)
                rows = slice(k * NT, (k + 1) * NT)
                m = mixed(y, c, rows)
                t = fz[2 + c, r, :] * m
                side = None
                if y + 1 < NY:
                    side = fy[0, r, :] * mixed(y + 1, c, rows)
                if y > 0:
                    less = fy[1, r, :] * mixed(y - 1, c, rows)
                    side = less if side is None else side + less
                t = t - (2.0 * side if c == 1 else side)
                side = fz[0, r, :] * pltpu.roll(m, NZ - 1, 1) + fz[1, r, :] * pltpu.roll(m, 1, 1)
                t = t - (2.0 * side if c == 2 else side)
                p, q = fx[0, r, :] * m, fx[1, r, :] * m
                own, up, down = (t, p, q) if own is None else (own + t, up + p, down + q)
            if c == 0:
                up, down = 2.0 * up, 2.0 * down
            yc = y * 3 + c
            own = load[yc * NT : (yc + 1) * NT, :] - own if first else -own
            for kind, val in enumerate((own, up, down)):
                at = (kind * NY + y) * ROWS + c * SIX
                for d in range(QUAD):
                    out[d, at : at + SIX, :] = val[d * SIX : (d + 1) * SIX]
    zeros = jnp.zeros((NY, NZ), F32)
    tail = jnp.concatenate([e[NK * NY : NK * NY + NY] if first else zeros, zeros], axis=0)
    for d in range(QUAD):
        out[d, 3 * SLAB : SENT, :] = tail


def edges_kernel(first, *refs):
    if first:
        q, own, up, down = refs
    else:
        q, rest, own, up, down = refs
    rs = []
    for s in range(QUAD):
        r = q[s, 0:SLAB, :]
        if not first:
            r = r + rest[s]
        if s > 0:
            r = r + q[s - 1, SLAB : 2 * SLAB, :]
        if s + 1 < QUAD:
            r = r + q[s + 1, 2 * SLAB : 3 * SLAB, :]
        own[s] = r
        rs.append(r)
    for j in range(3):
        up[j * SLAB : (j + 1) * SLAB, :] = rs[j + 1]
        down[j * SLAB : (j + 1) * SLAB, :] = rs[j]
    up[3 * SLAB : 4 * SLAB, :] = q[3, SLAB : 2 * SLAB, :]
    down[3 * SLAB : 4 * SLAB, :] = q[0, 2 * SLAB : 3 * SLAB, :]
    if first:
        for j in range(3):
            at = 4 * SLAB + j * NY
            up[at : at + NY, :] = q[j + 1, 3 * SLAB : 3 * SLAB + NY, :]
            down[at : at + NY, :] = q[j, 3 * SLAB : 3 * SLAB + NY, :]
        up[4 * SLAB + 12 :, :] = jnp.zeros((4, NZ), F32)
        down[4 * SLAB + 12 :, :] = jnp.zeros((4, NZ), F32)


def powers_kernel(first, *refs):
    if first:
        q, own, low, high, v0, v1, v2, v3, mom, ec, w0, w1, w2, dg = refs
        for j in range(3):
            at = 4 * SLAB + j * NY
            ec[j * NY : (j + 1) * NY, :] = low[at : at + NY, :]
            ec[(7 + j) * NY : (8 + j) * NY, :] = high[at : at + NY, :]
        for s in range(QUAD):
            ec[(3 + s) * NY : (4 + s) * NY, :] = q[s, 3 * SLAB : 3 * SLAB + NY, :]
    else:
        q, own, low, high, ec, v0, v1, v2, v3, mom, w0, w1, w2, dg = refs

    def rows(ref, at, y):
        return ref[at + y * ROWS : at + (y + 1) * ROWS, :]

    rid = lax.broadcasted_iota(jnp.int32, (ROWS, NZ), 0)
    wx = jnp.where(rid < SIX, 2.0, 1.0)
    wy = jnp.where((rid >= SIX) & (rid < 2 * SIX), 2.0, 1.0)
    wz = jnp.where(rid >= 2 * SIX, 2.0, 1.0)
    lane1 = lax.broadcasted_iota(jnp.int32, (1, NZ), 1)
    em = [[ec[p * NY + y : p * NY + y + 1, :] for y in range(NY)] for p in range(10)]
    zero = jnp.zeros((1, NZ), F32)

    def inside(p, y, val):
        return val if 3 <= p <= 6 else jnp.where(em[p][y] > 0.0, val, 0.0)

    for y in range(NY):
        for p in range(3):
            lo = rows(low, p * SLAB, y)
            hi = rows(high, p * SLAB, y)
            if p == 2:
                lo = lo + rows(q.at[0], 2 * SLAB, y)
            if p == 0:
                hi = hi + rows(q.at[QUAD - 1], SLAB, y)
            w0[p * NY + y] = inside(p, y, lo)
            w0[(7 + p) * NY + y] = inside(7 + p, y, hi)
        for s in range(QUAD):
            r = rows(own.at[s], 0, y)
            if s == 0:
                r = r + rows(low, 3 * SLAB, y)
            if s == QUAD - 1:
                r = r + rows(high, 3 * SLAB, y)
            w0[(3 + s) * NY + y] = r
            v0[s * NY + y] = r

    def face(p, y):
        e = em[p][y]
        xu, xd = faces(e, em[p + 1][y]), faces(e, em[p - 1][y])
        yu = faces(e, em[p][y + 1] if y + 1 < NY else zero)
        yd = faces(e, em[p][y - 1] if y > 0 else zero)
        zu = faces(e, jnp.where(lane1 == NZ - 1, 0.0, pltpu.roll(e, NZ - 1, 1)))
        zd = faces(e, jnp.where(lane1 == 0, 0.0, pltpu.roll(e, 1, 1)))
        return xu, xd, yu, yd, zu, zd

    coef = {}
    for p in range(1, 9):
        for y in range(NY):
            xu, xd, yu, yd, zu, zd = face(p, y)
            dg[p * NY + y] = wx * (xu + xd) + wy * (yu + yd) + wz * (zu + zd) - SHIFT
            coef[p, y] = (
                xu, xd, yu, yd,
                jnp.where(lane1 == NZ - 1, 0.0, zu),
                jnp.where(lane1 == 0, 0.0, zd),
            )

    def apply(src, p, y):
        xu, xd, yu, yd, zu, zd = coef[p, y]
        m = src[p * NY + y]
        t = dg[p * NY + y] * m
        t = t - wx * (xu * src[(p + 1) * NY + y] + xd * src[(p - 1) * NY + y])
        side = None
        if y + 1 < NY:
            side = yu * src[p * NY + y + 1]
        if y > 0:
            less = yd * src[p * NY + y - 1]
            side = less if side is None else side + less
        t = t - wy * side
        t = t - wz * (zu * pltpu.roll(m, NZ - 1, 1) + zd * pltpu.roll(m, 1, 1))
        return inside(p, y, t)

    for p in range(1, 9):
        for y in range(NY):
            t = apply(w0, p, y)
            w1[p * NY + y] = t
            if 3 <= p <= 6:
                v1[(p - 3) * NY + y] = t
    for p in range(2, 8):
        for y in range(NY):
            t = apply(w1, p, y)
            w2[p * NY + y] = t
            if 3 <= p <= 6:
                v2[(p - 3) * NY + y] = t
    sums = [None] * 6
    for p in range(3, 7):
        for y in range(NY):
            a, b, d = w0[p * NY + y], w1[p * NY + y], w2[p * NY + y]
            t = apply(w2, p, y)
            v3[(p - 3) * NY + y] = t
            for j, val in enumerate((a * a, a * b, b * b, b * d, d * d, d * t)):
                sums[j] = val if sums[j] is None else sums[j] + val
    lane = lax.broadcasted_iota(jnp.int32, (ROWS, NZ), 1)
    spot = lane - 8 * (rid % SIX)
    packed = jnp.zeros((ROWS, NZ), F32)
    for j in range(6):
        packed = jnp.where(spot == j, jnp.sum(sums[j], axis=1, keepdims=True), packed)
    mom[...] = jnp.broadcast_to(jnp.sum(packed, axis=0, keepdims=True), mom.shape)


def step_coefficients(mom):
    def inner(a, b):
        total = None
        for i, s in enumerate(a):
            for j, t in enumerate(b):
                term = s * t * mom[i + j]
                total = term if total is None else total + term
        return total

    def image(a):
        q = [SHIFT * s for s in a] + [None]
        for i, s in enumerate(a):
            q[i + 1] = s if q[i + 1] is None else q[i + 1] + s
        return q

    one = jnp.ones_like(mom[0])
    x, r, p = [], [one], [one]
    rr = mom[0]
    for step in range(3):
        q = image(p)
        alpha = rr / inner(p, q)
        x = [x[i] + alpha * s if i < len(x) else alpha * s for i, s in enumerate(p)]
        r = [r[i] - alpha * s if i < len(r) else -alpha * s for i, s in enumerate(q)]
        if step < 2:
            new = inner(r, r)
            beta = new / rr
            p = [s + beta * p[i] if i < len(p) else s for i, s in enumerate(r)]
            rr = new
    return x, r


def update_kernel(first, *refs):
    if first:
        mom, v0, v1, v2, v3, out, rest = refs
    else:
        mom, half, v0, v1, v2, before, out = refs
        upper = half[...] > 0.0
    total = jnp.sum(mom[...], axis=0, keepdims=True)
    rid = lax.broadcasted_iota(jnp.int32, (ROWS, NZ), 0)
    lane = lax.broadcasted_iota(jnp.int32, (ROWS, NZ), 1)
    spot = lane - 8 * (rid % SIX)
    picked = [jnp.sum(jnp.where(spot == j, total, 0.0), axis=1, keepdims=True) for j in range(6)]
    x, r = step_coefficients(picked)
    x = [jnp.broadcast_to(s, (ROWS, NZ)) for s in x]
    r = [jnp.broadcast_to(s, (ROWS, NZ)) for s in r]
    for s in range(QUAD):
        for y in range(NY):
            at = s * NY + y
            rows = slice(y * ROWS, (y + 1) * ROWS)
            a, b, d = v0[at], v1[at], v2[at]
            change = x[0] * a + x[1] * b + x[2] * d
            if first:
                rest[s, rows, :] = r[0] * a + r[1] * b + r[2] * d + r[3] * v3[at]
            else:
                change = change + before[s, rows, :]
                for c in range(3):
                    at = c * SIX
                    pick = jnp.where(upper, change[at + TRI : at + SIX], change[at : at + TRI])
                    to = (y * 3 + c) * TRI
                    out[s, to : to + TRI, :] = pick
                continue
            out[s, rows, :] = change


def fan_kernel(blocks, field, out):
    for d in range(blocks):
        own = field[d]
        for x in range(NX):
            out[x * blocks + d] = own


def packed(field):
    return field.transpose(0, 3, 2, 1, 4).reshape(1, 2 * NY * 3 * NM, NZ)


def by_target(field):
    field = field.reshape(2, QUAD, TRI, 3, NY, NZ)
    return field.transpose(4, 3, 1, 0, 2, 5).reshape(NY * 3 * NT, NZ)


def rows_of(table, x):
    table = lax.dynamic_index_in_dim(table.reshape(2, NX, QUAD, TRI, -1), x, 1, keepdims=False)
    return table.transpose(1, 0, 2, 3).reshape(NT, -1)


def shards(load_modes, first_guess, kl_fields, region_labels, partner, variable, weight):
    mean = jnp.where(region_labels == 0, 1.3, jnp.where(region_labels == 1, 1.0, 0.6)).astype(F32)
    varying = jnp.where(region_labels[None] == 1, kl_fields, 0.0)
    moduli = jnp.concatenate([varying, mean[None]], 0).reshape((NK + 1) * NY, NZ)
    em = lax.ppermute(moduli, SLABS, line(16, 1))
    ep = lax.ppermute(moduli, SLABS, line(16, -1))
    e0 = moduli
    mine = lax.optimization_barrier(jnp.concatenate([first_guess, load_modes], 0))
    far = lax.ppermute(mine, "zh", [(0, 1), (1, 0)])
    zh, x = lax.axis_index("zh"), lax.axis_index("x")
    lower = zh == 0
    both = jnp.stack([jnp.where(lower, mine, far), jnp.where(lower, far, mine)])
    both = both.reshape(2, 2, NM, 3, NY, NZ)
    guess, load = packed(both[:, 0]), by_target(both[:, 1])
    half = jnp.broadcast_to(zh.astype(F32), (TRI, NZ))

    own = rows_of(jnp.arange(MODES, dtype=jnp.int32), x)
    rows_partner = jnp.concatenate([rows_of(partner, x), own], 1)
    rows_variable = rows_of(variable, x)
    rows_weight = jnp.concatenate([rows_of(weight, x), jnp.ones((NT, 1), F32)], 1)
    links = (rows_partner, rows_variable, rows_weight)

    chunk, cells = (QUAD, SLAB, NZ), (QUAD * NY, ROWS, NZ)
    for sweep in range(2):
        first = sweep == 0
        nk = NK + 1 if first else NK
        blocks = 1 if first else QUAD
        field = guess if first else change
        (copies,) = call(
            functools.partial(fan_kernel, blocks), [(NX * blocks,) + field.shape[1:]]
        )(field)
        u = lax.all_to_all(copies, ("x",) if first else ("x",) + WITHIN, 0, 0, tiled=True)
        fields = (u, load, e0, em, ep) if first else (u, e0, em, ep)
        face_rows = ((NK + 1) * NY, NZ)
        (sent,) = call(
            functools.partial(coupling_kernel, nk),
            [(QUAD, SENT, NZ)],
            [
                (NY * 3 // 2, MODES, 2 * NZ),
                (NY * 3 // 2, nk * NT, 2 * NZ),
                (2,) + face_rows,
                (2,) + face_rows,
                (5,) + face_rows,
            ],
        )(*fields, *links)
        q = lax.all_to_all(sent, WITHIN, 0, 0, tiled=True)
        edge = (4 * SLAB + 16 if first else 4 * SLAB, NZ)
        chunk_r, up, down = call(functools.partial(edges_kernel, first), [chunk, edge, edge])(
            *((q,) if first else (q, rest))
        )
        low = lax.ppermute(up, CHAIN, line(4, 1))
        high = lax.ppermute(down, CHAIN, line(4, -1))
        scratch = [(10 * NY, ROWS, NZ)] * 4
        outs = [cells] * 4 + [(16, NZ)]
        if first:
            v0, v1, v2, v3, mom, ec = call(
                functools.partial(powers_kernel, True), outs + [(10 * NY, NZ)], scratch
            )(q, chunk_r, low, high)
        else:
            v0, v1, v2, v3, mom = call(functools.partial(powers_kernel, False), outs, scratch)(
                q, chunk_r, low, high, ec
            )
        mom = lax.all_to_all(mom, CHUNKS, 0, 0, tiled=True)
        if first:
            change, rest = call(functools.partial(update_kernel, True), [chunk, chunk])(
                mom, v0, v1, v2, v3
            )
        else:
            (total,) = call(
                functools.partial(update_kernel, False), [(QUAD, NY * 3 * TRI, NZ)]
            )(mom, half, v0, v1, v2, change)
    total = lax.all_to_all(total, WITHIN, 0, 0, tiled=True)
    total = total.reshape(QUAD, NY, 3, TRI, NZ).transpose(0, 3, 2, 1, 4)
    return mine[:NM] + total.reshape(NM, 3, 1, NY, NZ)


def solution(mesh):
    split = Mesh(mesh.devices.reshape(2, 4, 4, 4, 2, 2), AXES)
    mode, space = ("zh", "x"), ("y", "zp", "zq", "c")
    return jax.shard_map(
        shards,
        mesh=split,
        in_specs=(
            P(mode, None, space, None, None),
            P(mode, None, space, None, None),
            P(None, space, None, None),
            P(space, None, None),
            P(),
            P(),
            P(),
        ),
        out_specs=P(mode, None, space, None, None),
        check_vma=False,
    )
```

```python
import functools

import jax
import jax.numpy as jnp
from jax import lax
from jax.experimental import pallas as pl
from jax.experimental.pallas import tpu as pltpu
from jax.sharding import Mesh
from jax.sharding import PartitionSpec as P

AXES = ("zh", "x", "y", "zp", "zq", "c")
SLABS = ("zh", "y", "zp", "zq", "c")
CHAIN = ("zh", "y", "zp")
CHUNKS = ("y", "zp")
WITHIN = ("zq", "c")
NX, NM, NT, NL, NK = 4, 12, 24, 8, 8
MODES = 2 * NX * NM
NY, NZ, SHIFT = 4, 128, 4.0
QUAD = 4
TRI = NM // QUAD
SIX = 2 * TRI
ROWS = 3 * SIX
SLAB = NY * ROWS
SENT = 3 * SLAB + 8
F32 = jnp.float32


def line(inner, step):
    count = 4 * inner
    pairs = []
    for zh in range(2):
        for i in range(count):
            j = i + step
            if 0 <= j < count:
                other = zh ^ (i // inner != j // inner)
                pairs.append((zh * count + i, other * count + j))
    return pairs


def call(kernel, outs, scratch=()):
    vmem = pl.BlockSpec(memory_space=pltpu.VMEM)

    def run(*args):
        return pl.pallas_call(
            kernel,
            out_shape=[pltpu.VMEM(s, F32) for s in outs],
            in_specs=[vmem] * len(args),
            out_specs=[vmem] * len(outs),
            scratch_shapes=[pltpu.VMEM(s, F32) for s in scratch],
        )(*[pltpu.with_memory_space_constraint(a, pltpu.VMEM) for a in args])

    return run


def faces(e, other):
    return 0.5 * (e + other)


def coupling_kernel(nk, *refs):
    first = nk > NK
    if first:
        (u, load, e0, em, ep, partner, variable, weight, out, us, mx, fx, fy, fz) = refs
    else:
        (u, e0, em, ep, partner, variable, weight, out, us, mx, fx, fy, fz) = refs

    def lanes(yc):
        return slice(yc % 2 * NZ, (yc % 2 + 1) * NZ)

    def mixed(y, c, rows):
        yc = y * 3 + c
        return mx[yc // 2, rows, lanes(yc)]

    for g in range(2 * NX):
        half, x = divmod(g, NX)
        for y in range(NY):
            for c in range(3):
                yc = y * 3 + c
                if first:
                    at = (half * NY * 3 + yc) * NM
                    us[yc // 2, g * NM : (g + 1) * NM, lanes(yc)] = u[x, at : at + NM, :]
                    continue
                for d in range(QUAD):
                    at, to = y * ROWS + c * SIX + half * TRI, g * NM + d * TRI
                    us[yc // 2, to : to + TRI, lanes(yc)] = u[x * QUAD + d, at : at + TRI, :]
    lane = lax.broadcasted_iota(jnp.int32, (NT, MODES), 1)
    pr, vr, wr = partner[...], variable[...], weight[...]
    links = NL + 1 if first else NL
    hit = [jnp.where(lane == pr[:, l : l + 1], wr[:, l : l + 1], 0.0) for l in range(links)]
    blocks = []
    for k in range(nk):
        acc = None
        for l in range(links):
            if (k == NK) != (l == NL):
                continue
            term = hit[l] if l == NL else jnp.where(vr[:, l : l + 1] == k, hit[l], 0.0)
            acc = term if acc is None else acc + term
        blocks.append(acc)
    mix = jnp.concatenate(blocks, axis=0)
    for pair in range(NY * 3 // 2):
        mx[pair] = lax.dot_general(
            mix,
            us[pair],
            (((1,), (0,)), ((), ())),
            precision=lax.Precision.HIGHEST,
            preferred_element_type=F32,
        )
    e = e0[...]
    zlane = lax.broadcasted_iota(jnp.int32, e.shape, 1)
    row = lax.broadcasted_iota(jnp.int32, e.shape, 0)
    zup = jnp.where(zlane == NZ - 1, 0.0, pltpu.roll(e, NZ - 1, 1))
    zdn = jnp.where(zlane == 0, 0.0, pltpu.roll(e, 1, 1))
    count = e.shape[0]
    yup = jnp.where(row % NY == NY - 1, 0.0, pltpu.roll(e, count - 1, 0))
    ydn = jnp.where(row % NY == 0, 0.0, pltpu.roll(e, 1, 0))
    fx[0] = faces(e, ep[...])
    fx[1] = faces(e, em[...])
    fy[0] = faces(e, yup)
    fy[1] = faces(e, ydn)
    fzu, fzd = faces(e, zup), faces(e, zdn)
    base = fx[0] + fx[1] + fy[0] + fy[1] + fzu + fzd
    fz[0] = jnp.where(zlane == NZ - 1, 0.0, fzu)
    fz[1] = jnp.where(zlane == 0, 0.0, fzd)
    fz[2] = base + fx[0] + fx[1]
    fz[3] = base + fy[0] + fy[1]
    fz[4] = base + fzu + fzd
    for y in range(NY):
        for c in range(3):
            own = up = down = None
            for k in range(nk):
                r = slice(k * NY + y, k * NY + y + 1)
                rows = slice(k * NT, (k + 1) * NT)
                m = mixed(y, c, rows)
                t = fz[2 + c, r, :] * m
                side = None
                if y + 1 < NY:
                    side = fy[0, r, :] * mixed(y + 1, c, rows)
                if y > 0:
                    less = fy[1, r, :] * mixed(y - 1, c, rows)
                    side = less if side is None else side + less
                t = t - (2.0 * side if c == 1 else side)
                side = fz[0, r, :] * pltpu.roll(m, NZ - 1, 1) + fz[1, r, :] * pltpu.roll(m, 1, 1)
                t = t - (2.0 * side if c == 2 else side)
                p, q = fx[0, r, :] * m, fx[1, r, :] * m
                own, up, down = (t, p, q) if own is None else (own + t, up + p, down + q)
            if c == 0:
                up, down = 2.0 * up, 2.0 * down
            yc = y * 3 + c
            own = load[yc * NT : (yc + 1) * NT, :] - own if first else -own
            for kind, val in enumerate((own, up, down)):
                at = (kind * NY + y) * ROWS + c * SIX
                for d in range(QUAD):
                    out[d, at : at + SIX, :] = val[d * SIX : (d + 1) * SIX]
    zeros = jnp.zeros((NY, NZ), F32)
    tail = jnp.concatenate([e[NK * NY : NK * NY + NY] if first else zeros, zeros], axis=0)
    for d in range(QUAD):
        out[d, 3 * SLAB : SENT, :] = tail


def edges_kernel(first, *refs):
    if first:
        q, own, up, down = refs
    else:
        q, rest, own, up, down = refs
    rs = []
    for s in range(QUAD):
        r = q[s, 0:SLAB, :]
        if not first:
            r = r + rest[s]
        if s > 0:
            r = r + q[s - 1, SLAB : 2 * SLAB, :]
        if s + 1 < QUAD:
            r = r + q[s + 1, 2 * SLAB : 3 * SLAB, :]
        own[s] = r
        rs.append(r)
    for j in range(3):
        up[j * SLAB : (j + 1) * SLAB, :] = rs[j + 1]
        down[j * SLAB : (j + 1) * SLAB, :] = rs[j]
    up[3 * SLAB : 4 * SLAB, :] = q[3, SLAB : 2 * SLAB, :]
    down[3 * SLAB : 4 * SLAB, :] = q[0, 2 * SLAB : 3 * SLAB, :]
    if first:
        for j in range(3):
            at = 4 * SLAB + j * NY
            up[at : at + NY, :] = q[j + 1, 3 * SLAB : 3 * SLAB + NY, :]
            down[at : at + NY, :] = q[j, 3 * SLAB : 3 * SLAB + NY, :]
        up[4 * SLAB + 12 :, :] = jnp.zeros((4, NZ), F32)
        down[4 * SLAB + 12 :, :] = jnp.zeros((4, NZ), F32)


def powers_kernel(first, *refs):
    if first:
        q, own, low, high, v0, v1, v2, v3, mom, ec, w0, w1, w2, dg = refs
        for j in range(3):
            at = 4 * SLAB + j * NY
            ec[j * NY : (j + 1) * NY, :] = low[at : at + NY, :]
            ec[(7 + j) * NY : (8 + j) * NY, :] = high[at : at + NY, :]
        for s in range(QUAD):
            ec[(3 + s) * NY : (4 + s) * NY, :] = q[s, 3 * SLAB : 3 * SLAB + NY, :]
    else:
        q, own, low, high, ec, v0, v1, v2, v3, mom, w0, w1, w2, dg = refs

    def rows(ref, at, y):
        return ref[at + y * ROWS : at + (y + 1) * ROWS, :]

    rid = lax.broadcasted_iota(jnp.int32, (ROWS, NZ), 0)
    wx = jnp.where(rid < SIX, 2.0, 1.0)
    wy = jnp.where((rid >= SIX) & (rid < 2 * SIX), 2.0, 1.0)
    wz = jnp.where(rid >= 2 * SIX, 2.0, 1.0)
    lane1 = lax.broadcasted_iota(jnp.int32, (1, NZ), 1)
    em = [[ec[p * NY + y : p * NY + y + 1, :] for y in range(NY)] for p in range(10)]
    zero = jnp.zeros((1, NZ), F32)

    def inside(p, y, val):
        return val if 3 <= p <= 6 else jnp.where(em[p][y] > 0.0, val, 0.0)

    for y in range(NY):
        for p in range(3):
            lo = rows(low, p * SLAB, y)
            hi = rows(high, p * SLAB, y)
            if p == 2:
                lo = lo + rows(q.at[0], 2 * SLAB, y)
            if p == 0:
                hi = hi + rows(q.at[QUAD - 1], SLAB, y)
            w0[p * NY + y] = inside(p, y, lo)
            w0[(7 + p) * NY + y] = inside(7 + p, y, hi)
        for s in range(QUAD):
            r = rows(own.at[s], 0, y)
            if s == 0:
                r = r + rows(low, 3 * SLAB, y)
            if s == QUAD - 1:
                r = r + rows(high, 3 * SLAB, y)
            w0[(3 + s) * NY + y] = r
            v0[s * NY + y] = r

    def face(p, y):
        e = em[p][y]
        xu, xd = faces(e, em[p + 1][y]), faces(e, em[p - 1][y])
        yu = faces(e, em[p][y + 1] if y + 1 < NY else zero)
        yd = faces(e, em[p][y - 1] if y > 0 else zero)
        zu = faces(e, jnp.where(lane1 == NZ - 1, 0.0, pltpu.roll(e, NZ - 1, 1)))
        zd = faces(e, jnp.where(lane1 == 0, 0.0, pltpu.roll(e, 1, 1)))
        return xu, xd, yu, yd, zu, zd

    coef = {}
    for p in range(1, 9):
        for y in range(NY):
            xu, xd, yu, yd, zu, zd = face(p, y)
            dg[p * NY + y] = wx * (xu + xd) + wy * (yu + yd) + wz * (zu + zd) - SHIFT
            coef[p, y] = (
                xu, xd, yu, yd,
                jnp.where(lane1 == NZ - 1, 0.0, zu),
                jnp.where(lane1 == 0, 0.0, zd),
            )

    def apply(src, p, y):
        xu, xd, yu, yd, zu, zd = coef[p, y]
        m = src[p * NY + y]
        t = dg[p * NY + y] * m
        t = t - wx * (xu * src[(p + 1) * NY + y] + xd * src[(p - 1) * NY + y])
        side = None
        if y + 1 < NY:
            side = yu * src[p * NY + y + 1]
        if y > 0:
            less = yd * src[p * NY + y - 1]
            side = less if side is None else side + less
        t = t - wy * side
        t = t - wz * (zu * pltpu.roll(m, NZ - 1, 1) + zd * pltpu.roll(m, 1, 1))
        return inside(p, y, t)

    for p in range(1, 9):
        for y in range(NY):
            t = apply(w0, p, y)
            w1[p * NY + y] = t
            if 3 <= p <= 6:
                v1[(p - 3) * NY + y] = t
    for p in range(2, 8):
        for y in range(NY):
            t = apply(w1, p, y)
            w2[p * NY + y] = t
            if 3 <= p <= 6:
                v2[(p - 3) * NY + y] = t
    sums = [None] * 6
    for p in range(3, 7):
        for y in range(NY):
            a, b, d = w0[p * NY + y], w1[p * NY + y], w2[p * NY + y]
            t = apply(w2, p, y)
            v3[(p - 3) * NY + y] = t
            for j, val in enumerate((a * a, a * b, b * b, b * d, d * d, d * t)):
                sums[j] = val if sums[j] is None else sums[j] + val
    lane = lax.broadcasted_iota(jnp.int32, (ROWS, NZ), 1)
    spot = lane - 8 * (rid % SIX)
    packed = jnp.zeros((ROWS, NZ), F32)
    for j in range(6):
        packed = jnp.where(spot == j, jnp.sum(sums[j], axis=1, keepdims=True), packed)
    mom[...] = jnp.broadcast_to(jnp.sum(packed, axis=0, keepdims=True), mom.shape)


def step_coefficients(mom):
    def inner(a, b):
        total = None
        for i, s in enumerate(a):
            for j, t in enumerate(b):
                term = s * t * mom[i + j]
                total = term if total is None else total + term
        return total

    def image(a):
        q = [SHIFT * s for s in a] + [None]
        for i, s in enumerate(a):
            q[i + 1] = s if q[i + 1] is None else q[i + 1] + s
        return q

    one = jnp.ones_like(mom[0])
    x, r, p = [], [one], [one]
    rr = mom[0]
    for step in range(3):
        q = image(p)
        alpha = rr / inner(p, q)
        x = [x[i] + alpha * s if i < len(x) else alpha * s for i, s in enumerate(p)]
        r = [r[i] - alpha * s if i < len(r) else -alpha * s for i, s in enumerate(q)]
        if step < 2:
            new = inner(r, r)
            beta = new / rr
            p = [s + beta * p[i] if i < len(p) else s for i, s in enumerate(r)]
            rr = new
    return x, r


def update_kernel(first, *refs):
    if first:
        mom, v0, v1, v2, v3, out, rest = refs
    else:
        mom, half, v0, v1, v2, before, out = refs
        upper = half[...] > 0.0
    total = jnp.sum(mom[...], axis=0, keepdims=True)
    rid = lax.broadcasted_iota(jnp.int32, (ROWS, NZ), 0)
    lane = lax.broadcasted_iota(jnp.int32, (ROWS, NZ), 1)
    spot = lane - 8 * (rid % SIX)
    picked = [jnp.sum(jnp.where(spot == j, total, 0.0), axis=1, keepdims=True) for j in range(6)]
    x, r = step_coefficients(picked)
    x = [jnp.broadcast_to(s, (ROWS, NZ)) for s in x]
    r = [jnp.broadcast_to(s, (ROWS, NZ)) for s in r]
    for s in range(QUAD):
        for y in range(NY):
            at = s * NY + y
            rows = slice(y * ROWS, (y + 1) * ROWS)
            a, b, d = v0[at], v1[at], v2[at]
            change = x[0] * a + x[1] * b + x[2] * d
            if first:
                rest[s, rows, :] = r[0] * a + r[1] * b + r[2] * d + r[3] * v3[at]
            else:
                change = change + before[s, rows, :]
                for c in range(3):
                    at = c * SIX
                    pick = jnp.where(upper, change[at + TRI : at + SIX], change[at : at + TRI])
                    to = (y * 3 + c) * TRI
                    out[s, to : to + TRI, :] = pick
                continue
            out[s, rows, :] = change


def fan_kernel(blocks, field, out):
    for d in range(blocks):
        own = field[d]
        for x in range(NX):
            out[x * blocks + d] = own


def packed(field):
    return field.transpose(0, 3, 2, 1, 4).reshape(1, 2 * NY * 3 * NM, NZ)


def by_target(field):
    field = field.reshape(2, QUAD, TRI, 3, NY, NZ)
    return field.transpose(4, 3, 1, 0, 2, 5).reshape(NY * 3 * NT, NZ)


def rows_of(table, x):
    table = lax.dynamic_index_in_dim(table.reshape(2, NX, QUAD, TRI, -1), x, 1, keepdims=False)
    return table.transpose(1, 0, 2, 3).reshape(NT, -1)


def shards(load_modes, first_guess, kl_fields, region_labels, partner, variable, weight):
    mean = jnp.where(region_labels == 0, 1.3, jnp.where(region_labels == 1, 1.0, 0.6)).astype(F32)
    varying = jnp.where(region_labels[None] == 1, kl_fields, 0.0)
    moduli = jnp.concatenate([varying, mean[None]], 0).reshape((NK + 1) * NY, NZ)
    em = lax.ppermute(moduli, SLABS, line(16, 1))
    ep = lax.ppermute(moduli, SLABS, line(16, -1))
    e0 = moduli
    mine = lax.optimization_barrier(jnp.concatenate([first_guess, load_modes], 0))
    zh, x = lax.axis_index("zh"), lax.axis_index("x")
    both = lax.all_to_all(jnp.stack([mine, mine]), "zh", 0, 0, tiled=True)
    both = both.reshape(2, 2, NM, 3, NY, NZ)
    guess, load = packed(both[:, 0]), by_target(both[:, 1])
    half = jnp.broadcast_to(zh.astype(F32), (TRI, NZ))

    own = rows_of(jnp.arange(MODES, dtype=jnp.int32), x)
    rows_partner = jnp.concatenate([rows_of(partner, x), own], 1)
    rows_variable = rows_of(variable, x)
    rows_weight = jnp.concatenate([rows_of(weight, x), jnp.ones((NT, 1), F32)], 1)
    links = (rows_partner, rows_variable, rows_weight)

    chunk, cells = (QUAD, SLAB, NZ), (QUAD * NY, ROWS, NZ)
    for sweep in range(2):
        first = sweep == 0
        nk = NK + 1 if first else NK
        blocks = 1 if first else QUAD
        field = guess if first else change
        (copies,) = call(
            functools.partial(fan_kernel, blocks), [(NX * blocks,) + field.shape[1:]]
        )(field)
        u = lax.all_to_all(copies, ("x",) if first else ("x",) + WITHIN, 0, 0, tiled=True)
        fields = (u, load, e0, em, ep) if first else (u, e0, em, ep)
        face_rows = ((NK + 1) * NY, NZ)
        (sent,) = call(
            functools.partial(coupling_kernel, nk),
            [(QUAD, SENT, NZ)],
            [
                (NY * 3 // 2, MODES, 2 * NZ),
                (NY * 3 // 2, nk * NT, 2 * NZ),
                (2,) + face_rows,
                (2,) + face_rows,
                (5,) + face_rows,
            ],
        )(*fields, *links)
        q = lax.all_to_all(sent, WITHIN, 0, 0, tiled=True)
        edge = (4 * SLAB + 16 if first else 4 * SLAB, NZ)
        chunk_r, up, down = call(functools.partial(edges_kernel, first), [chunk, edge, edge])(
            *((q,) if first else (q, rest))
        )
        low = lax.ppermute(up, CHAIN, line(4, 1))
        high = lax.ppermute(down, CHAIN, line(4, -1))
        scratch = [(10 * NY, ROWS, NZ)] * 4
        outs = [cells] * 4 + [(16, NZ)]
        if first:
            v0, v1, v2, v3, mom, ec = call(
                functools.partial(powers_kernel, True), outs + [(10 * NY, NZ)], scratch
            )(q, chunk_r, low, high)
        else:
            v0, v1, v2, v3, mom = call(functools.partial(powers_kernel, False), outs, scratch)(
                q, chunk_r, low, high, ec
            )
        mom = lax.all_to_all(mom, CHUNKS, 0, 0, tiled=True)
        if first:
            change, rest = call(functools.partial(update_kernel, True), [chunk, chunk])(
                mom, v0, v1, v2, v3
            )
        else:
            (total,) = call(
                functools.partial(update_kernel, False), [(QUAD, NY * 3 * TRI, NZ)]
            )(mom, half, v0, v1, v2, change)
    total = lax.all_to_all(total, WITHIN, 0, 0, tiled=True)
    total = total.reshape(QUAD, NY, 3, TRI, NZ).transpose(0, 3, 2, 1, 4)
    return mine[:NM] + total.reshape(NM, 3, 1, NY, NZ)


def solution(mesh):
    split = Mesh(mesh.devices.reshape(2, 4, 4, 4, 2, 2), AXES)
    mode, space = ("zh", "x"), ("y", "zp", "zq", "c")
    return jax.shard_map(
        shards,
        mesh=split,
        in_specs=(
            P(mode, None, space, None, None),
            P(mode, None, space, None, None),
            P(None, space, None, None),
            P(space, None, None),
            P(),
            P(),
            P(),
        ),
        out_specs=P(mode, None, space, None, None),
        check_vma=False,
    )
```

```python
import functools

import jax
import jax.numpy as jnp
from jax import lax
from jax.experimental import pallas as pl
from jax.experimental.pallas import tpu as pltpu
from jax.sharding import Mesh
from jax.sharding import PartitionSpec as P

AXES = ("zh", "x", "y", "zp", "zq", "c")
SLABS = ("zh", "y", "zp", "zq", "c")
CHAIN = ("zh", "y", "zp")
CHUNKS = ("y", "zp")
WITHIN = ("zq", "c")
NX, NM, NT, NL, NK = 4, 12, 24, 8, 8
MODES = 2 * NX * NM
NY, NZ, SHIFT = 4, 128, 4.0
QUAD = 4
TRI = NM // QUAD
SIX = 2 * TRI
ROWS = 3 * SIX
SLAB = NY * ROWS
SENT = 3 * SLAB + 8
F32 = jnp.float32


def line(inner, step):
    count = 4 * inner
    pairs = []
    for zh in range(2):
        for i in range(count):
            j = i + step
            if 0 <= j < count:
                other = zh ^ (i // inner != j // inner)
                pairs.append((zh * count + i, other * count + j))
    return pairs


def call(kernel, outs, scratch=()):
    vmem = pl.BlockSpec(memory_space=pltpu.VMEM)

    def run(*args):
        return pl.pallas_call(
            kernel,
            out_shape=[pltpu.VMEM(s, F32) for s in outs],
            in_specs=[vmem] * len(args),
            out_specs=[vmem] * len(outs),
            scratch_shapes=[pltpu.VMEM(s, F32) for s in scratch],
        )(*[pltpu.with_memory_space_constraint(a, pltpu.VMEM) for a in args])

    return run


def faces(e, other):
    return 0.5 * (e + other)


def coupling_kernel(nk, *refs):
    first = nk > NK
    if first:
        (u, load, e0, em, ep, partner, variable, weight, out, us, mx, fx, fy, fz) = refs
    else:
        (u, e0, em, ep, partner, variable, weight, out, us, mx, fx, fy, fz) = refs

    def lanes(yc):
        return slice(yc % 2 * NZ, (yc % 2 + 1) * NZ)

    def mixed(y, c, rows):
        yc = y * 3 + c
        return mx[yc // 2, rows, lanes(yc)]

    for g in range(2 * NX):
        half, x = divmod(g, NX)
        for y in range(NY):
            for c in range(3):
                yc = y * 3 + c
                if first:
                    at = (half * NY * 3 + yc) * NM
                    us[yc // 2, g * NM : (g + 1) * NM, lanes(yc)] = u[x, at : at + NM, :]
                    continue
                for d in range(QUAD):
                    at, to = y * ROWS + c * SIX + half * TRI, g * NM + d * TRI
                    us[yc // 2, to : to + TRI, lanes(yc)] = u[x * QUAD + d, at : at + TRI, :]
    lane = lax.broadcasted_iota(jnp.int32, (NT, MODES), 1)
    pr, vr, wr = partner[...], variable[...], weight[...]
    links = NL + 1 if first else NL
    hit = [jnp.where(lane == pr[:, l : l + 1], wr[:, l : l + 1], 0.0) for l in range(links)]
    blocks = []
    for k in range(nk):
        acc = None
        for l in range(links):
            if (k == NK) != (l == NL):
                continue
            term = hit[l] if l == NL else jnp.where(vr[:, l : l + 1] == k, hit[l], 0.0)
            acc = term if acc is None else acc + term
        blocks.append(acc)
    mix = jnp.concatenate(blocks, axis=0)
    for pair in range(NY * 3 // 2):
        mx[pair] = lax.dot_general(
            mix,
            us[pair],
            (((1,), (0,)), ((), ())),
            precision=lax.Precision.HIGHEST,
            preferred_element_type=F32,
        )
    e = e0[...]
    zlane = lax.broadcasted_iota(jnp.int32, e.shape, 1)
    row = lax.broadcasted_iota(jnp.int32, e.shape, 0)
    zup = jnp.where(zlane == NZ - 1, 0.0, pltpu.roll(e, NZ - 1, 1))
    zdn = jnp.where(zlane == 0, 0.0, pltpu.roll(e, 1, 1))
    count = e.shape[0]
    yup = jnp.where(row % NY == NY - 1, 0.0, pltpu.roll(e, count - 1, 0))
    ydn = jnp.where(row % NY == 0, 0.0, pltpu.roll(e, 1, 0))
    fx[0] = faces(e, ep[...])
    fx[1] = faces(e, em[...])
    fy[0] = faces(e, yup)
    fy[1] = faces(e, ydn)
    fzu, fzd = faces(e, zup), faces(e, zdn)
    base = fx[0] + fx[1] + fy[0] + fy[1] + fzu + fzd
    fz[0] = jnp.where(zlane == NZ - 1, 0.0, fzu)
    fz[1] = jnp.where(zlane == 0, 0.0, fzd)
    fz[2] = base + fx[0] + fx[1]
    fz[3] = base + fy[0] + fy[1]
    fz[4] = base + fzu + fzd
    for y in range(NY):
        for c in range(3):
            own = up = down = None
            for k in range(nk):
                r = slice(k * NY + y, k * NY + y + 1)
                rows = slice(k * NT, (k + 1) * NT)
                m = mixed(y, c, rows)
                t = fz[2 + c, r, :] * m
                side = None
                if y + 1 < NY:
                    side = fy[0, r, :] * mixed(y + 1, c, rows)
                if y > 0:
                    less = fy[1, r, :] * mixed(y - 1, c, rows)
                    side = less if side is None else side + less
                t = t - (2.0 * side if c == 1 else side)
                side = fz[0, r, :] * pltpu.roll(m, NZ - 1, 1) + fz[1, r, :] * pltpu.roll(m, 1, 1)
                t = t - (2.0 * side if c == 2 else side)
                p, q = fx[0, r, :] * m, fx[1, r, :] * m
                own, up, down = (t, p, q) if own is None else (own + t, up + p, down + q)
            if c == 0:
                up, down = 2.0 * up, 2.0 * down
            yc = y * 3 + c
            own = load[yc * NT : (yc + 1) * NT, :] - own if first else -own
            for kind, val in enumerate((own, up, down)):
                at = (kind * NY + y) * ROWS + c * SIX
                for d in range(QUAD):
                    out[d, at : at + SIX, :] = val[d * SIX : (d + 1) * SIX]
    zeros = jnp.zeros((NY, NZ), F32)
    tail = jnp.concatenate([e[NK * NY : NK * NY + NY] if first else zeros, zeros], axis=0)
    for d in range(QUAD):
        out[d, 3 * SLAB : SENT, :] = tail


def edges_kernel(first, *refs):
    if first:
        q, own, up, down = refs
    else:
        q, rest, own, up, down = refs
    rs = []
    for s in range(QUAD):
        r = q[s, 0:SLAB, :]
        if not first:
            r = r + rest[s]
        if s > 0:
            r = r + q[s - 1, SLAB : 2 * SLAB, :]
        if s + 1 < QUAD:
            r = r + q[s + 1, 2 * SLAB : 3 * SLAB, :]
        own[s] = r
        rs.append(r)
    for j in range(3):
        up[j * SLAB : (j + 1) * SLAB, :] = rs[j + 1]
        down[j * SLAB : (j + 1) * SLAB, :] = rs[j]
    up[3 * SLAB : 4 * SLAB, :] = q[3, SLAB : 2 * SLAB, :]
    down[3 * SLAB : 4 * SLAB, :] = q[0, 2 * SLAB : 3 * SLAB, :]
    if first:
        for j in range(3):
            at = 4 * SLAB + j * NY
            up[at : at + NY, :] = q[j + 1, 3 * SLAB : 3 * SLAB + NY, :]
            down[at : at + NY, :] = q[j, 3 * SLAB : 3 * SLAB + NY, :]
        up[4 * SLAB + 12 :, :] = jnp.zeros((4, NZ), F32)
        down[4 * SLAB + 12 :, :] = jnp.zeros((4, NZ), F32)


def powers_kernel(first, *refs):
    if first:
        q, own, low, high, v0, v1, v2, v3, mom, ec, w0, w1, w2, dg = refs
        for j in range(3):
            at = 4 * SLAB + j * NY
            ec[j * NY : (j + 1) * NY, :] = low[at : at + NY, :]
            ec[(7 + j) * NY : (8 + j) * NY, :] = high[at : at + NY, :]
        for s in range(QUAD):
            ec[(3 + s) * NY : (4 + s) * NY, :] = q[s, 3 * SLAB : 3 * SLAB + NY, :]
    else:
        q, own, low, high, ec, v0, v1, v2, v3, mom, w0, w1, w2, dg = refs

    def rows(ref, at, y):
        return ref[at + y * ROWS : at + (y + 1) * ROWS, :]

    rid = lax.broadcasted_iota(jnp.int32, (ROWS, NZ), 0)
    wx = jnp.where(rid < SIX, 2.0, 1.0)
    wy = jnp.where((rid >= SIX) & (rid < 2 * SIX), 2.0, 1.0)
    wz = jnp.where(rid >= 2 * SIX, 2.0, 1.0)
    lane1 = lax.broadcasted_iota(jnp.int32, (1, NZ), 1)
    em = [[ec[p * NY + y : p * NY + y + 1, :] for y in range(NY)] for p in range(10)]
    zero = jnp.zeros((1, NZ), F32)

    def inside(p, y, val):
        return val if 3 <= p <= 6 else jnp.where(em[p][y] > 0.0, val, 0.0)

    for y in range(NY):
        for p in range(3):
            lo = rows(low, p * SLAB, y)
            hi = rows(high, p * SLAB, y)
            if p == 2:
                lo = lo + rows(q.at[0], 2 * SLAB, y)
            if p == 0:
                hi = hi + rows(q.at[QUAD - 1], SLAB, y)
            w0[p * NY + y] = inside(p, y, lo)
            w0[(7 + p) * NY + y] = inside(7 + p, y, hi)
        for s in range(QUAD):
            r = rows(own.at[s], 0, y)
            if s == 0:
                r = r + rows(low, 3 * SLAB, y)
            if s == QUAD - 1:
                r = r + rows(high, 3 * SLAB, y)
            w0[(3 + s) * NY + y] = r
            v0[s * NY + y] = r

    def face(p, y):
        e = em[p][y]
        xu, xd = faces(e, em[p + 1][y]), faces(e, em[p - 1][y])
        yu = faces(e, em[p][y + 1] if y + 1 < NY else zero)
        yd = faces(e, em[p][y - 1] if y > 0 else zero)
        zu = faces(e, jnp.where(lane1 == NZ - 1, 0.0, pltpu.roll(e, NZ - 1, 1)))
        zd = faces(e, jnp.where(lane1 == 0, 0.0, pltpu.roll(e, 1, 1)))
        return xu, xd, yu, yd, zu, zd

    coef = {}
    for p in range(1, 9):
        for y in range(NY):
            xu, xd, yu, yd, zu, zd = face(p, y)
            dg[p * NY + y] = wx * (xu + xd) + wy * (yu + yd) + wz * (zu + zd) - SHIFT
            coef[p, y] = (
                xu, xd, yu, yd,
                jnp.where(lane1 == NZ - 1, 0.0, zu),
                jnp.where(lane1 == 0, 0.0, zd),
            )

    def apply(src, p, y):
        xu, xd, yu, yd, zu, zd = coef[p, y]
        m = src[p * NY + y]
        t = dg[p * NY + y] * m
        t = t - wx * (xu * src[(p + 1) * NY + y] + xd * src[(p - 1) * NY + y])
        side = None
        if y + 1 < NY:
            side = yu * src[p * NY + y + 1]
        if y > 0:
            less = yd * src[p * NY + y - 1]
            side = less if side is None else side + less
        t = t - wy * side
        t = t - wz * (zu * pltpu.roll(m, NZ - 1, 1) + zd * pltpu.roll(m, 1, 1))
        return inside(p, y, t)

    for p in range(1, 9):
        for y in range(NY):
            t = apply(w0, p, y)
            w1[p * NY + y] = t
            if 3 <= p <= 6:
                v1[(p - 3) * NY + y] = t
    for p in range(2, 8):
        for y in range(NY):
            t = apply(w1, p, y)
            w2[p * NY + y] = t
            if 3 <= p <= 6:
                v2[(p - 3) * NY + y] = t
    sums = [None] * 6
    for p in range(3, 7):
        for y in range(NY):
            a, b, d = w0[p * NY + y], w1[p * NY + y], w2[p * NY + y]
            t = apply(w2, p, y)
            v3[(p - 3) * NY + y] = t
            for j, val in enumerate((a * a, a * b, b * b, b * d, d * d, d * t)):
                sums[j] = val if sums[j] is None else sums[j] + val
    lane = lax.broadcasted_iota(jnp.int32, (ROWS, NZ), 1)
    spot = lane - 8 * (rid % SIX)
    packed = jnp.zeros((ROWS, NZ), F32)
    for j in range(6):
        packed = jnp.where(spot == j, jnp.sum(sums[j], axis=1, keepdims=True), packed)
    mom[...] = jnp.broadcast_to(jnp.sum(packed, axis=0, keepdims=True), mom.shape)


def step_coefficients(mom):
    def inner(a, b):
        total = None
        for i, s in enumerate(a):
            for j, t in enumerate(b):
                term = s * t * mom[i + j]
                total = term if total is None else total + term
        return total

    def image(a):
        q = [SHIFT * s for s in a] + [None]
        for i, s in enumerate(a):
            q[i + 1] = s if q[i + 1] is None else q[i + 1] + s
        return q

    one = jnp.ones_like(mom[0])
    x, r, p = [], [one], [one]
    rr = mom[0]
    for step in range(3):
        q = image(p)
        alpha = rr / inner(p, q)
        x = [x[i] + alpha * s if i < len(x) else alpha * s for i, s in enumerate(p)]
        r = [r[i] - alpha * s if i < len(r) else -alpha * s for i, s in enumerate(q)]
        if step < 2:
            new = inner(r, r)
            beta = new / rr
            p = [s + beta * p[i] if i < len(p) else s for i, s in enumerate(r)]
            rr = new
    return x, r


def update_kernel(first, *refs):
    if first:
        mom, v0, v1, v2, v3, out, rest, copies = refs
    else:
        mom, half, v0, v1, v2, before, out = refs
        upper = half[...] > 0.0
    total = jnp.sum(mom[...], axis=0, keepdims=True)
    rid = lax.broadcasted_iota(jnp.int32, (ROWS, NZ), 0)
    lane = lax.broadcasted_iota(jnp.int32, (ROWS, NZ), 1)
    spot = lane - 8 * (rid % SIX)
    picked = [jnp.sum(jnp.where(spot == j, total, 0.0), axis=1, keepdims=True) for j in range(6)]
    x, r = step_coefficients(picked)
    x = [jnp.broadcast_to(s, (ROWS, NZ)) for s in x]
    r = [jnp.broadcast_to(s, (ROWS, NZ)) for s in r]
    for s in range(QUAD):
        for y in range(NY):
            at = s * NY + y
            rows = slice(y * ROWS, (y + 1) * ROWS)
            a, b, d = v0[at], v1[at], v2[at]
            change = x[0] * a + x[1] * b + x[2] * d
            if first:
                rest[s, rows, :] = r[0] * a + r[1] * b + r[2] * d + r[3] * v3[at]
            else:
                change = change + before[s, rows, :]
                for c in range(3):
                    at = c * SIX
                    pick = jnp.where(upper, change[at + TRI : at + SIX], change[at : at + TRI])
                    to = (y * 3 + c) * TRI
                    out[s, to : to + TRI, :] = pick
                continue
            out[s, rows, :] = change
            for place in range(NX):
                copies[place * QUAD + s, rows, :] = change


def fan_kernel(blocks, field, out):
    for d in range(blocks):
        own = field[d]
        for x in range(NX):
            out[x * blocks + d] = own


def packed(field):
    return field.transpose(0, 3, 2, 1, 4).reshape(1, 2 * NY * 3 * NM, NZ)


def by_target(field):
    field = field.reshape(2, QUAD, TRI, 3, NY, NZ)
    return field.transpose(4, 3, 1, 0, 2, 5).reshape(NY * 3 * NT, NZ)


def rows_of(table, x):
    table = lax.dynamic_index_in_dim(table.reshape(2, NX, QUAD, TRI, -1), x, 1, keepdims=False)
    return table.transpose(1, 0, 2, 3).reshape(NT, -1)


def shards(load_modes, first_guess, kl_fields, region_labels, partner, variable, weight):
    mean = jnp.where(region_labels == 0, 1.3, jnp.where(region_labels == 1, 1.0, 0.6)).astype(F32)
    varying = jnp.where(region_labels[None] == 1, kl_fields, 0.0)
    moduli = jnp.concatenate([varying, mean[None]], 0).reshape((NK + 1) * NY, NZ)
    em = lax.ppermute(moduli, SLABS, line(16, 1))
    ep = lax.ppermute(moduli, SLABS, line(16, -1))
    e0 = moduli
    mine = lax.optimization_barrier(jnp.concatenate([first_guess, load_modes], 0))
    far = lax.ppermute(mine, "zh", [(0, 1), (1, 0)])
    zh, x = lax.axis_index("zh"), lax.axis_index("x")
    lower = zh == 0
    both = jnp.stack([jnp.where(lower, mine, far), jnp.where(lower, far, mine)])
    both = both.reshape(2, 2, NM, 3, NY, NZ)
    guess, load = packed(both[:, 0]), by_target(both[:, 1])
    half = jnp.broadcast_to(zh.astype(F32), (TRI, NZ))

    own = rows_of(jnp.arange(MODES, dtype=jnp.int32), x)
    rows_partner = jnp.concatenate([rows_of(partner, x), own], 1)
    rows_variable = rows_of(variable, x)
    rows_weight = jnp.concatenate([rows_of(weight, x), jnp.ones((NT, 1), F32)], 1)
    links = (rows_partner, rows_variable, rows_weight)

    chunk, cells = (QUAD, SLAB, NZ), (QUAD * NY, ROWS, NZ)
    for sweep in range(2):
        first = sweep == 0
        nk = NK + 1 if first else NK
        if first:
            (copies,) = call(functools.partial(fan_kernel, 1), [(NX,) + guess.shape[1:]])(guess)
        u = lax.all_to_all(copies, ("x",) if first else ("x",) + WITHIN, 0, 0, tiled=True)
        fields = (u, load, e0, em, ep) if first else (u, e0, em, ep)
        face_rows = ((NK + 1) * NY, NZ)
        (sent,) = call(
            functools.partial(coupling_kernel, nk),
            [(QUAD, SENT, NZ)],
            [
                (NY * 3 // 2, MODES, 2 * NZ),
                (NY * 3 // 2, nk * NT, 2 * NZ),
                (2,) + face_rows,
                (2,) + face_rows,
                (5,) + face_rows,
            ],
        )(*fields, *links)
        q = lax.all_to_all(sent, WITHIN, 0, 0, tiled=True)
        edge = (4 * SLAB + 16 if first else 4 * SLAB, NZ)
        chunk_r, up, down = call(functools.partial(edges_kernel, first), [chunk, edge, edge])(
            *((q,) if first else (q, rest))
        )
        low = lax.ppermute(up, CHAIN, line(4, 1))
        high = lax.ppermute(down, CHAIN, line(4, -1))
        scratch = [(10 * NY, ROWS, NZ)] * 4
        outs = [cells] * 4 + [(16, NZ)]
        if first:
            v0, v1, v2, v3, mom, ec = call(
                functools.partial(powers_kernel, True), outs + [(10 * NY, NZ)], scratch
            )(q, chunk_r, low, high)
        else:
            v0, v1, v2, v3, mom = call(functools.partial(powers_kernel, False), outs, scratch)(
                q, chunk_r, low, high, ec
            )
        mom = lax.all_to_all(mom, CHUNKS, 0, 0, tiled=True)
        if first:
            change, rest, copies = call(
                functools.partial(update_kernel, True), [chunk, chunk, (NX * QUAD, SLAB, NZ)]
            )(
                mom, v0, v1, v2, v3
            )
        else:
            (total,) = call(
                functools.partial(update_kernel, False), [(QUAD, NY * 3 * TRI, NZ)]
            )(mom, half, v0, v1, v2, change)
    total = lax.all_to_all(total, WITHIN, 0, 0, tiled=True)
    total = total.reshape(QUAD, NY, 3, TRI, NZ).transpose(0, 3, 2, 1, 4)
    return mine[:NM] + total.reshape(NM, 3, 1, NY, NZ)


def solution(mesh):
    split = Mesh(mesh.devices.reshape(2, 4, 4, 4, 2, 2), AXES)
    mode, space = ("zh", "x"), ("y", "zp", "zq", "c")
    return jax.shard_map(
        shards,
        mesh=split,
        in_specs=(
            P(mode, None, space, None, None),
            P(mode, None, space, None, None),
            P(None, space, None, None),
            P(space, None, None),
            P(),
            P(),
            P(),
        ),
        out_specs=P(mode, None, space, None, None),
        check_vma=False,
    )
```

```python
import functools

import jax
import jax.numpy as jnp
from jax import lax
from jax.experimental import pallas as pl
from jax.experimental.pallas import tpu as pltpu
from jax.sharding import Mesh
from jax.sharding import PartitionSpec as P

AXES = ("zh", "x", "y", "zp", "zq", "c")
SLABS = ("zh", "y", "zp", "zq", "c")
CHAIN = ("zh", "y", "zp")
CHUNKS = ("y", "zp")
WITHIN = ("zq", "c")
NX, NM, NT, NL, NK = 4, 12, 24, 8, 8
MODES = 2 * NX * NM
NY, NZ, SHIFT = 4, 128, 4.0
QUAD = 4
TRI = NM // QUAD
SIX = 2 * TRI
ROWS = 3 * SIX
SLAB = NY * ROWS
SENT = 3 * SLAB + 8
F32 = jnp.float32


def line(inner, step):
    count = 4 * inner
    pairs = []
    for zh in range(2):
        for i in range(count):
            j = i + step
            if 0 <= j < count:
                other = zh ^ (i // inner != j // inner)
                pairs.append((zh * count + i, other * count + j))
    return pairs


def call(kernel, outs, scratch=()):
    vmem = pl.BlockSpec(memory_space=pltpu.VMEM)

    def run(*args):
        return pl.pallas_call(
            kernel,
            out_shape=[pltpu.VMEM(s, F32) for s in outs],
            in_specs=[vmem] * len(args),
            out_specs=[vmem] * len(outs),
            scratch_shapes=[pltpu.VMEM(s, F32) for s in scratch],
        )(*[pltpu.with_memory_space_constraint(a, pltpu.VMEM) for a in args])

    return run


def faces(e, other):
    return 0.5 * (e + other)


def coupling_kernel(nk, *refs):
    first = nk > NK
    if first:
        (u, load, e0, em, ep, partner, variable, weight, out, us, mx, fx, fy, fz) = refs
    else:
        (u, e0, em, ep, partner, variable, weight, out, us, mx, fx, fy, fz) = refs

    def lanes(yc):
        return slice(yc % 2 * NZ, (yc % 2 + 1) * NZ)

    def mixed(y, c, rows):
        yc = y * 3 + c
        return mx[yc // 2, rows, lanes(yc)]

    for g in range(2 * NX):
        half, x = divmod(g, NX)
        for y in range(NY):
            for c in range(3):
                yc = y * 3 + c
                if first:
                    at = (half * NY * 3 + yc) * NM
                    us[yc // 2, g * NM : (g + 1) * NM, lanes(yc)] = u[x, at : at + NM, :]
                    continue
                for d in range(QUAD):
                    at, to = y * ROWS + c * SIX + half * TRI, g * NM + d * TRI
                    us[yc // 2, to : to + TRI, lanes(yc)] = u[x * QUAD + d, at : at + TRI, :]
    lane = lax.broadcasted_iota(jnp.int32, (NT, MODES), 1)
    pr, vr, wr = partner[...], variable[...], weight[...]
    links = NL + 1 if first else NL
    hit = [jnp.where(lane == pr[:, l : l + 1], wr[:, l : l + 1], 0.0) for l in range(links)]
    blocks = []
    for k in range(nk):
        acc = None
        for l in range(links):
            if (k == NK) != (l == NL):
                continue
            term = hit[l] if l == NL else jnp.where(vr[:, l : l + 1] == k, hit[l], 0.0)
            acc = term if acc is None else acc + term
        blocks.append(acc)
    mix = jnp.concatenate(blocks, axis=0)
    for pair in range(NY * 3 // 2):
        mx[pair] = lax.dot_general(
            mix,
            us[pair],
            (((1,), (0,)), ((), ())),
            precision=lax.Precision.HIGHEST,
            preferred_element_type=F32,
        )
    e = e0[...]
    zlane = lax.broadcasted_iota(jnp.int32, e.shape, 1)
    row = lax.broadcasted_iota(jnp.int32, e.shape, 0)
    zup = jnp.where(zlane == NZ - 1, 0.0, pltpu.roll(e, NZ - 1, 1))
    zdn = jnp.where(zlane == 0, 0.0, pltpu.roll(e, 1, 1))
    count = e.shape[0]
    yup = jnp.where(row % NY == NY - 1, 0.0, pltpu.roll(e, count - 1, 0))
    ydn = jnp.where(row % NY == 0, 0.0, pltpu.roll(e, 1, 0))
    fx[0] = faces(e, ep[...])
    fx[1] = faces(e, em[...])
    fy[0] = faces(e, yup)
    fy[1] = faces(e, ydn)
    fzu, fzd = faces(e, zup), faces(e, zdn)
    base = fx[0] + fx[1] + fy[0] + fy[1] + fzu + fzd
    fz[0] = jnp.where(zlane == NZ - 1, 0.0, fzu)
    fz[1] = jnp.where(zlane == 0, 0.0, fzd)
    fz[2] = base + fx[0] + fx[1]
    fz[3] = base + fy[0] + fy[1]
    fz[4] = base + fzu + fzd
    for y in range(NY):
        for c in range(3):
            own = up = down = None
            for k in range(nk):
                r = slice(k * NY + y, k * NY + y + 1)
                rows = slice(k * NT, (k + 1) * NT)
                m = mixed(y, c, rows)
                t = fz[2 + c, r, :] * m
                side = None
                if y + 1 < NY:
                    side = fy[0, r, :] * mixed(y + 1, c, rows)
                if y > 0:
                    less = fy[1, r, :] * mixed(y - 1, c, rows)
                    side = less if side is None else side + less
                t = t - (2.0 * side if c == 1 else side)
                side = fz[0, r, :] * pltpu.roll(m, NZ - 1, 1) + fz[1, r, :] * pltpu.roll(m, 1, 1)
                t = t - (2.0 * side if c == 2 else side)
                p, q = fx[0, r, :] * m, fx[1, r, :] * m
                own, up, down = (t, p, q) if own is None else (own + t, up + p, down + q)
            if c == 0:
                up, down = 2.0 * up, 2.0 * down
            yc = y * 3 + c
            own = load[yc * NT : (yc + 1) * NT, :] - own if first else -own
            for kind, val in enumerate((own, up, down)):
                at = (kind * NY + y) * ROWS + c * SIX
                for d in range(QUAD):
                    out[d, at : at + SIX, :] = val[d * SIX : (d + 1) * SIX]
    if first:
        tail = jnp.concatenate([e[NK * NY : NK * NY + NY], jnp.zeros((NY, NZ), F32)], axis=0)
        for d in range(QUAD):
            out[d, 3 * SLAB : SENT, :] = tail


def edges_kernel(first, *refs):
    if first:
        q, own, up, down = refs
    else:
        q, rest, own, up, down = refs
    rs = []
    for s in range(QUAD):
        r = q[s, 0:SLAB, :]
        if not first:
            r = r + rest[s]
        if s > 0:
            r = r + q[s - 1, SLAB : 2 * SLAB, :]
        if s + 1 < QUAD:
            r = r + q[s + 1, 2 * SLAB : 3 * SLAB, :]
        own[s] = r
        rs.append(r)
    for j in range(3):
        up[j * SLAB : (j + 1) * SLAB, :] = rs[j + 1]
        down[j * SLAB : (j + 1) * SLAB, :] = rs[j]
    up[3 * SLAB : 4 * SLAB, :] = q[3, SLAB : 2 * SLAB, :]
    down[3 * SLAB : 4 * SLAB, :] = q[0, 2 * SLAB : 3 * SLAB, :]
    if first:
        for j in range(3):
            at = 4 * SLAB + j * NY
            up[at : at + NY, :] = q[j + 1, 3 * SLAB : 3 * SLAB + NY, :]
            down[at : at + NY, :] = q[j, 3 * SLAB : 3 * SLAB + NY, :]
        up[4 * SLAB + 12 :, :] = jnp.zeros((4, NZ), F32)
        down[4 * SLAB + 12 :, :] = jnp.zeros((4, NZ), F32)


def powers_kernel(first, *refs):
    if first:
        q, own, low, high, v0, v1, v2, v3, mom, ec, w0, w1, w2, dg = refs
        for j in range(3):
            at = 4 * SLAB + j * NY
            ec[j * NY : (j + 1) * NY, :] = low[at : at + NY, :]
            ec[(7 + j) * NY : (8 + j) * NY, :] = high[at : at + NY, :]
        for s in range(QUAD):
            ec[(3 + s) * NY : (4 + s) * NY, :] = q[s, 3 * SLAB : 3 * SLAB + NY, :]
    else:
        q, own, low, high, ec, v0, v1, v2, v3, mom, w0, w1, w2, dg = refs

    def rows(ref, at, y):
        return ref[at + y * ROWS : at + (y + 1) * ROWS, :]

    rid = lax.broadcasted_iota(jnp.int32, (ROWS, NZ), 0)
    wx = jnp.where(rid < SIX, 2.0, 1.0)
    wy = jnp.where((rid >= SIX) & (rid < 2 * SIX), 2.0, 1.0)
    wz = jnp.where(rid >= 2 * SIX, 2.0, 1.0)
    lane1 = lax.broadcasted_iota(jnp.int32, (1, NZ), 1)
    em = [[ec[p * NY + y : p * NY + y + 1, :] for y in range(NY)] for p in range(10)]
    zero = jnp.zeros((1, NZ), F32)

    def inside(p, y, val):
        return val if 3 <= p <= 6 else jnp.where(em[p][y] > 0.0, val, 0.0)

    for y in range(NY):
        for p in range(3):
            lo = rows(low, p * SLAB, y)
            hi = rows(high, p * SLAB, y)
            if p == 2:
                lo = lo + rows(q.at[0], 2 * SLAB, y)
            if p == 0:
                hi = hi + rows(q.at[QUAD - 1], SLAB, y)
            w0[p * NY + y] = inside(p, y, lo)
            w0[(7 + p) * NY + y] = inside(7 + p, y, hi)
        for s in range(QUAD):
            r = rows(own.at[s], 0, y)
            if s == 0:
                r = r + rows(low, 3 * SLAB, y)
            if s == QUAD - 1:
                r = r + rows(high, 3 * SLAB, y)
            w0[(3 + s) * NY + y] = r
            v0[s * NY + y] = r

    def face(p, y):
        e = em[p][y]
        xu, xd = faces(e, em[p + 1][y]), faces(e, em[p - 1][y])
        yu = faces(e, em[p][y + 1] if y + 1 < NY else zero)
        yd = faces(e, em[p][y - 1] if y > 0 else zero)
        zu = faces(e, jnp.where(lane1 == NZ - 1, 0.0, pltpu.roll(e, NZ - 1, 1)))
        zd = faces(e, jnp.where(lane1 == 0, 0.0, pltpu.roll(e, 1, 1)))
        return xu, xd, yu, yd, zu, zd

    coef = {}
    for p in range(1, 9):
        for y in range(NY):
            xu, xd, yu, yd, zu, zd = face(p, y)
            dg[p * NY + y] = wx * (xu + xd) + wy * (yu + yd) + wz * (zu + zd) - SHIFT
            coef[p, y] = (
                xu, xd, yu, yd,
                jnp.where(lane1 == NZ - 1, 0.0, zu),
                jnp.where(lane1 == 0, 0.0, zd),
            )

    def apply(src, p, y):
        xu, xd, yu, yd, zu, zd = coef[p, y]
        m = src[p * NY + y]
        t = dg[p * NY + y] * m
        t = t - wx * (xu * src[(p + 1) * NY + y] + xd * src[(p - 1) * NY + y])
        side = None
        if y + 1 < NY:
            side = yu * src[p * NY + y + 1]
        if y > 0:
            less = yd * src[p * NY + y - 1]
            side = less if side is None else side + less
        t = t - wy * side
        t = t - wz * (zu * pltpu.roll(m, NZ - 1, 1) + zd * pltpu.roll(m, 1, 1))
        return inside(p, y, t)

    for p in range(1, 9):
        for y in range(NY):
            t = apply(w0, p, y)
            w1[p * NY + y] = t
            if 3 <= p <= 6:
                v1[(p - 3) * NY + y] = t
    for p in range(2, 8):
        for y in range(NY):
            t = apply(w1, p, y)
            w2[p * NY + y] = t
            if 3 <= p <= 6:
                v2[(p - 3) * NY + y] = t
    sums = [None] * 6
    for p in range(3, 7):
        for y in range(NY):
            a, b, d = w0[p * NY + y], w1[p * NY + y], w2[p * NY + y]
            t = apply(w2, p, y)
            v3[(p - 3) * NY + y] = t
            for j, val in enumerate((a * a, a * b, b * b, b * d, d * d, d * t)):
                sums[j] = val if sums[j] is None else sums[j] + val
    lane = lax.broadcasted_iota(jnp.int32, (ROWS, NZ), 1)
    spot = lane - 8 * (rid % SIX)
    packed = jnp.zeros((ROWS, NZ), F32)
    for j in range(6):
        packed = jnp.where(spot == j, jnp.sum(sums[j], axis=1, keepdims=True), packed)
    mom[...] = jnp.broadcast_to(jnp.sum(packed, axis=0, keepdims=True), mom.shape)


def step_coefficients(mom):
    def inner(a, b):
        total = None
        for i, s in enumerate(a):
            for j, t in enumerate(b):
                term = s * t * mom[i + j]
                total = term if total is None else total + term
        return total

    def image(a):
        q = [SHIFT * s for s in a] + [None]
        for i, s in enumerate(a):
            q[i + 1] = s if q[i + 1] is None else q[i + 1] + s
        return q

    one = jnp.ones_like(mom[0])
    x, r, p = [], [one], [one]
    rr = mom[0]
    for step in range(3):
        q = image(p)
        alpha = rr / inner(p, q)
        x = [x[i] + alpha * s if i < len(x) else alpha * s for i, s in enumerate(p)]
        r = [r[i] - alpha * s if i < len(r) else -alpha * s for i, s in enumerate(q)]
        if step < 2:
            new = inner(r, r)
            beta = new / rr
            p = [s + beta * p[i] if i < len(p) else s for i, s in enumerate(r)]
            rr = new
    return x, r


def update_kernel(first, *refs):
    if first:
        mom, v0, v1, v2, v3, out, rest, copies = refs
    else:
        mom, half, v0, v1, v2, before, out = refs
        upper = half[...] > 0.0
    total = jnp.sum(mom[...], axis=0, keepdims=True)
    rid = lax.broadcasted_iota(jnp.int32, (ROWS, NZ), 0)
    lane = lax.broadcasted_iota(jnp.int32, (ROWS, NZ), 1)
    spot = lane - 8 * (rid % SIX)
    picked = [jnp.sum(jnp.where(spot == j, total, 0.0), axis=1, keepdims=True) for j in range(6)]
    x, r = step_coefficients(picked)
    x = [jnp.broadcast_to(s, (ROWS, NZ)) for s in x]
    r = [jnp.broadcast_to(s, (ROWS, NZ)) for s in r]
    for s in range(QUAD):
        for y in range(NY):
            at = s * NY + y
            rows = slice(y * ROWS, (y + 1) * ROWS)
            a, b, d = v0[at], v1[at], v2[at]
            change = x[0] * a + x[1] * b + x[2] * d
            if first:
                rest[s, rows, :] = r[0] * a + r[1] * b + r[2] * d + r[3] * v3[at]
            else:
                change = change + before[s, rows, :]
                for c in range(3):
                    at = c * SIX
                    pick = jnp.where(upper, change[at + TRI : at + SIX], change[at : at + TRI])
                    to = (y * 3 + c) * TRI
                    out[s, to : to + TRI, :] = pick
                continue
            out[s, rows, :] = change
            for place in range(NX):
                copies[place * QUAD + s, rows, :] = change


def fan_kernel(blocks, field, out):
    for d in range(blocks):
        own = field[d]
        for x in range(NX):
            out[x * blocks + d] = own


def packed(field):
    return field.transpose(0, 3, 2, 1, 4).reshape(1, 2 * NY * 3 * NM, NZ)


def by_target(field):
    field = field.reshape(2, QUAD, TRI, 3, NY, NZ)
    return field.transpose(4, 3, 1, 0, 2, 5).reshape(NY * 3 * NT, NZ)


def rows_of(table, x):
    table = lax.dynamic_index_in_dim(table.reshape(2, NX, QUAD, TRI, -1), x, 1, keepdims=False)
    return table.transpose(1, 0, 2, 3).reshape(NT, -1)


def shards(load_modes, first_guess, kl_fields, region_labels, partner, variable, weight):
    mean = jnp.where(region_labels == 0, 1.3, jnp.where(region_labels == 1, 1.0, 0.6)).astype(F32)
    varying = jnp.where(region_labels[None] == 1, kl_fields, 0.0)
    moduli = jnp.concatenate([varying, mean[None]], 0).reshape((NK + 1) * NY, NZ)
    em = lax.ppermute(moduli, SLABS, line(16, 1))
    ep = lax.ppermute(moduli, SLABS, line(16, -1))
    e0 = moduli
    mine = lax.optimization_barrier(jnp.concatenate([first_guess, load_modes], 0))
    far = lax.ppermute(mine, "zh", [(0, 1), (1, 0)])
    zh, x = lax.axis_index("zh"), lax.axis_index("x")
    lower = zh == 0
    both = jnp.stack([jnp.where(lower, mine, far), jnp.where(lower, far, mine)])
    both = both.reshape(2, 2, NM, 3, NY, NZ)
    guess, load = packed(both[:, 0]), by_target(both[:, 1])
    half = jnp.broadcast_to(zh.astype(F32), (TRI, NZ))

    own = rows_of(jnp.arange(MODES, dtype=jnp.int32), x)
    rows_partner = jnp.concatenate([rows_of(partner, x), own], 1)
    rows_variable = rows_of(variable, x)
    rows_weight = jnp.concatenate([rows_of(weight, x), jnp.ones((NT, 1), F32)], 1)
    links = (rows_partner, rows_variable, rows_weight)

    chunk, cells = (QUAD, SLAB, NZ), (QUAD * NY, ROWS, NZ)
    for sweep in range(2):
        first = sweep == 0
        nk = NK + 1 if first else NK
        if first:
            (copies,) = call(functools.partial(fan_kernel, 1), [(NX,) + guess.shape[1:]])(guess)
        u = lax.all_to_all(copies, ("x",) if first else ("x",) + WITHIN, 0, 0, tiled=True)
        fields = (u, load, e0, em, ep) if first else (u, e0, em, ep)
        face_rows = ((NK + 1) * NY, NZ)
        (sent,) = call(
            functools.partial(coupling_kernel, nk),
            [(QUAD, SENT if first else 3 * SLAB, NZ)],
            [
                (NY * 3 // 2, MODES, 2 * NZ),
                (NY * 3 // 2, nk * NT, 2 * NZ),
                (2,) + face_rows,
                (2,) + face_rows,
                (5,) + face_rows,
            ],
        )(*fields, *links)
        q = lax.all_to_all(sent, WITHIN, 0, 0, tiled=True)
        edge = (4 * SLAB + 16 if first else 4 * SLAB, NZ)
        chunk_r, up, down = call(functools.partial(edges_kernel, first), [chunk, edge, edge])(
            *((q,) if first else (q, rest))
        )
        low = lax.ppermute(up, CHAIN, line(4, 1))
        high = lax.ppermute(down, CHAIN, line(4, -1))
        scratch = [(10 * NY, ROWS, NZ)] * 4
        outs = [cells] * 4 + [(16, NZ)]
        if first:
            v0, v1, v2, v3, mom, ec = call(
                functools.partial(powers_kernel, True), outs + [(10 * NY, NZ)], scratch
            )(q, chunk_r, low, high)
        else:
            v0, v1, v2, v3, mom = call(functools.partial(powers_kernel, False), outs, scratch)(
                q, chunk_r, low, high, ec
            )
        mom = lax.all_to_all(mom, CHUNKS, 0, 0, tiled=True)
        if first:
            change, rest, copies = call(
                functools.partial(update_kernel, True), [chunk, chunk, (NX * QUAD, SLAB, NZ)]
            )(
                mom, v0, v1, v2, v3
            )
        else:
            (total,) = call(
                functools.partial(update_kernel, False), [(QUAD, NY * 3 * TRI, NZ)]
            )(mom, half, v0, v1, v2, change)
    total = lax.all_to_all(total, WITHIN, 0, 0, tiled=True)
    total = total.reshape(QUAD, NY, 3, TRI, NZ).transpose(0, 3, 2, 1, 4)
    return mine[:NM] + total.reshape(NM, 3, 1, NY, NZ)


def solution(mesh):
    split = Mesh(mesh.devices.reshape(2, 4, 4, 4, 2, 2), AXES)
    mode, space = ("zh", "x"), ("y", "zp", "zq", "c")
    return jax.shard_map(
        shards,
        mesh=split,
        in_specs=(
            P(mode, None, space, None, None),
            P(mode, None, space, None, None),
            P(None, space, None, None),
            P(space, None, None),
            P(),
            P(),
            P(),
        ),
        out_specs=P(mode, None, space, None, None),
        check_vma=False,
    )
```
